32 devices in a mesh: blk: 16 (over z, y, core), ffn: 2 (over x).
Axes of the slice: x: 2, y: 2, z: 4, core: 2. Of those that a mesh axis runs over, the one named last changes fastest.
Arguments:
- tokens: bfloat16 [4096, 4608], P('blk'), may hold values from -6 to 6
- ln_gain: float32 [4608], replicated, may hold values from 0.5 to 2
- ln_bias: float32 [4608], replicated, may hold values from -3 to 3
- fc1_tiles: bfloat16 [16, 2, 101, 128, 128], P('blk', 'ffn'), may hold values from -0.125 to 0.125
- fc1_index: int32 [16, 2, 101], P('blk', 'ffn'), may hold values from 0 to 2591, as said below
- fc1_count: int32 [16, 2], P('blk', 'ffn'), may hold values from 60 to 101, as said below
- fc1_bias: float32 [18432], P('ffn'), may hold values from -3 to 3
- fc2_tiles: bfloat16 [16, 2, 101, 128, 128], P('blk', 'ffn'), may hold values from -0.09375 to 0.09375
- fc2_index: int32 [16, 2, 101], P('blk', 'ffn'), may hold values from 0 to 2591, as said below
- fc2_count: int32 [16, 2], P('blk', 'ffn'), may hold values from 60 to 101, as said below
- fc2_bias: float32 [4608], P('ffn'), may hold values from -3 to 3
Outputs:
- result: bfloat16 [4096, 4608], P('blk', 'ffn')
The draws below stay inside these ranges and needn't reach their ends.
Inputs may be any that keep to these rules, and one draw needn't show every extreme that they name: `fc1_index`: within one index f of ffn, the positions of all live slots (s < the shard's count) are distinct. `fc2_index`: as for fc1_index. `fc1_count`: some shard of every index of ffn has all 101 slots live. `fc2_count`: as for fc1_count.
All inputs are finite; a program needn't handle non-finite values.
Results may differ from the reference program's by a relative error of at most 0.01.
Values may be sent and summed in bfloat16 or wider, within the bound.
No kernel may reach another device: no remote copies, remote signals or barrier semaphores. Data moves between devices by JAX's collectives and lax.ppermute only.
A program may use at most 256 MiB of HBM per device.

```python
import math
import jax
import jax.numpy as jnp
from jax import lax

D = 4608
FF = 18432
TB = 128
TOKENS = 4096
RB = 36
FFS = 9216
CB = 72
MEAN_TILES = 81
SLOTS = 101
N_BLK = 16
N_FFN = 2


def tile_layout(key, salt):
    base = jax.random.fold_in(key, salt)
    key_counts, key_top, key_perm = jax.random.split(base, 3)
    lowest = MEAN_TILES * 3 // 4
    counts = jax.random.randint(key_counts, (N_BLK, N_FFN), lowest, SLOTS + 1)
    top_row = jax.random.randint(key_top, (N_FFN,), 0, N_BLK)
    low_row = (top_row + 1) % N_BLK
    shard_ids = jnp.arange(N_BLK)[:, None]
    counts = jnp.where(shard_ids == top_row[None, :], SLOTS, counts)
    counts = jnp.where(shard_ids == low_row[None, :], lowest, counts)
    starts = jnp.cumsum(counts, axis=0) - counts
    perm_keys = jax.random.split(key_perm, N_FFN)
    perms = jax.vmap(lambda one_key: jax.random.permutation(one_key, RB * CB))(perm_keys)
    rotate = RB * CB - 1 - perms[:, 0:1]
    perms = (perms + rotate) % (RB * CB)
    offsets = jnp.minimum(starts[:, :, None] + jnp.arange(SLOTS)[None, None, :], RB * CB - 1)
    groups = jnp.arange(N_FFN)[None, :, None]
    positions = perms[groups, offsets]
    return (positions.astype(jnp.int32), counts.astype(jnp.int32))


def draw_fc1_index(key, part):
    return tile_layout(key, 11)[0]


def draw_fc1_count(key, part):
    return tile_layout(key, 11)[1]


def draw_fc2_index(key, part):
    return tile_layout(key, 23)[0]


def draw_fc2_count(key, part):
    return tile_layout(key, 23)[1]


def level_of(key, dims, shards, low, largest):
    loudness = 1.0
    for dim, shards_of in shards:
        heights = jax.random.uniform(jax.random.fold_in(jax.random.fold_in(key, 6), dim), (shards_of,), jnp.float32, low / len(shards), largest / len(shards))
        loudness = loudness * jnp.repeat(jnp.exp(heights), dims[dim] // shards_of).reshape((-1,) + (1,) * (len(dims) - 1 - dim))
    return loudness


def scatter_about(stream_key, dims, scale, most, cuts=(), held_as=jnp.bfloat16):
    factor_of = level_of(stream_key, dims, cuts, -0.22, 0.18) if cuts else 1.0
    values = jax.random.normal(stream_key, dims, jnp.float32) * scale * factor_of
    return jnp.minimum(jnp.maximum(values, -most), most).astype(held_as)


def setup_inputs(seed: int = 0) -> dict:
    splits = jax.random.split(jax.random.key(seed), 12)
    tokens = scatter_about(splits[0], (TOKENS, D), 1.0, 6.0, ((0, 16),))
    ln_gain = jnp.clip(jnp.exp(jax.random.uniform(splits[1], (D,), jnp.float32, math.log(0.5), math.log(2.0))), 0.5, 2.0)
    ln_bias = scatter_about(splits[2], (D,), 0.5, 3.0, (), jnp.float32)
    fc1_tiles = scatter_about(splits[3], (N_BLK, N_FFN, SLOTS, TB, TB), (D // 2) ** -0.5, 0.125, ((0, 16), (1, 2)))
    fc1_index = draw_fc1_index(jax.random.fold_in(splits[11], 71), 0)
    fc1_count = draw_fc1_count(jax.random.fold_in(splits[11], 71), 0)
    fc1_bias = scatter_about(splits[6], (FF,), 0.5, 3.0, ((0, 2),), jnp.float32)
    fc2_tiles = scatter_about(splits[7], (N_BLK, N_FFN, SLOTS, TB, TB), (FF // 4) ** -0.5, 0.09375, ((0, 16), (1, 2)))
    fc2_index = draw_fc2_index(jax.random.fold_in(splits[11], 71), 0)
    fc2_count = draw_fc2_count(jax.random.fold_in(splits[11], 71), 0)
    fc2_bias = scatter_about(splits[10], (D,), 0.5, 3.0, ((0, 2),), jnp.float32)
    return {"tokens": tokens, "ln_gain": ln_gain, "ln_bias": ln_bias, "fc1_tiles": fc1_tiles, "fc1_index": fc1_index, "fc1_count": fc1_count, "fc1_bias": fc1_bias, "fc2_tiles": fc2_tiles, "fc2_index": fc2_index, "fc2_count": fc2_count, "fc2_bias": fc2_bias}


def dense_group(tile_data, slot_pos, live_count, group, rows, cols):
    flat = tile_data[:, group].reshape(N_BLK * SLOTS, TB, TB).astype(jnp.float32)
    alive = (jnp.arange(SLOTS)[None, :] < live_count[:, group][:, None]).reshape(-1)
    places = slot_pos[:, group].reshape(-1).astype(jnp.int32)
    grid = jnp.zeros((rows * cols, TB, TB), jnp.float32)
    grid = grid.at[places].add(jnp.where(alive[:, None, None], flat, jnp.float32(0.0)))
    grid = grid.reshape(rows, cols, TB, TB).transpose(0, 2, 1, 3).reshape(rows * TB, cols * TB)
    return grid.astype(jnp.bfloat16)

def reference(tokens, ln_gain, ln_bias, fc1_tiles, fc1_index, fc1_count, fc1_bias, fc2_tiles, fc2_index, fc2_count, fc2_bias):
    rows_f = tokens.astype(jnp.float32)
    center = lax.optimization_barrier(jnp.mean(rows_f, axis=1, keepdims=True))
    spread = lax.optimization_barrier(jnp.mean((rows_f - center) ** 2, axis=1, keepdims=True))
    normed = ((rows_f - center) / jnp.sqrt(spread + 1e-05) * ln_gain + ln_bias).astype(jnp.bfloat16)
    branch = jnp.zeros((TOKENS, D), jnp.float32)
    for group in range(N_FFN):
        first = dense_group(fc1_tiles, fc1_index, fc1_count, group, RB, CB)
        hidden = jnp.dot(normed, first, preferred_element_type=jnp.float32) + fc1_bias[group * FFS:(group + 1) * FFS]
        hidden = jnp.maximum(hidden, 0.0).astype(jnp.bfloat16)
        second = dense_group(fc2_tiles, fc2_index, fc2_count, group, CB, RB)
        partial_f = jnp.dot(hidden, second, preferred_element_type=jnp.float32).astype(jnp.bfloat16)
        branch = branch + partial_f.astype(jnp.float32)
    return (rows_f + branch + fc2_bias).astype(jnp.bfloat16)
```

```python
import functools

import jax
import jax.numpy as jnp
from jax import lax
from jax.experimental import pallas as pl
from jax.experimental.pallas import tpu as pltpu
from jax.sharding import PartitionSpec as P

UNROLL = 4
VMEM_BYTES = 56 * 1024 * 1024


def add_tiles(row_ref, col_ref, live, base, x_ref, w_ref, acc):
    def one(slot):
        row, col = row_ref[base + slot], col_ref[base + slot]
        return col, jnp.dot(x_ref[row], w_ref[0, 0, slot], preferred_element_type=jnp.float32)

    def several(step, carry):
        products = [one(step * UNROLL + u) for u in range(UNROLL)]
        for col, product in products:
            acc[col] += product
        return carry

    def single(slot, carry):
        col, product = one(slot)
        acc[col] += product
        return carry

    whole = lax.div(live, jnp.int32(UNROLL))
    lax.fori_loop(0, whole, several, 0)
    lax.fori_loop(whole * UNROLL, live, single, 0)


def first_kernel(row_ref, col_ref, count_ref, x_ref, bias_ref, w_ref, out_ref, acc):
    step = pl.program_id(0)
    blocks = acc.shape[0]

    @pl.when(step == 0)
    def _():
        def fill(c, carry):
            acc[c] = jnp.broadcast_to(bias_ref[c], acc.shape[1:])
            return carry

        lax.fori_loop(0, blocks, fill, 0)

    add_tiles(row_ref, col_ref, count_ref[step], step * w_ref.shape[2], x_ref, w_ref, acc)

    @pl.when(step == pl.num_programs(0) - 1)
    def _():
        def finish(c, carry):
            out_ref[c] = jnp.maximum(acc[c], 0.0).astype(out_ref.dtype)
            return carry

        lax.fori_loop(0, blocks, finish, 0)


def second_kernel(row_ref, col_ref, count_ref, x_ref, sum_ref, w_ref, out_ref, acc):
    step = pl.program_id(0)
    blocks = acc.shape[0]

    @pl.when(step == 0)
    def _():
        acc[...] = sum_ref[...]

    add_tiles(row_ref, col_ref, count_ref[step], step * w_ref.shape[2], x_ref, w_ref, acc)

    @pl.when(step == pl.num_programs(0) - 1)
    def _():
        if len(out_ref.shape) == 3:
            out_ref[...] = acc[...]
        else:
            width = acc.shape[2]
            for c in range(blocks):
                out_ref[:, c * width : (c + 1) * width] = acc[c].astype(out_ref.dtype)


def whole_block(shape):
    return pl.BlockSpec(shape, lambda i, *_: (0,) * len(shape))


def tile_pass(kernel, rows, cols, counts, x, start, tiles, out_shape, blocks):
    shards, slots, side = tiles.shape[0], tiles.shape[2], tiles.shape[3]
    tokens = x.shape[1]
    return pl.pallas_call(
        kernel,
        out_shape=out_shape,
        grid_spec=pltpu.PrefetchScalarGridSpec(
            num_scalar_prefetch=3,
            grid=(shards,),
            in_specs=[
                whole_block(x.shape),
                whole_block(start.shape),
                pl.BlockSpec((1, 1, slots, side, side), lambda i, *_: (i, 0, 0, 0, 0)),
            ],
            out_specs=whole_block(out_shape.shape),
            scratch_shapes=[pltpu.VMEM((blocks, tokens, side), jnp.float32)],
        ),
        compiler_params=pltpu.CompilerParams(vmem_limit_bytes=VMEM_BYTES),
        cost_estimate=pl.CostEstimate(
            flops=8 * shards * slots * tokens * side * side,
            bytes_accessed=shards * slots * side * side * 2,
            transcendentals=0,
        ),
    )(rows.reshape(-1), cols.reshape(-1), counts, x, start, tiles)


def on_device(
    tokens,
    ln_gain,
    ln_bias,
    fc1_tiles,
    fc1_index,
    fc1_count,
    fc1_bias,
    fc2_tiles,
    fc2_index,
    fc2_count,
    fc2_bias,
    ffn_size,
):
    side = fc1_tiles.shape[-1]
    slots = fc1_tiles.shape[2]
    token_rows, width = tokens.shape
    first_blocks = fc1_bias.shape[0] // side
    second_blocks = width // side

    gathered1 = lax.all_gather(fc1_tiles, "blk", axis=0, tiled=True)
    cuts = [0, slots // 2, slots - slots // 6, slots]
    gathered2 = [
        lax.all_gather(fc2_tiles[:, :, lo:hi], "blk", axis=0, tiled=True)
        for lo, hi in zip(cuts[:-1], cuts[1:])
    ]
    meta = jnp.concatenate(
        [fc1_index[:, 0], fc2_index[:, 0], fc1_count, fc2_count], axis=1
    )
    meta = lax.all_gather(meta, "blk", axis=0, tiled=True)
    index1, index2 = meta[:, :slots], meta[:, slots : 2 * slots]
    count1, count2 = meta[:, 2 * slots], meta[:, 2 * slots + 1]

    rows_f = tokens.astype(jnp.float32)
    center = jnp.mean(rows_f, axis=1, keepdims=True)
    spread = jnp.mean((rows_f - center) ** 2, axis=1, keepdims=True)
    normed = ((rows_f - center) / jnp.sqrt(spread + 1e-05) * ln_gain + ln_bias).astype(jnp.bfloat16)
    normed_blocks = normed.reshape(token_rows, second_blocks, side).transpose(1, 0, 2)

    hidden = tile_pass(
        first_kernel,
        index1 // first_blocks,
        index1 % first_blocks,
        count1,
        normed_blocks,
        fc1_bias.reshape(first_blocks, 1, side),
        gathered1,
        jax.ShapeDtypeStruct((first_blocks, token_rows, side), jnp.bfloat16),
        first_blocks,
    )

    partial_value = jnp.zeros((second_blocks, token_rows, side), jnp.float32)
    for part, (lo, hi) in enumerate(zip(cuts[:-1], cuts[1:])):
        last = part == len(gathered2) - 1
        shape = (
            jax.ShapeDtypeStruct((token_rows, width), jnp.bfloat16)
            if last
            else jax.ShapeDtypeStruct(partial_value.shape, jnp.float32)
        )
        partial_value = tile_pass(
            second_kernel,
            index2[:, lo:hi] // second_blocks,
            index2[:, lo:hi] % second_blocks,
            jnp.clip(count2 - lo, 0, hi - lo),
            hidden,
            partial_value,
            gathered2[part],
            shape,
            second_blocks,
        )

    me = lax.axis_index("ffn")
    share = width // ffn_size
    branch = lax.dynamic_slice_in_dim(partial_value, me * share, share, 1).astype(jnp.float32)
    for shift in range(1, ffn_size):
        to = lax.rem(me + shift, ffn_size)
        piece = lax.dynamic_slice_in_dim(partial_value, to * share, share, 1)
        arrived = lax.ppermute(
            piece, "ffn", [(i, (i + shift) % ffn_size) for i in range(ffn_size)]
        )
        branch = branch + arrived.astype(jnp.float32)
    own_cols = lax.dynamic_slice_in_dim(rows_f, me * share, share, 1)
    return (own_cols + branch + fc2_bias).astype(jnp.bfloat16)


def solution(mesh):
    placed = (
        P("blk", None),
        P(),
        P(),
        P("blk", "ffn", None, None, None),
        P("blk", "ffn", None),
        P("blk", "ffn"),
        P("ffn"),
        P("blk", "ffn", None, None, None),
        P("blk", "ffn", None),
        P("blk", "ffn"),
        P("ffn"),
    )
    return jax.shard_map(
        functools.partial(on_device, ffn_size=mesh.shape["ffn"]),
        mesh=mesh,
        in_specs=placed,
        out_specs=P("blk", "ffn"),
        check_vma=False,
    )
```

```python
import functools

import jax
import jax.numpy as jnp
from jax import lax
from jax.experimental import pallas as pl
from jax.experimental.pallas import tpu as pltpu
from jax.sharding import PartitionSpec as P

UNROLL = 4
VMEM_BYTES = 56 * 1024 * 1024


def add_tiles(row_ref, col_ref, live, base, x_ref, w_ref, acc):
    def one(slot):
        row, col = row_ref[base + slot], col_ref[base + slot]
        return col, jnp.dot(x_ref[row], w_ref[0, 0, slot], preferred_element_type=jnp.float32)

    def several(step, carry):
        products = [one(step * UNROLL + u) for u in range(UNROLL)]
        for col, product in products:
            acc[col] += product
        return carry

    def single(slot, carry):
        col, product = one(slot)
        acc[col] += product
        return carry

    whole = lax.div(live, jnp.int32(UNROLL))
    lax.fori_loop(0, whole, several, 0)
    lax.fori_loop(whole * UNROLL, live, single, 0)


def pass_kernel(row_ref, col_ref, count_ref, x_ref, sum_ref, w_ref, out_ref, acc):
    step = pl.program_id(0)
    blocks = acc.shape[0]

    @pl.when(step == 0)
    def _():
        acc[...] = sum_ref[...]

    add_tiles(row_ref, col_ref, count_ref[step], step * w_ref.shape[2], x_ref, w_ref, acc)

    @pl.when(step == pl.num_programs(0) - 1)
    def _():
        if len(out_ref.shape) == 3:
            out_ref[...] = acc[...]
        else:
            width = acc.shape[2]
            for c in range(blocks):
                out_ref[:, c * width : (c + 1) * width] = acc[c].astype(out_ref.dtype)


def tile_pass(rows, cols, counts, x, start, tiles, rows_of=None):
    shards, slots, side = tiles.shape[0], tiles.shape[2], tiles.shape[3]
    blocks, tokens = start.shape[0], x.shape[1]
    place = 0
    out_shape = jax.ShapeDtypeStruct(start.shape, jnp.float32)
    if rows_of is not None:
        place, tokens = rows_of[0] // rows_of[1], rows_of[1]
        out_shape = jax.ShapeDtypeStruct((tokens, blocks * side), jnp.bfloat16)
    return pl.pallas_call(
        pass_kernel,
        out_shape=out_shape,
        grid_spec=pltpu.PrefetchScalarGridSpec(
            num_scalar_prefetch=3,
            grid=(shards,),
            in_specs=[
                pl.BlockSpec((x.shape[0], tokens, side), lambda i, *_: (0, place, 0)),
                pl.BlockSpec((blocks, tokens, side), lambda i, *_: (0, place, 0)),
                pl.BlockSpec((1, 1, slots, side, side), lambda i, *_: (i, 0, 0, 0, 0)),
            ],
            out_specs=pl.BlockSpec(out_shape.shape, lambda i, *_: (0,) * len(out_shape.shape)),
            scratch_shapes=[pltpu.VMEM((blocks, tokens, side), jnp.float32)],
        ),
        compiler_params=pltpu.CompilerParams(vmem_limit_bytes=VMEM_BYTES),
        cost_estimate=pl.CostEstimate(
            flops=8 * shards * slots * tokens * side * side,
            bytes_accessed=shards * slots * side * side * 2,
            transcendentals=0,
        ),
    )(rows.reshape(-1), cols.reshape(-1), counts, x, start, tiles)


def pick(mask, size, values):
    marks = mask.astype(jnp.int32)
    rank = jnp.cumsum(marks, axis=-1) - marks
    hit = mask[..., None, :] & (rank[..., None, :] == jnp.arange(size, dtype=jnp.int32)[:, None])
    return jnp.sum(jnp.where(hit, values[..., None, :], 0), axis=-1)


def after(mask, size):
    marks = mask.astype(jnp.int32)
    return mask & (jnp.cumsum(marks, axis=-1) - marks >= size)


def norm(tokens, gain, bias, side):
    rows_f = tokens.astype(jnp.float32)
    center = jnp.mean(rows_f, axis=1, keepdims=True)
    spread = jnp.mean((rows_f - center) ** 2, axis=1, keepdims=True)
    normed = ((rows_f - center) / jnp.sqrt(spread + 1e-05) * gain + bias).astype(jnp.bfloat16)
    return normed.reshape(tokens.shape[0], -1, side).transpose(1, 0, 2)


def on_device(
    tokens,
    ln_gain,
    ln_bias,
    fc1_tiles,
    fc1_index,
    fc1_count,
    fc1_bias,
    fc2_tiles,
    fc2_index,
    fc2_count,
    fc2_bias,
    blk_size,
    ffn_size,
):
    side = fc1_tiles.shape[-1]
    slots = fc1_tiles.shape[2]
    token_rows, width = tokens.shape
    first_blocks = fc1_bias.shape[0] // side
    second_blocks = width // side
    half_blocks = (first_blocks + 1) // 2
    half_size = blk_size // 2
    listed = min(slots, -(-slots * 5 // 8))
    spare = slots - listed
    blk, ffn = lax.axis_index("blk"), lax.axis_index("ffn")
    half = lax.div(blk, half_size)
    halves = [list(range(half_size)), list(range(half_size, blk_size))]
    across = [(i, (i + half_size) % blk_size) for i in range(blk_size)]
    slot_ids = jnp.arange(slots, dtype=jnp.int32)

    def first_place(p):
        row, col = p // first_blocks, p % first_blocks
        group = (col >= half_blocks).astype(jnp.int32)
        return group, row, col - group * half_blocks

    def second_place(p):
        row, col = p // second_blocks, p % second_blocks
        group = (row >= half_blocks).astype(jnp.int32)
        return group, row - group * half_blocks, col

    def split(tiles, index, count, place):
        live = slot_ids < count[0, 0]
        group = place(index[0, 0])[0]
        mine, other = live & (group == half), live & (group != half)
        order = pick(jnp.stack([mine, other]), listed, slot_ids[None])
        kept = jnp.take(tiles[0, 0], order[0], axis=0, mode="clip")[None, None]
        sent = jnp.take(tiles[0, 0], order[1], axis=0, mode="clip")[None, None]
        left = pick(after(mine, listed) | after(other, listed), max(spare, 1), slot_ids)
        return kept, lax.ppermute(sent, "blk", across), left

    def share_out(tiles):
        return lax.all_gather(tiles, "blk", axis=0, axis_index_groups=halves, tiled=True)

    kept1, got1, left1 = split(fc1_tiles, fc1_index, fc1_count, first_place)
    kept2, got2, left2 = split(fc2_tiles, fc2_index, fc2_count, second_place)
    other_tokens = lax.ppermute(tokens, "blk", across)
    kept1, kept2 = share_out(kept1), share_out(kept2)
    got1, got2 = share_out(got1), share_out(got2)

    meta = jnp.concatenate([fc1_index[:, 0], fc2_index[:, 0], fc1_count, fc2_count], axis=1)
    meta = lax.all_gather(meta, ("blk", "ffn"), axis=0, tiled=True)
    meta = meta.reshape(blk_size, ffn_size, -1)
    own_meta = lax.dynamic_index_in_dim(meta, ffn, 1, keepdims=False)

    def lists(index, counts, place):
        group, row, col = place(index)
        wanted = (slot_ids < counts[:, None]) & (group == half)
        total = jnp.sum(wanted.astype(jnp.int32), axis=1)
        fields = [
            pick(wanted, listed, row),
            pick(wanted, listed, col),
            jnp.minimum(total, listed),
        ]
        kept = [lax.dynamic_slice_in_dim(f, half * half_size, half_size) for f in fields]
        got = [lax.dynamic_slice_in_dim(f, (1 - half) * half_size, half_size) for f in fields]
        late = after(wanted, listed)
        left = [
            pick(late, max(spare, 1), row),
            pick(late, max(spare, 1), col),
            jnp.maximum(total - listed, 0),
        ]
        return kept, got, left

    def overflow(index, counts, place):
        group = place(index)[0]
        live = slot_ids < counts[..., None]
        ones = jnp.sum((live & (group == 1)).astype(jnp.int32), axis=-1)
        return jnp.any(jnp.maximum(ones, counts - ones) > listed)

    fields1 = lists(own_meta[:, :slots], own_meta[:, 2 * slots], first_place)
    fields2 = lists(own_meta[:, slots : 2 * slots], own_meta[:, 2 * slots + 1], second_place)
    over1 = overflow(meta[..., :slots], meta[..., 2 * slots], first_place)
    over2 = overflow(meta[..., slots : 2 * slots], meta[..., 2 * slots + 1], second_place)

    def with_left(over, tiles, order, fields, x, start):
        if spare == 0:
            return start

        def extra(x, start):
            rest = jnp.take(tiles[0, 0], order, axis=0, mode="clip")[None, None]
            return tile_pass(*fields, x, start, lax.all_gather(rest, "blk", axis=0, tiled=True))

        return lax.cond(over, extra, lambda x, start: start, x, start)

    normed = jnp.concatenate(
        [norm(tokens, ln_gain, ln_bias, side), norm(other_tokens, ln_gain, ln_bias, side)], axis=1
    )
    bias = jnp.pad(fc1_bias, (0, (2 * half_blocks - first_blocks) * side))
    bias = lax.dynamic_slice_in_dim(bias, half * half_blocks * side, half_blocks * side)
    total = jnp.broadcast_to(bias.reshape(-1, 1, side), (half_blocks, 2 * token_rows, side))
    total = with_left(over1, fc1_tiles, left1, fields1[2], normed, total)
    total = tile_pass(*fields1[0], normed, total, kept1)
    total = tile_pass(*fields1[1], normed, total, got1)
    hidden = jnp.maximum(total, 0.0).astype(jnp.bfloat16)

    total = jnp.zeros((second_blocks, 2 * token_rows, side), jnp.float32)
    total = with_left(over2, fc2_tiles, left2, fields2[2], hidden, total)
    total = tile_pass(*fields2[0], hidden, total, kept2)
    other_part = tile_pass(*fields2[1], hidden, total, got2, (token_rows, token_rows))
    own_part = tile_pass(*fields2[1], hidden, total, got2, (0, token_rows))

    share = width // ffn_size

    def over_ffn(part):
        branch = lax.dynamic_slice_in_dim(part, ffn * share, share, 1).astype(jnp.float32)
        for shift in range(1, ffn_size):
            to = lax.rem(ffn + shift, ffn_size)
            arrived = lax.ppermute(
                lax.dynamic_slice_in_dim(part, to * share, share, 1),
                "ffn",
                [(i, (i + shift) % ffn_size) for i in range(ffn_size)],
            )
            branch = branch + arrived.astype(jnp.float32)
        return branch

    from_other = lax.ppermute(over_ffn(other_part).astype(jnp.bfloat16), "blk", across)
    branch = over_ffn(own_part) + from_other.astype(jnp.float32)
    own_cols = lax.dynamic_slice_in_dim(tokens, ffn * share, share, 1).astype(jnp.float32)
    return (own_cols + branch + fc2_bias).astype(jnp.bfloat16)


def solution(mesh):
    placed = (
        P("blk", None),
        P(),
        P(),
        P("blk", "ffn", None, None, None),
        P("blk", "ffn", None),
        P("blk", "ffn"),
        P("ffn"),
        P("blk", "ffn", None, None, None),
        P("blk", "ffn", None),
        P("blk", "ffn"),
        P("ffn"),
    )
    return jax.shard_map(
        functools.partial(on_device, blk_size=mesh.shape["blk"], ffn_size=mesh.shape["ffn"]),
        mesh=mesh,
        in_specs=placed,
        out_specs=P("blk", "ffn"),
        check_vma=False,
    )
```

```python
import functools

import jax
import jax.numpy as jnp
from jax import lax
from jax.experimental import pallas as pl
from jax.experimental.pallas import tpu as pltpu
from jax.sharding import PartitionSpec as P

UNROLL = 4
VMEM_BYTES = 56 * 1024 * 1024


def add_tiles(row_ref, col_ref, live, base, x_ref, w_ref, acc):
    def one(slot):
        row, col = row_ref[base + slot], col_ref[base + slot]
        return col, jnp.dot(x_ref[row], w_ref[0, 0, slot], preferred_element_type=jnp.float32)

    def several(step, carry):
        products = [one(step * UNROLL + u) for u in range(UNROLL)]
        for col, product in products:
            acc[col] += product
        return carry

    def single(slot, carry):
        col, product = one(slot)
        acc[col] += product
        return carry

    whole = lax.div(live, jnp.int32(UNROLL))
    lax.fori_loop(0, whole, several, 0)
    lax.fori_loop(whole * UNROLL, live, single, 0)


def second_kernel(row_ref, col_ref, count_ref, x_ref, sum_ref, w_ref, out_ref, acc):
    step = pl.program_id(0)
    blocks = acc.shape[0]

    @pl.when(step == 0)
    def _():
        acc[...] = sum_ref[...]

    add_tiles(row_ref, col_ref, count_ref[step], step * w_ref.shape[2], x_ref, w_ref, acc)

    @pl.when(step == pl.num_programs(0) - 1)
    def _():
        if out_ref.dtype == jnp.float32:
            out_ref[...] = acc[...]
        elif len(out_ref.shape) == 3:
            for c in range(blocks):
                out_ref[c] = jnp.maximum(acc[c], 0.0).astype(out_ref.dtype)
        else:
            width = acc.shape[2]
            for c in range(blocks):
                out_ref[:, c * width : (c + 1) * width] = acc[c].astype(out_ref.dtype)


def whole_block(shape):
    return pl.BlockSpec(shape, lambda i, *_: (0,) * len(shape))


def tile_pass(kernel, rows, cols, counts, x, start, tiles, out_shape, blocks):
    shards, slots, side = tiles.shape[0], tiles.shape[2], tiles.shape[3]
    tokens = x.shape[1]
    return pl.pallas_call(
        kernel,
        out_shape=out_shape,
        grid_spec=pltpu.PrefetchScalarGridSpec(
            num_scalar_prefetch=3,
            grid=(shards,),
            in_specs=[
                whole_block(x.shape),
                whole_block(start.shape),
                pl.BlockSpec((1, 1, slots, side, side), lambda i, *_: (i, 0, 0, 0, 0)),
            ],
            out_specs=whole_block(out_shape.shape),
            scratch_shapes=[pltpu.VMEM((blocks, tokens, side), jnp.float32)],
        ),
        compiler_params=pltpu.CompilerParams(vmem_limit_bytes=VMEM_BYTES),
        cost_estimate=pl.CostEstimate(
            flops=8 * shards * slots * tokens * side * side,
            bytes_accessed=shards * slots * side * side * 2,
            transcendentals=0,
        ),
    )(rows.reshape(-1), cols.reshape(-1), counts, x, start, tiles)


def on_device(
    tokens,
    ln_gain,
    ln_bias,
    fc1_tiles,
    fc1_index,
    fc1_count,
    fc1_bias,
    fc2_tiles,
    fc2_index,
    fc2_count,
    fc2_bias,
    blk_size,
    ffn_size,
):
    side = fc1_tiles.shape[-1]
    slots = fc1_tiles.shape[2]
    token_rows, width = tokens.shape
    first_blocks = fc1_bias.shape[0] // side
    second_blocks = width // side
    both = ("blk", "ffn")
    part_size = blk_size // ffn_size
    blk, ffn = lax.axis_index("blk"), lax.axis_index("ffn")
    part = lax.div(blk, part_size)

    def device(h, j, f):
        return (h * part_size + j) * ffn_size + f

    ids = [(h, j, f) for h in range(ffn_size) for j in range(part_size) for f in range(ffn_size)]
    swap = [(device(h, j, f), device(f, j, h)) for h, j, f in ids]
    parts = [[device(h, j, f) for j in range(part_size) for f in range(ffn_size)] for h in range(ffn_size)]

    def swapped(value):
        return lax.ppermute(value, both, swap)

    def gathered(value):
        return lax.all_gather(value, both, axis=0, axis_index_groups=parts, tiled=True)

    meta = jnp.concatenate([fc1_index[:, 0], fc2_index[:, 0], fc1_count, fc2_count], axis=1)
    meta = gathered(swapped(meta))
    index1, index2 = meta[:, :slots], meta[:, slots : 2 * slots]
    count1, count2 = meta[:, 2 * slots], meta[:, 2 * slots + 1]

    cuts1 = [0, slots // 2, slots]
    cuts2 = [0, slots // 2, slots]
    tiles1 = [gathered(swapped(fc1_tiles[:, :, lo:hi])) for lo, hi in zip(cuts1[:-1], cuts1[1:])]
    tiles2 = [gathered(swapped(fc2_tiles[:, :, lo:hi])) for lo, hi in zip(cuts2[:-1], cuts2[1:])]

    rows_f = swapped(tokens).astype(jnp.float32)
    center = jnp.mean(rows_f, axis=1, keepdims=True)
    spread = jnp.mean((rows_f - center) ** 2, axis=1, keepdims=True)
    normed = ((rows_f - center) / jnp.sqrt(spread + 1e-05) * ln_gain + ln_bias).astype(jnp.bfloat16)
    normed_blocks = normed.reshape(token_rows, second_blocks, side).transpose(1, 0, 2)

    def passes(x, total, tiles, cuts, index, counts, blocks, last_shape):
        for number, (lo, hi) in enumerate(zip(cuts[:-1], cuts[1:])):
            last = number == len(tiles) - 1
            total = tile_pass(
                second_kernel,
                index[:, lo:hi] // blocks,
                index[:, lo:hi] % blocks,
                jnp.clip(counts - lo, 0, hi - lo),
                x,
                total,
                tiles[number],
                last_shape if last else jax.ShapeDtypeStruct(total.shape, jnp.float32),
                blocks,
            )
        return total

    bias = swapped(fc1_bias).reshape(first_blocks, 1, side)
    total = jnp.broadcast_to(bias, (first_blocks, token_rows, side))
    hidden = passes(
        normed_blocks, total, tiles1, cuts1, index1, count1, first_blocks,
        jax.ShapeDtypeStruct(total.shape, jnp.bfloat16),
    )
    total = jnp.zeros((second_blocks, token_rows, side), jnp.float32)
    partial_value = passes(
        hidden, total, tiles2, cuts2, index2, count2, second_blocks,
        jax.ShapeDtypeStruct((token_rows, width), jnp.bfloat16),
    )

    share = width // ffn_size
    branch = jnp.zeros((token_rows, share), jnp.float32)
    for shift in range(ffn_size):
        to = lax.rem(part + shift, ffn_size)
        piece = lax.dynamic_slice_in_dim(partial_value, to * share, share, 1)
        route = [(device(h, j, f), device(f, j, (h + shift) % ffn_size)) for h, j, f in ids]
        branch = branch + lax.ppermute(piece, both, route).astype(jnp.float32)
    own_cols = lax.dynamic_slice_in_dim(tokens, ffn * share, share, 1).astype(jnp.float32)
    return (own_cols + branch + fc2_bias).astype(jnp.bfloat16)


def solution(mesh):
    placed = (
        P("blk", None),
        P(),
        P(),
        P("blk", "ffn", None, None, None),
        P("blk", "ffn", None),
        P("blk", "ffn"),
        P("ffn"),
        P("blk", "ffn", None, None, None),
        P("blk", "ffn", None),
        P("blk", "ffn"),
        P("ffn"),
    )
    return jax.shard_map(
        functools.partial(on_device, blk_size=mesh.shape["blk"], ffn_size=mesh.shape["ffn"]),
        mesh=mesh,
        in_specs=placed,
        out_specs=P("blk", "ffn"),
        check_vma=False,
    )
```

```python
import functools

import jax
import jax.numpy as jnp
from jax import lax
from jax.experimental import pallas as pl
from jax.experimental.pallas import tpu as pltpu
from jax.sharding import PartitionSpec as P

UNROLL = 4
VMEM_BYTES = 56 * 1024 * 1024


def add_tiles(row_ref, col_ref, first, last, base, x_ref, w_ref, acc):
    def one(slot):
        row, col = row_ref[base + slot], col_ref[base + slot]
        acc[col] += jnp.dot(x_ref[row], w_ref[0, 0, slot], preferred_element_type=jnp.float32)

    def several(step, carry):
        for u in range(UNROLL):
            one(first + step * UNROLL + u)
        return carry

    def single(slot, carry):
        one(slot)
        return carry

    whole = lax.div(jnp.maximum(last - first, 0), jnp.int32(UNROLL))
    lax.fori_loop(0, whole, several, 0)
    lax.fori_loop(first + whole * UNROLL, last, single, 0)


def add_block(row_ref, col_ref, first_ref, last_ref, x_ref, w_ref, acc):
    step = pl.program_id(0)
    base = step * w_ref.shape[2]
    add_tiles(row_ref, col_ref, first_ref[step], last_ref[step], base, x_ref, w_ref, acc)


def at_end(work):
    pl.when(pl.program_id(0) == pl.num_programs(0) - 1)(work)


def hidden_kernel(row_ref, col_ref, first_ref, last_ref, at_ref, x_ref, w_ref, bias_ref, out_ref, acc):
    blocks = acc.shape[0]

    @pl.when(pl.program_id(0) == 0)
    def _():
        def fill(c, carry):
            acc[c] = jnp.broadcast_to(bias_ref[c], acc.shape[1:])
            return carry

        lax.fori_loop(0, blocks, fill, 0)

    add_block(row_ref, col_ref, first_ref, last_ref, x_ref, w_ref, acc)

    @at_end
    def _():
        def finish(c, carry):
            out_ref[c] = jnp.maximum(acc[c], 0.0).astype(out_ref.dtype)
            return carry

        lax.fori_loop(0, blocks, finish, 0)


def partial_kernel(row_ref, col_ref, first_ref, last_ref, at_ref, x_ref, w_ref, sum_ref, out_ref, acc):
    @pl.when(pl.program_id(0) == 0)
    def _():
        acc[...] = jnp.zeros_like(acc)

    add_block(row_ref, col_ref, first_ref, last_ref, x_ref, w_ref, acc)

    @at_end
    def _():
        width = acc.shape[2]
        sum_ref[...] = acc[...]
        for c in range(acc.shape[0]):
            out_ref[:, c * width : (c + 1) * width] = acc[c].astype(out_ref.dtype)


def result_kernel(
    row_ref, col_ref, first_ref, last_ref, at_ref,
    x_ref, w_ref, sum_ref, token_ref, other_ref, bias_ref, out_ref, acc,
):
    @pl.when(pl.program_id(0) == 0)
    def _():
        acc[...] = sum_ref[...]

    add_block(row_ref, col_ref, first_ref, last_ref, x_ref, w_ref, acc)

    @at_end
    def _():
        width = acc.shape[2]
        for c in range(acc.shape[0]):
            cols = slice(c * width, (c + 1) * width)
            branch = acc[c] + other_ref[:, cols]
            value = token_ref[:, cols].astype(jnp.float32) + branch + bias_ref[:, cols]
            out_ref[:, cols] = value.astype(out_ref.dtype)


def fixed(shape):
    return pl.BlockSpec(shape, lambda i, *_: (0,) * len(shape))


def tile_pass(kernel, rows, cols, first, last, at, x, tiles, more, more_specs, out_shapes, blocks):
    shards, slots, side = tiles.shape[0], tiles.shape[2], tiles.shape[3]
    tokens = x.shape[1]
    out_specs = [fixed(o.shape) for o in out_shapes]
    return pl.pallas_call(
        kernel,
        out_shape=out_shapes,
        grid_spec=pltpu.PrefetchScalarGridSpec(
            num_scalar_prefetch=5,
            grid=(shards,),
            in_specs=[
                fixed(x.shape),
                pl.BlockSpec((1, 1, slots, side, side), lambda i, *_: (i, 0, 0, 0, 0)),
                *more_specs,
            ],
            out_specs=out_specs,
            scratch_shapes=[pltpu.VMEM((blocks, tokens, side), jnp.float32)],
        ),
        compiler_params=pltpu.CompilerParams(vmem_limit_bytes=VMEM_BYTES),
        cost_estimate=pl.CostEstimate(
            flops=8 * shards * slots * tokens * side * side,
            bytes_accessed=shards * slots * side * side * 2,
            transcendentals=0,
        ),
    )(rows.reshape(-1), cols.reshape(-1), first, last, at.reshape(1), x, tiles, *more)


def on_device(
    tokens,
    ln_gain,
    ln_bias,
    fc1_tiles,
    fc1_index,
    fc1_count,
    fc1_bias,
    fc2_tiles,
    fc2_index,
    fc2_count,
    fc2_bias,
    ffn_size,
):
    side = fc1_tiles.shape[-1]
    slots = fc1_tiles.shape[2]
    shards = lax.axis_size("blk")
    token_rows, width = tokens.shape
    first_blocks = fc1_bias.shape[0] // side
    second_blocks = width // side
    share = width // ffn_size
    ffn = lax.axis_index("ffn")
    slot_ids = jnp.arange(slots, dtype=jnp.int32)
    aligned = share % side == 0
    early = slots - slots * 7 // 20

    def in_share(index, at):
        if not aligned:
            return jnp.zeros(index.shape, jnp.bool_)
        return index % second_blocks // (share // side) == at

    def ordered(index, count, values):
        live = slot_ids < count[:, None]
        own = in_share(index, ffn)
        other = (live & ~own).astype(jnp.int32)
        mine = (live & own).astype(jnp.int32)
        others = jnp.sum(other, axis=1, keepdims=True)
        place = jnp.where(own, others + jnp.cumsum(mine, axis=1) - 1, jnp.cumsum(other, axis=1) - 1)
        hit = live[:, None, :] & (place[:, None, :] == slot_ids[:, None])
        return jnp.sum(jnp.where(hit, values[:, None, :], 0), axis=2), others[:, 0]

    def gathered(value):
        return lax.all_gather(value, "blk", axis=0, tiled=True)

    tiles1 = gathered(fc1_tiles)
    order, _ = ordered(fc2_index[:, 0], fc2_count[:, 0], slot_ids[None])
    pieces = [
        jnp.take(fc2_tiles[0, 0], part, axis=0, mode="clip")[None, None]
        for part in (order[0, :early], order[0, early:])
    ]
    tiles2a, tiles2b = gathered(pieces[0]), gathered(pieces[1])

    meta = jnp.concatenate([fc1_index[:, 0], fc2_index[:, 0], fc1_count, fc2_count], axis=1)
    meta = lax.all_gather(meta, ("blk", "ffn"), axis=0, tiled=True).reshape(shards, ffn_size, -1)
    all_index2, all_count2 = meta[..., slots : 2 * slots], meta[..., 2 * slots + 1]
    all_other = (slot_ids < all_count2[..., None]) & ~in_share(
        all_index2, jnp.arange(ffn_size, dtype=jnp.int32)[:, None]
    )
    some_late = jnp.any(jnp.sum(all_other.astype(jnp.int32), axis=2) > early)
    meta = lax.dynamic_index_in_dim(meta, ffn, 1, keepdims=False)
    index1, count1, count2 = meta[:, :slots], meta[:, 2 * slots], meta[:, 2 * slots + 1]
    index2, others = ordered(meta[:, slots : 2 * slots], count2, meta[:, slots : 2 * slots])
    none = jnp.zeros_like(count1)

    rows_f = tokens.astype(jnp.float32)
    center = jnp.mean(rows_f, axis=1, keepdims=True)
    spread = jnp.mean((rows_f - center) ** 2, axis=1, keepdims=True)
    normed = ((rows_f - center) / jnp.sqrt(spread + 1e-05) * ln_gain + ln_bias).astype(jnp.bfloat16)
    normed_blocks = normed.reshape(token_rows, second_blocks, side).transpose(1, 0, 2)

    (hidden,) = tile_pass(
        hidden_kernel,
        index1 // first_blocks,
        index1 % first_blocks,
        none,
        count1,
        ffn,
        normed_blocks,
        tiles1,
        [fc1_bias.reshape(first_blocks, 1, side)],
        [fixed((first_blocks, 1, side))],
        [jax.ShapeDtypeStruct((first_blocks, token_rows, side), jnp.bfloat16)],
        first_blocks,
    )

    def second_pass(lo, hi, first, last, tiles):
        return tile_pass(
            partial_kernel,
            index2[:, lo:hi] // second_blocks,
            index2[:, lo:hi] % second_blocks,
            first,
            last,
            ffn,
            hidden,
            tiles,
            [],
            [],
            [
                jax.ShapeDtypeStruct((second_blocks, token_rows, side), jnp.float32),
                jax.ShapeDtypeStruct((token_rows, width), jnp.bfloat16),
            ],
            second_blocks,
        )

    def from_others(partial_value):
        branch = jnp.zeros((token_rows, share), jnp.float32)
        for shift in range(1, ffn_size):
            to = lax.rem(ffn + shift, ffn_size)
            arrived = lax.ppermute(
                lax.dynamic_slice_in_dim(partial_value, to * share, share, 1),
                "ffn",
                [(i, (i + shift) % ffn_size) for i in range(ffn_size)],
            )
            branch = branch + arrived.astype(jnp.float32)
        return branch

    count2a, count2b = jnp.minimum(count2, early), jnp.maximum(count2 - early, 0)
    total, partial_value = second_pass(0, early, none, count2a, tiles2a)

    if not aligned:
        more, late_value = second_pass(early, slots, none, count2b, tiles2b)
        both = total + more
        partial_value = both.transpose(1, 0, 2).reshape(token_rows, width).astype(jnp.bfloat16)
        own = lax.dynamic_slice_in_dim(partial_value, ffn * share, share, 1).astype(jnp.float32)
        own_cols = lax.dynamic_slice_in_dim(rows_f, ffn * share, share, 1)
        return (own_cols + own + from_others(partial_value) + fc2_bias).astype(jnp.bfloat16)

    branch = from_others(partial_value)
    late = jnp.maximum(others - early, 0)

    def with_late(branch, hidden, tiles):
        return branch + from_others(second_pass(early, slots, none, late, tiles)[1])

    branch = lax.cond(some_late, with_late, lambda branch, *_: branch, branch, hidden, tiles2b)
    share_blocks = share // side
    (result,) = tile_pass(
        result_kernel,
        index2[:, early:] // second_blocks,
        index2[:, early:] % second_blocks % share_blocks,
        late,
        count2b,
        ffn,
        hidden,
        tiles2b,
        [total, tokens, branch, fc2_bias.reshape(1, share)],
        [
            pl.BlockSpec((share_blocks, token_rows, side), lambda i, r, c, f, l, at: (at[0], 0, 0)),
            pl.BlockSpec((token_rows, share), lambda i, r, c, f, l, at: (0, at[0])),
            fixed((token_rows, share)),
            fixed((1, share)),
        ],
        [jax.ShapeDtypeStruct((token_rows, share), jnp.bfloat16)],
        share_blocks,
    )
    return result


def solution(mesh):
    placed = (
        P("blk", None),
        P(),
        P(),
        P("blk", "ffn", None, None, None),
        P("blk", "ffn", None),
        P("blk", "ffn"),
        P("ffn"),
        P("blk", "ffn", None, None, None),
        P("blk", "ffn", None),
        P("blk", "ffn"),
        P("ffn"),
    )
    return jax.shard_map(
        functools.partial(on_device, ffn_size=mesh.shape["ffn"]),
        mesh=mesh,
        in_specs=placed,
        out_specs=P("blk", "ffn"),
        check_vma=False,
    )
```

```python
import functools

import jax
import jax.numpy as jnp
from jax import lax
from jax.experimental import pallas as pl
from jax.experimental.pallas import tpu as pltpu
from jax.sharding import PartitionSpec as P

UNROLL = 4
STEPS = 4
VMEM_BYTES = 56 * 1024 * 1024


def pair_up(rows, cols, live, blocks, zero_row):
    listed = rows.shape[1]
    ids = jnp.arange(listed, dtype=jnp.int32)
    block_ids = jnp.arange(blocks, dtype=jnp.int32)
    size = -(-((listed + min(blocks, listed)) // 2) // UNROLL) * UNROLL
    same = live[:, None, :] & (cols[:, :, None] == cols[:, None, :]) & (ids < ids[:, None])
    rank = jnp.sum(same.astype(jnp.int32), axis=2)
    in_block = live[:, None, :] & (cols[:, None, :] == block_ids[:, None])
    need = (jnp.sum(in_block.astype(jnp.int32), axis=2) + 1) // 2
    begin = jnp.cumsum(need, axis=1) - need
    begin = jnp.sum(jnp.where(cols[:, :, None] == block_ids, begin[:, None, :], 0), axis=2)
    place = jnp.where(live, begin + rank // 2, -1)
    hit = place[:, None, :] == jnp.arange(size, dtype=jnp.int32)[:, None]
    odd = (rank % 2 == 1)[:, None, :]

    def chosen(mask, values, default):
        found = jnp.sum(jnp.where(mask, values[:, None, :] - default, 0), axis=2)
        return found + default

    tile_ids = jnp.broadcast_to(ids, rows.shape)
    fields = [
        chosen(hit & ~odd, tile_ids, 0),
        chosen(hit & ~odd, rows, zero_row),
        chosen(hit & odd, tile_ids, 0),
        chosen(hit & odd, rows, zero_row),
        chosen(hit & ~odd, cols, 0),
    ]
    return jnp.stack(fields).reshape(-1), jnp.sum(need, axis=1)


def add_block(field_ref, count_ref, x_ref, w_ref, acc):
    step, steps = pl.program_id(0), pl.num_programs(0)
    size = field_ref.shape[0] // (5 * steps)

    def pair(at):
        tile0, row0, tile1, row1, col = (field_ref[(f * steps + step) * size + at] for f in range(5))
        left = jnp.concatenate([x_ref[row0], x_ref[row1]], axis=1)
        right = jnp.concatenate([w_ref[tile0], w_ref[tile1]], axis=0)
        acc[col] += jnp.dot(left, right, preferred_element_type=jnp.float32)

    def several(turn, carry):
        for u in range(UNROLL):
            pair(turn * UNROLL + u)
        return carry

    lax.fori_loop(0, lax.div(count_ref[step] + UNROLL - 1, jnp.int32(UNROLL)), several, 0)


def at_end(work):
    pl.when(pl.program_id(0) == pl.num_programs(0) - 1)(work)


def hidden_kernel(field_ref, count_ref, at_ref, x_ref, w_ref, bias_ref, out_ref, acc):
    blocks = acc.shape[0]

    @pl.when(pl.program_id(0) == 0)
    def _():
        def fill(c, carry):
            acc[c] = jnp.broadcast_to(bias_ref[c], acc.shape[1:])
            return carry

        lax.fori_loop(0, blocks, fill, 0)

    add_block(field_ref, count_ref, x_ref, w_ref, acc)

    @at_end
    def _():
        def finish(c, carry):
            out_ref[c] = jnp.maximum(acc[c], 0.0).astype(out_ref.dtype)
            return carry

        lax.fori_loop(0, blocks, finish, 0)
        out_ref[blocks] = jnp.zeros(out_ref.shape[1:], out_ref.dtype)


def partial_kernel(field_ref, count_ref, at_ref, x_ref, w_ref, sum_ref, out_ref, acc):
    @pl.when(pl.program_id(0) == 0)
    def _():
        acc[...] = jnp.zeros_like(acc)

    add_block(field_ref, count_ref, x_ref, w_ref, acc)

    @at_end
    def _():
        width = acc.shape[2]
        sum_ref[...] = acc[...]
        for c in range(acc.shape[0]):
            out_ref[:, c * width : (c + 1) * width] = acc[c].astype(out_ref.dtype)


def result_kernel(
    field_ref, count_ref, at_ref,
    x_ref, w_ref, sum_ref, token_ref, other_ref, bias_ref, out_ref, acc,
):
    @pl.when(pl.program_id(0) == 0)
    def _():
        acc[...] = sum_ref[...]

    add_block(field_ref, count_ref, x_ref, w_ref, acc)

    @at_end
    def _():
        width = acc.shape[2]
        for c in range(acc.shape[0]):
            cols = slice(c * width, (c + 1) * width)
            branch = acc[c] + other_ref[:, cols]
            value = token_ref[:, cols].astype(jnp.float32) + branch + bias_ref[:, cols]
            out_ref[:, cols] = value.astype(out_ref.dtype)


def fixed(shape):
    return pl.BlockSpec(shape, lambda i, *_: (0,) * len(shape))


def tile_pass(kernel, rows, cols, live, at, x, tiles, more, more_specs, out_shapes, blocks):
    shards, slots = rows.shape
    side, tokens = tiles.shape[-1], x.shape[1]
    steps = STEPS if shards % STEPS == 0 else 1
    listed = shards // steps * slots
    per_step = lambda v: v.reshape(steps, listed)
    fields, counts = pair_up(per_step(rows), per_step(cols), per_step(live), blocks, x.shape[0] - 1)
    return pl.pallas_call(
        kernel,
        out_shape=out_shapes,
        grid_spec=pltpu.PrefetchScalarGridSpec(
            num_scalar_prefetch=3,
            grid=(steps,),
            in_specs=[
                fixed(x.shape),
                pl.BlockSpec((listed, side, side), lambda i, *_: (i, 0, 0)),
                *more_specs,
            ],
            out_specs=[fixed(o.shape) for o in out_shapes],
            scratch_shapes=[pltpu.VMEM((blocks, tokens, side), jnp.float32)],
        ),
        compiler_params=pltpu.CompilerParams(vmem_limit_bytes=VMEM_BYTES),
        cost_estimate=pl.CostEstimate(
            flops=4 * shards * slots * tokens * side * side,
            bytes_accessed=shards * slots * side * side * 2,
            transcendentals=0,
        ),
    )(fields, counts, at.reshape(1), x, tiles.reshape(-1, side, side), *more)


def on_device(
    tokens,
    ln_gain,
    ln_bias,
    fc1_tiles,
    fc1_index,
    fc1_count,
    fc1_bias,
    fc2_tiles,
    fc2_index,
    fc2_count,
    fc2_bias,
    ffn_size,
):
    side = fc1_tiles.shape[-1]
    slots = fc1_tiles.shape[2]
    shards = lax.axis_size("blk")
    token_rows, width = tokens.shape
    first_blocks = fc1_bias.shape[0] // side
    second_blocks = width // side
    share = width // ffn_size
    ffn = lax.axis_index("ffn")
    slot_ids = jnp.arange(slots, dtype=jnp.int32)
    aligned = share % side == 0
    early = slots - slots * 7 // 20

    def in_share(index, at):
        if not aligned:
            return jnp.zeros(index.shape, jnp.bool_)
        return index % second_blocks // (share // side) == at

    def ordered(index, count, values):
        live = slot_ids < count[:, None]
        own = in_share(index, ffn)
        other = (live & ~own).astype(jnp.int32)
        mine = (live & own).astype(jnp.int32)
        others = jnp.sum(other, axis=1, keepdims=True)
        place = jnp.where(own, others + jnp.cumsum(mine, axis=1) - 1, jnp.cumsum(other, axis=1) - 1)
        hit = live[:, None, :] & (place[:, None, :] == slot_ids[:, None])
        return jnp.sum(jnp.where(hit, values[:, None, :], 0), axis=2), others[:, 0]

    def gathered(value):
        return lax.all_gather(value, "blk", axis=0, tiled=True)

    tiles1 = gathered(fc1_tiles)
    order, _ = ordered(fc2_index[:, 0], fc2_count[:, 0], slot_ids[None])
    pieces = [
        jnp.take(fc2_tiles[0, 0], part, axis=0, mode="clip")[None, None]
        for part in (order[0, :early], order[0, early:])
    ]
    tiles2a, tiles2b = gathered(pieces[0]), gathered(pieces[1])

    meta = jnp.concatenate([fc1_index[:, 0], fc2_index[:, 0], fc1_count, fc2_count], axis=1)
    meta = lax.all_gather(meta, ("blk", "ffn"), axis=0, tiled=True).reshape(shards, ffn_size, -1)
    all_index2, all_count2 = meta[..., slots : 2 * slots], meta[..., 2 * slots + 1]
    all_other = (slot_ids < all_count2[..., None]) & ~in_share(
        all_index2, jnp.arange(ffn_size, dtype=jnp.int32)[:, None]
    )
    some_late = jnp.any(jnp.sum(all_other.astype(jnp.int32), axis=2) > early)
    meta = lax.dynamic_index_in_dim(meta, ffn, 1, keepdims=False)
    index1, count1, count2 = meta[:, :slots], meta[:, 2 * slots], meta[:, 2 * slots + 1]
    index2, others = ordered(meta[:, slots : 2 * slots], count2, meta[:, slots : 2 * slots])

    rows_f = tokens.astype(jnp.float32)
    center = jnp.mean(rows_f, axis=1, keepdims=True)
    spread = jnp.mean((rows_f - center) ** 2, axis=1, keepdims=True)
    normed = ((rows_f - center) / jnp.sqrt(spread + 1e-05) * ln_gain + ln_bias).astype(jnp.bfloat16)
    normed_blocks = normed.reshape(token_rows, second_blocks, side).transpose(1, 0, 2)
    normed_blocks = jnp.pad(normed_blocks, ((0, 1), (0, 0), (0, 0)))

    (hidden,) = tile_pass(
        hidden_kernel,
        index1 // first_blocks,
        index1 % first_blocks,
        slot_ids < count1[:, None],
        ffn,
        normed_blocks,
        tiles1,
        [fc1_bias.reshape(first_blocks, 1, side)],
        [fixed((first_blocks, 1, side))],
        [jax.ShapeDtypeStruct((first_blocks + 1, token_rows, side), jnp.bfloat16)],
        first_blocks,
    )

    def second_pass(lo, hi, before, tiles):
        return tile_pass(
            partial_kernel,
            index2[:, lo:hi] // second_blocks,
            index2[:, lo:hi] % second_blocks,
            slot_ids[lo:hi] < before[:, None],
            ffn,
            hidden,
            tiles,
            [],
            [],
            [
                jax.ShapeDtypeStruct((second_blocks, token_rows, side), jnp.float32),
                jax.ShapeDtypeStruct((token_rows, width), jnp.bfloat16),
            ],
            second_blocks,
        )

    def from_others(partial_value):
        branch = jnp.zeros((token_rows, share), jnp.float32)
        for shift in range(1, ffn_size):
            to = lax.rem(ffn + shift, ffn_size)
            arrived = lax.ppermute(
                lax.dynamic_slice_in_dim(partial_value, to * share, share, 1),
                "ffn",
                [(i, (i + shift) % ffn_size) for i in range(ffn_size)],
            )
            branch = branch + arrived.astype(jnp.float32)
        return branch

    total, partial_value = second_pass(0, early, count2, tiles2a)

    if not aligned:
        more, late_value = second_pass(early, slots, count2, tiles2b)
        both = total + more
        partial_value = both.transpose(1, 0, 2).reshape(token_rows, width).astype(jnp.bfloat16)
        own = lax.dynamic_slice_in_dim(partial_value, ffn * share, share, 1).astype(jnp.float32)
        own_cols = lax.dynamic_slice_in_dim(rows_f, ffn * share, share, 1)
        return (own_cols + own + from_others(partial_value) + fc2_bias).astype(jnp.bfloat16)

    branch = from_others(partial_value)

    def with_late(branch, hidden, tiles):
        return branch + from_others(second_pass(early, slots, others, tiles)[1])

    branch = lax.cond(some_late, with_late, lambda branch, *_: branch, branch, hidden, tiles2b)
    share_blocks = share // side
    (result,) = tile_pass(
        result_kernel,
        index2[:, early:] // second_blocks,
        index2[:, early:] % second_blocks % share_blocks,
        (slot_ids[early:] < count2[:, None]) & (slot_ids[early:] >= others[:, None]),
        ffn,
        hidden,
        tiles2b,
        [total, tokens, branch, fc2_bias.reshape(1, share)],
        [
            pl.BlockSpec((share_blocks, token_rows, side), lambda i, fields, counts, at: (at[0], 0, 0)),
            pl.BlockSpec((token_rows, share), lambda i, fields, counts, at: (0, at[0])),
            fixed((token_rows, share)),
            fixed((1, share)),
        ],
        [jax.ShapeDtypeStruct((token_rows, share), jnp.bfloat16)],
        share_blocks,
    )
    return result


def solution(mesh):
    placed = (
        P("blk", None),
        P(),
        P(),
        P("blk", "ffn", None, None, None),
        P("blk", "ffn", None),
        P("blk", "ffn"),
        P("ffn"),
        P("blk", "ffn", None, None, None),
        P("blk", "ffn", None),
        P("blk", "ffn"),
        P("ffn"),
    )
    return jax.shard_map(
        functools.partial(on_device, ffn_size=mesh.shape["ffn"]),
        mesh=mesh,
        in_specs=placed,
        out_specs=P("blk", "ffn"),
        check_vma=False,
    )
```

```python
import functools

import jax
import jax.numpy as jnp
from jax import lax
from jax.experimental import pallas as pl
from jax.experimental.pallas import tpu as pltpu
from jax.sharding import PartitionSpec as P

UNROLL = 4
STEPS = 4
VMEM_BYTES = 56 * 1024 * 1024


def pair_up(rows, cols, live, blocks, zero_row):
    listed = rows.shape[1]
    ids = jnp.arange(listed, dtype=jnp.int32)
    block_ids = jnp.arange(blocks, dtype=jnp.int32)
    size = -(-((listed + min(blocks, listed)) // 2) // UNROLL) * UNROLL
    same = live[:, None, :] & (cols[:, :, None] == cols[:, None, :]) & (ids < ids[:, None])
    rank = jnp.sum(same.astype(jnp.int32), axis=2)
    in_block = live[:, None, :] & (cols[:, None, :] == block_ids[:, None])
    need = (jnp.sum(in_block.astype(jnp.int32), axis=2) + 1) // 2
    begin = jnp.cumsum(need, axis=1) - need
    begin = jnp.sum(jnp.where(cols[:, :, None] == block_ids, begin[:, None, :], 0), axis=2)
    place = jnp.where(live, begin + rank // 2, -1)
    hit = place[:, None, :] == jnp.arange(size, dtype=jnp.int32)[:, None]
    odd = (rank % 2 == 1)[:, None, :]

    def chosen(mask, values, default):
        found = jnp.sum(jnp.where(mask, values[:, None, :] - default, 0), axis=2)
        return found + default

    tile_ids = jnp.broadcast_to(ids, rows.shape)
    fields = [
        chosen(hit & ~odd, tile_ids, 0),
        chosen(hit & ~odd, rows, zero_row),
        chosen(hit & odd, tile_ids, 0),
        chosen(hit & odd, rows, zero_row),
        chosen(hit & ~odd, cols, 0),
    ]
    return jnp.stack(fields).reshape(-1), jnp.sum(need, axis=1)


def add_block(field_ref, count_ref, x_ref, w_ref, acc):
    step, steps = pl.program_id(0), pl.num_programs(0)
    w_ref = w_ref.reshape(-1, *w_ref.shape[2:])
    size = field_ref.shape[0] // (5 * steps)

    def pair(at):
        tile0, row0, tile1, row1, col = (field_ref[(f * steps + step) * size + at] for f in range(5))
        left = jnp.concatenate([x_ref[row0], x_ref[row1]], axis=1)
        right = jnp.concatenate([w_ref[tile0], w_ref[tile1]], axis=0)
        acc[col] += jnp.dot(left, right, preferred_element_type=jnp.float32)

    def several(turn, carry):
        for u in range(UNROLL):
            pair(turn * UNROLL + u)
        return carry

    lax.fori_loop(0, lax.div(count_ref[step] + UNROLL - 1, jnp.int32(UNROLL)), several, 0)


def at_end(work):
    pl.when(pl.program_id(0) == pl.num_programs(0) - 1)(work)


def first_kernel(field_ref, count_ref, at_ref, x_ref, w_ref, bias_ref, sum_ref, acc):
    @pl.when(pl.program_id(0) == 0)
    def _():
        def fill(c, carry):
            acc[c] = jnp.broadcast_to(bias_ref[c], acc.shape[1:])
            return carry

        lax.fori_loop(0, acc.shape[0], fill, 0)

    add_block(field_ref, count_ref, x_ref, w_ref, acc)

    @at_end
    def _():
        sum_ref[...] = acc[...]


def hidden_kernel(field_ref, count_ref, at_ref, x_ref, w_ref, sum_ref, out_ref, acc):
    blocks = acc.shape[0]

    @pl.when(pl.program_id(0) == 0)
    def _():
        acc[...] = sum_ref[...]

    add_block(field_ref, count_ref, x_ref, w_ref, acc)

    @at_end
    def _():
        def finish(c, carry):
            out_ref[c] = jnp.maximum(acc[c], 0.0).astype(out_ref.dtype)
            return carry

        lax.fori_loop(0, blocks, finish, 0)
        out_ref[blocks] = jnp.zeros(out_ref.shape[1:], out_ref.dtype)


def partial_kernel(field_ref, count_ref, at_ref, x_ref, w_ref, sum_ref, out_ref, acc):
    @pl.when(pl.program_id(0) == 0)
    def _():
        acc[...] = jnp.zeros_like(acc)

    add_block(field_ref, count_ref, x_ref, w_ref, acc)

    @at_end
    def _():
        width = acc.shape[2]
        sum_ref[...] = acc[...]
        for c in range(acc.shape[0]):
            out_ref[:, c * width : (c + 1) * width] = acc[c].astype(out_ref.dtype)


def result_kernel(
    field_ref, count_ref, at_ref,
    x_ref, w_ref, sum_ref, token_ref, other_ref, bias_ref, out_ref, acc,
):
    @pl.when(pl.program_id(0) == 0)
    def _():
        acc[...] = sum_ref[...]

    add_block(field_ref, count_ref, x_ref, w_ref, acc)

    @at_end
    def _():
        width = acc.shape[2]
        for c in range(acc.shape[0]):
            cols = slice(c * width, (c + 1) * width)
            branch = acc[c] + other_ref[:, cols]
            value = token_ref[:, cols].astype(jnp.float32) + branch + bias_ref[:, cols]
            out_ref[:, cols] = value.astype(out_ref.dtype)


def fixed(shape):
    return pl.BlockSpec(shape, lambda i, *_: (0,) * len(shape))


def tile_pass(kernel, rows, cols, live, at, x, tiles, more, more_specs, out_shapes, blocks):
    shards, slots = rows.shape
    side, tokens = tiles.shape[-1], x.shape[1]
    steps = STEPS if shards % STEPS == 0 else 1
    listed = shards // steps * slots
    per_step = lambda v: v.reshape(steps, listed)
    fields, counts = pair_up(per_step(rows), per_step(cols), per_step(live), blocks, x.shape[0] - 1)
    return pl.pallas_call(
        kernel,
        out_shape=out_shapes,
        grid_spec=pltpu.PrefetchScalarGridSpec(
            num_scalar_prefetch=3,
            grid=(steps,),
            in_specs=[
                fixed(x.shape),
                pl.BlockSpec((shards // steps, slots, side, side), lambda i, *_: (i, 0, 0, 0)),
                *more_specs,
            ],
            out_specs=[fixed(o.shape) for o in out_shapes],
            scratch_shapes=[pltpu.VMEM((blocks, tokens, side), jnp.float32)],
        ),
        compiler_params=pltpu.CompilerParams(vmem_limit_bytes=VMEM_BYTES),
        cost_estimate=pl.CostEstimate(
            flops=4 * shards * slots * tokens * side * side,
            bytes_accessed=shards * slots * side * side * 2,
            transcendentals=0,
        ),
    )(fields, counts, at.reshape(1), x, tiles, *more)


def swapped(values, stride):
    return values.reshape(-1, 2, stride, *values.shape[1:])[:, ::-1].reshape(values.shape)


def moved(values, by):
    ids = jnp.arange(values.shape[1], dtype=jnp.int32)
    hit = (ids[:, None] - by[:, None, None]) == ids
    return jnp.sum(jnp.where(hit, values[:, None, :], 0), axis=2)


def on_device(
    tokens,
    ln_gain,
    ln_bias,
    fc1_tiles,
    fc1_index,
    fc1_count,
    fc1_bias,
    fc2_tiles,
    fc2_index,
    fc2_count,
    fc2_bias,
    ffn_size,
):
    side = fc1_tiles.shape[-1]
    slots = fc1_tiles.shape[2]
    shards = lax.axis_size("blk")
    token_rows, width = tokens.shape
    first_blocks = fc1_bias.shape[0] // side
    second_blocks = width // side
    share = width // ffn_size
    blk, ffn = lax.axis_index("blk"), lax.axis_index("ffn")
    aligned = share % side == 0
    opening = slots * 4 // 5
    rest = slots - opening
    held = slots - slots // 40
    late_from = held - slots // 3
    levels = [
        (stride, max(slots // most, 1), max(slots // least, 1))
        for stride, most, least in ((1, 6, 8), (2, 8, 10), (4, 12, 16))
        if shards % (2 * stride) == 0
    ]
    slot_ids = jnp.arange(slots, dtype=jnp.int32)
    stream_ids = jnp.arange(rest + slots, dtype=jnp.int32)

    def gathered(value):
        return lax.all_gather(value, "blk", axis=0, tiled=True).reshape(shards, -1, side, side)

    tiles1 = gathered(fc1_tiles[0, 0, :opening])
    meta = jnp.concatenate([fc1_index[:, 0], fc2_index[:, 0], fc1_count, fc2_count], axis=1)
    meta = lax.all_gather(meta, "blk", axis=0, tiled=True)
    index1, index2 = meta[:, :slots], meta[:, slots : 2 * slots]
    count1, count2 = meta[:, 2 * slots], meta[:, 2 * slots + 1]
    left1 = jnp.maximum(count1 - opening, 0)

    def in_own_share(index):
        if not aligned:
            return jnp.zeros(index.shape, jnp.bool_)
        return index % second_blocks // (share // side) == ffn

    def streams(index, count, left, first_values, values):
        live = slot_ids < count[:, None]
        own = in_own_share(index)
        front, back = live & ~own, live & own
        front_place = left[:, None] + jnp.cumsum(front.astype(jnp.int32), axis=1) - 1
        back_place = jnp.cumsum(back.astype(jnp.int32), axis=1) - 1

        def placed(mask, place):
            hit = mask[:, None, :] & (place[:, None, :] == stream_ids[:, None])
            return jnp.sum(jnp.where(hit, values[:, None, :], 0), axis=2)

        first = jnp.where(stream_ids < left[:, None], jnp.pad(first_values, ((0, 0), (0, slots))), 0)
        return (
            first + placed(front, front_place),
            placed(back, back_place),
            left + jnp.sum(front.astype(jnp.int32), axis=1),
            jnp.sum(back.astype(jnp.int32), axis=1),
        )

    front, back, fronts, backs = streams(
        index2, count2, left1, jnp.zeros((shards, rest), jnp.int32), index2
    )
    own_left = jnp.maximum(fc1_count[:, 0] - opening, 0)
    own_front, own_back, _, _ = streams(
        fc2_index[:, 0], fc2_count[:, 0], own_left, jnp.arange(rest, dtype=jnp.int32)[None], rest + slot_ids[None]
    )
    own_front, own_back = own_front[0], own_back[0]
    sources = jnp.concatenate([fc1_tiles[0, 0, opening:], fc2_tiles[0, 0]], axis=0)

    def evened(values, numbers, fixed_numbers, stride, most):
        partners = swapped(numbers, stride)
        sent = jnp.clip((numbers - partners) // 2, 0, jnp.minimum(most, numbers - fixed_numbers))
        kept = numbers - sent
        got = swapped(sent, stride)
        arrived = moved(swapped(values, stride), kept - (partners - got))
        return jnp.where(stream_ids < kept[:, None], values, arrived), kept, kept + got

    def tail(stream, kept, most):
        return lax.dynamic_slice_in_dim(jnp.pad(stream, (0, most)), kept, most)

    for stride, most_front, most_back in levels:
        front, kept_front, fronts = evened(front, fronts, left1, stride, most_front)
        back, kept_back, backs = evened(back, backs, jnp.zeros_like(backs), stride, most_back)
        kept_front, kept_back = kept_front[blk], kept_back[blk]
        sending = jnp.concatenate(
            [tail(own_front, kept_front, most_front), tail(own_back, kept_back, most_back)]
        )
        arrived = lax.ppermute(
            jnp.take(sources, sending, axis=0, mode="clip"),
            "blk",
            [(i, i ^ stride) for i in range(shards)],
        )
        so_far = sources.shape[0]
        own_front = jnp.where(stream_ids < kept_front, own_front, so_far + stream_ids - kept_front)
        own_back = jnp.where(stream_ids < kept_back, own_back, so_far + most_front + stream_ids - kept_back)
        sources = jnp.concatenate([sources, arrived], axis=0)

    total_ids = jnp.arange(2 * stream_ids.shape[0] + slots // 4, dtype=jnp.int32)
    double = ((0, 0), (0, total_ids.shape[0] - stream_ids.shape[0]))
    lengths = fronts + backs
    codes = jnp.where(
        total_ids < fronts[:, None], jnp.pad(front, double), moved(jnp.pad(back, double), fronts)
    )
    own_fronts = fronts[blk]
    order = jnp.where(
        total_ids < own_fronts,
        jnp.pad(own_front, double[1]),
        moved(jnp.pad(own_back, double[1])[None], own_fronts[None])[0],
    )
    tiles2a = gathered(jnp.take(sources, order[:late_from], axis=0, mode="clip"))
    tiles2b = gathered(jnp.take(sources, order[late_from:held], axis=0, mode="clip"))
    chunk = slots // 4
    misplaced = jnp.stack([jnp.max(fronts) - late_from, jnp.max(lengths) - held])
    misplaced = lax.pmax(misplaced, "ffn")
    some_late = jnp.max(misplaced) > 0

    rows_f = tokens.astype(jnp.float32)
    center = jnp.mean(rows_f, axis=1, keepdims=True)
    spread = jnp.mean((rows_f - center) ** 2, axis=1, keepdims=True)
    normed = ((rows_f - center) / jnp.sqrt(spread + 1e-05) * ln_gain + ln_bias).astype(jnp.bfloat16)
    normed_blocks = normed.reshape(token_rows, second_blocks, side).transpose(1, 0, 2)
    normed_blocks = jnp.pad(normed_blocks, ((0, 1), (0, 0), (0, 0)))

    (total,) = tile_pass(
        first_kernel,
        index1[:, :opening] // first_blocks,
        index1[:, :opening] % first_blocks,
        slot_ids[:opening] < count1[:, None],
        ffn,
        normed_blocks,
        tiles1,
        [fc1_bias.reshape(first_blocks, 1, side)],
        [fixed((first_blocks, 1, side))],
        [jax.ShapeDtypeStruct((first_blocks, token_rows, side), jnp.float32)],
        first_blocks,
    )
    (hidden,) = tile_pass(
        hidden_kernel,
        index1[:, opening:] // first_blocks,
        index1[:, opening:] % first_blocks,
        slot_ids[opening:] < count1[:, None],
        ffn,
        normed_blocks,
        tiles2a,
        [total],
        [fixed(total.shape)],
        [jax.ShapeDtypeStruct((first_blocks + 1, token_rows, side), jnp.bfloat16)],
        first_blocks,
    )

    def second_pass(places, live, tiles):
        return tile_pass(
            partial_kernel,
            places // second_blocks,
            places % second_blocks,
            live,
            ffn,
            hidden,
            tiles,
            [],
            [],
            [
                jax.ShapeDtypeStruct((second_blocks, token_rows, side), jnp.float32),
                jax.ShapeDtypeStruct((token_rows, width), jnp.bfloat16),
            ],
            second_blocks,
        )

    def own_cols(value):
        return lax.dynamic_slice_in_dim(value, ffn * share, share, 1).astype(jnp.float32)

    def from_others(partial_value):
        branch = jnp.zeros((token_rows, share), jnp.float32)
        for shift in range(1, ffn_size):
            to = lax.rem(ffn + shift, ffn_size)
            arrived = lax.ppermute(
                lax.dynamic_slice_in_dim(partial_value, to * share, share, 1),
                "ffn",
                [(i, (i + shift) % ffn_size) for i in range(ffn_size)],
            )
            branch = branch + arrived.astype(jnp.float32)
        return branch

    in_front = total_ids < fronts[:, None]
    in_second = (total_ids >= left1[:, None]) & (total_ids < lengths[:, None])
    total, partial_value = second_pass(codes[:, :late_from], in_second[:, :late_from], tiles2a)
    last_codes = codes[:, late_from:held]
    last_own = (in_second & ~in_front)[:, late_from:held]
    branch = from_others(partial_value)

    def with_late(branch):
        _, late = second_pass(last_codes, (in_second & in_front)[:, late_from:held], tiles2b)
        branch = branch + from_others(late) + own_cols(late)

        def one_more(number, branch):
            at = held + number * chunk
            here = jnp.take(sources, lax.dynamic_slice_in_dim(order, at, chunk), axis=0, mode="clip")
            part = [lax.dynamic_slice_in_dim(v, at, chunk, 1) for v in (codes, in_second)]
            _, extra = second_pass(*part, gathered(here))
            return branch + from_others(extra) + own_cols(extra)

        return lax.fori_loop(0, (misplaced[1] + chunk - 1) // chunk, one_more, branch)

    branch = lax.cond(some_late, with_late, lambda branch: branch, branch)

    if not aligned:
        more, _ = second_pass(last_codes, last_own, tiles2b)
        own = (total + more).transpose(1, 0, 2).reshape(token_rows, width)
        return (own_cols(tokens) + own_cols(own) + branch + fc2_bias).astype(jnp.bfloat16)

    share_blocks = share // side
    (result,) = tile_pass(
        result_kernel,
        last_codes // second_blocks,
        last_codes % second_blocks % share_blocks,
        last_own,
        ffn,
        hidden,
        tiles2b,
        [total, tokens, branch, fc2_bias.reshape(1, share)],
        [
            pl.BlockSpec((share_blocks, token_rows, side), lambda i, fields, counts, at: (at[0], 0, 0)),
            pl.BlockSpec((token_rows, share), lambda i, fields, counts, at: (0, at[0])),
            fixed((token_rows, share)),
            fixed((1, share)),
        ],
        [jax.ShapeDtypeStruct((token_rows, share), jnp.bfloat16)],
        share_blocks,
    )
    return result


def solution(mesh):
    placed = (
        P("blk", None),
        P(),
        P(),
        P("blk", "ffn", None, None, None),
        P("blk", "ffn", None),
        P("blk", "ffn"),
        P("ffn"),
        P("blk", "ffn", None, None, None),
        P("blk", "ffn", None),
        P("blk", "ffn"),
        P("ffn"),
    )
    return jax.shard_map(
        functools.partial(on_device, ffn_size=mesh.shape["ffn"]),
        mesh=mesh,
        in_specs=placed,
        out_specs=P("blk", "ffn"),
        check_vma=False,
    )
```

```python
import functools

import jax
import jax.numpy as jnp
from jax import lax
from jax.experimental import pallas as pl
from jax.experimental.pallas import tpu as pltpu
from jax.sharding import PartitionSpec as P

UNROLL = 4
VMEM_BYTES = 56 * 1024 * 1024
LAST_VMEM_BYTES = 36 * 1024 * 1024


def group_up(rows, cols, live, blocks, zero_row, group):
    listed = rows.shape[1]
    ids = jnp.arange(listed, dtype=jnp.int32)
    block_ids = jnp.arange(blocks, dtype=jnp.int32)
    most = (listed + (group - 1) * min(blocks, listed)) // group
    size = -(-most // UNROLL) * UNROLL
    same = live[:, None, :] & (cols[:, :, None] == cols[:, None, :]) & (ids < ids[:, None])
    rank = jnp.sum(same.astype(jnp.int32), axis=2)
    in_block = live[:, None, :] & (cols[:, None, :] == block_ids[:, None])
    need = (jnp.sum(in_block.astype(jnp.int32), axis=2) + group - 1) // group
    begin = jnp.cumsum(need, axis=1) - need
    begin = jnp.sum(jnp.where(cols[:, :, None] == block_ids, begin[:, None, :], 0), axis=2)
    place = jnp.where(live, begin + rank // group, -1)
    hit = place[:, None, :] == jnp.arange(size, dtype=jnp.int32)[:, None]
    turn = (rank % group)[:, None, :]

    def chosen(mask, values, default):
        found = jnp.sum(jnp.where(mask, values[:, None, :] - default, 0), axis=2)
        return found + default

    tile_ids = jnp.broadcast_to(ids, rows.shape)
    fields = [chosen(hit & (turn == 0), cols, 0)]
    fields += [chosen(hit & (turn == g), tile_ids, 0) for g in range(group)]
    fields += [chosen(hit & (turn == g), rows, zero_row) for g in range(group)]
    return jnp.stack(fields).reshape(-1), jnp.sum(need, axis=1)


def add_block(field_ref, count_ref, x_ref, w_ref, acc, group):
    step, steps = pl.program_id(0), pl.num_programs(0)
    w_ref = w_ref.reshape(-1, *w_ref.shape[2:])
    fields = 2 * group + 1
    size = field_ref.shape[0] // (fields * steps)

    def one(at):
        col, *parts = (field_ref[(f * steps + step) * size + at] for f in range(fields))
        left = jnp.concatenate([x_ref[row] for row in parts[group:]], axis=1)
        right = jnp.concatenate([w_ref[tile] for tile in parts[:group]], axis=0)
        acc[col] += jnp.dot(left, right, preferred_element_type=jnp.float32)

    def several(turn, carry):
        for u in range(UNROLL):
            one(turn * UNROLL + u)
        return carry

    lax.fori_loop(0, lax.div(count_ref[step] + UNROLL - 1, jnp.int32(UNROLL)), several, 0)


def at_end(work):
    pl.when(pl.program_id(0) == pl.num_programs(0) - 1)(work)


def first_kernel(group, field_ref, count_ref, at_ref, x_ref, w_ref, bias_ref, sum_ref, acc):
    @pl.when(pl.program_id(0) == 0)
    def _():
        def fill(c, carry):
            acc[c] = jnp.broadcast_to(bias_ref[c], acc.shape[1:])
            return carry

        lax.fori_loop(0, acc.shape[0], fill, 0)

    add_block(field_ref, count_ref, x_ref, w_ref, acc, group)

    @at_end
    def _():
        sum_ref[...] = acc[...]


def hidden_kernel(group, field_ref, count_ref, at_ref, x_ref, w_ref, sum_ref, out_ref, acc):
    blocks = acc.shape[0]

    @pl.when(pl.program_id(0) == 0)
    def _():
        acc[...] = sum_ref[...]

    add_block(field_ref, count_ref, x_ref, w_ref, acc, group)

    @at_end
    def _():
        def finish(c, carry):
            out_ref[c] = jnp.maximum(acc[c], 0.0).astype(out_ref.dtype)
            return carry

        lax.fori_loop(0, blocks, finish, 0)
        out_ref[blocks] = jnp.zeros(out_ref.shape[1:], out_ref.dtype)


def partial_kernel(group, field_ref, count_ref, at_ref, x_ref, w_ref, sum_ref, out_ref):
    @pl.when(pl.program_id(0) == 0)
    def _():
        sum_ref[...] = jnp.zeros_like(sum_ref)

    add_block(field_ref, count_ref, x_ref, w_ref, sum_ref, group)

    @at_end
    def _():
        width = sum_ref.shape[2]
        for c in range(sum_ref.shape[0]):
            out_ref[:, c * width : (c + 1) * width] = sum_ref[c].astype(out_ref.dtype)


def result_kernel(
    group, field_ref, count_ref, at_ref,
    x_ref, w_ref, sum_ref, token_ref, other_ref, bias_ref, out_ref, acc,
):
    @pl.when(pl.program_id(0) == 0)
    def _():
        acc[...] = sum_ref[...]

    add_block(field_ref, count_ref, x_ref, w_ref, acc, group)

    @at_end
    def _():
        width = acc.shape[2]
        for c in range(acc.shape[0]):
            cols = slice(c * width, (c + 1) * width)
            branch = acc[c] + other_ref[:, cols]
            value = token_ref[:, cols].astype(jnp.float32) + branch + bias_ref[:, cols]
            out_ref[:, cols] = value.astype(out_ref.dtype)


def fixed(shape):
    return pl.BlockSpec(shape, lambda i, *_: (0,) * len(shape), pipeline_mode=pl.Buffered(1))


def planned(rows, cols, live, blocks, zero_row, steps, group):
    steps = steps if rows.shape[0] % steps == 0 else 1
    return group_up(*(v.reshape(steps, -1) for v in (rows, cols, live)), blocks, zero_row, group)


def tile_pass(
    kernel, rows, cols, live, at, x, tiles, more, more_specs, out_shapes, blocks,
    steps=4, group=2, scratch=True, vmem=VMEM_BYTES, plan=None,
):
    shards, slots = rows.shape
    side, tokens = tiles.shape[-1], x.shape[1]
    steps = steps if shards % steps == 0 else 1
    if plan is None:
        plan = planned(rows, cols, live, blocks, x.shape[0] - 1, steps, group)
    fields, counts = plan
    return pl.pallas_call(
        functools.partial(kernel, group),
        out_shape=out_shapes,
        grid_spec=pltpu.PrefetchScalarGridSpec(
            num_scalar_prefetch=3,
            grid=(steps,),
            in_specs=[
                fixed(x.shape),
                pl.BlockSpec((shards // steps, slots, side, side), lambda i, *_: (i, 0, 0, 0)),
                *more_specs,
            ],
            out_specs=[
                pl.BlockSpec(o.shape, lambda i, *_, rank=len(o.shape): (0,) * rank) for o in out_shapes
            ],
            scratch_shapes=[pltpu.VMEM((blocks, tokens, side), jnp.float32)] if scratch else [],
        ),
        compiler_params=pltpu.CompilerParams(vmem_limit_bytes=vmem),
        cost_estimate=pl.CostEstimate(
            flops=4 * shards * slots * tokens * side * side,
            bytes_accessed=shards * slots * side * side * 2,
            transcendentals=0,
        ),
    )(fields, counts, at.reshape(1), x, tiles, *more)


def swapped(values, stride):
    return values.reshape(-1, 2, stride, *values.shape[1:])[:, ::-1].reshape(values.shape)


def moved(values, by):
    ids = jnp.arange(values.shape[1], dtype=jnp.int32)
    hit = (ids[:, None] - by[:, None, None]) == ids
    return jnp.sum(jnp.where(hit, values[:, None, :], 0), axis=2)


def on_device(
    tokens,
    ln_gain,
    ln_bias,
    fc1_tiles,
    fc1_index,
    fc1_count,
    fc1_bias,
    fc2_tiles,
    fc2_index,
    fc2_count,
    fc2_bias,
    ffn_size,
):
    side = fc1_tiles.shape[-1]
    slots = fc1_tiles.shape[2]
    shards = lax.axis_size("blk")
    token_rows, width = tokens.shape
    first_blocks = fc1_bias.shape[0] // side
    second_blocks = width // side
    share = width // ffn_size
    blk, ffn = lax.axis_index("blk"), lax.axis_index("ffn")
    aligned = share % side == 0
    opening = slots * 4 // 5
    rest = slots - opening
    held = slots
    late_from = held - slots * 3 // 10
    levels = [
        (stride, max(slots // most, 1), max(slots // least, 1))
        for stride, most, least in ((1, 6, 8), (2, 12, 16), (4, 16, 24))
        if shards % (2 * stride) == 0
    ]
    slot_ids = jnp.arange(slots, dtype=jnp.int32)
    stream_ids = jnp.arange(rest + slots, dtype=jnp.int32)

    def gathered(value):
        return lax.all_gather(value, "blk", axis=0, tiled=True).reshape(shards, -1, side, side)

    tiles1 = gathered(fc1_tiles[0, 0, :opening])
    meta = jnp.concatenate([fc1_index[:, 0], fc2_index[:, 0], fc1_count, fc2_count], axis=1)
    meta = lax.all_gather(meta, "blk", axis=0, tiled=True)
    index1, index2 = meta[:, :slots], meta[:, slots : 2 * slots]
    count1, count2 = meta[:, 2 * slots], meta[:, 2 * slots + 1]
    left1 = jnp.maximum(count1 - opening, 0)

    def in_own_share(index):
        if not aligned:
            return jnp.zeros(index.shape, jnp.bool_)
        return index % second_blocks // (share // side) == ffn

    def streams(index, count, left, first_values, values):
        live = slot_ids < count[:, None]
        own = in_own_share(index)
        front, back = live & ~own, live & own
        front_place = left[:, None] + jnp.cumsum(front.astype(jnp.int32), axis=1) - 1
        back_place = jnp.cumsum(back.astype(jnp.int32), axis=1) - 1

        def placed(mask, place):
            hit = mask[:, None, :] & (place[:, None, :] == stream_ids[:, None])
            return jnp.sum(jnp.where(hit, values[:, None, :], 0), axis=2)

        first = jnp.where(stream_ids < left[:, None], jnp.pad(first_values, ((0, 0), (0, slots))), 0)
        return (
            first + placed(front, front_place),
            placed(back, back_place),
            left + jnp.sum(front.astype(jnp.int32), axis=1),
            jnp.sum(back.astype(jnp.int32), axis=1),
        )

    front, back, fronts, backs = streams(
        index2, count2, left1, jnp.zeros((shards, rest), jnp.int32), index2
    )
    own_left = jnp.maximum(fc1_count[:, 0] - opening, 0)
    own_front, own_back, _, _ = streams(
        fc2_index[:, 0], fc2_count[:, 0], own_left, jnp.arange(rest, dtype=jnp.int32)[None], rest + slot_ids[None]
    )
    own_front, own_back = own_front[0], own_back[0]
    sources = jnp.concatenate([fc1_tiles[0, 0, opening:], fc2_tiles[0, 0]], axis=0)

    def evened(values, numbers, fixed_numbers, stride, most):
        partners = swapped(numbers, stride)
        sent = jnp.clip((numbers - partners) // 2, 0, jnp.minimum(most, numbers - fixed_numbers))
        kept = numbers - sent
        got = swapped(sent, stride)
        arrived = moved(swapped(values, stride), kept - (partners - got))
        return jnp.where(stream_ids < kept[:, None], values, arrived), kept, kept + got

    def tail(stream, kept, most):
        return lax.dynamic_slice_in_dim(jnp.pad(stream, (0, most)), kept, most)

    for stride, most_front, most_back in levels:
        front, kept_front, fronts = evened(front, fronts, left1, stride, most_front)
        back, kept_back, backs = evened(back, backs, jnp.zeros_like(backs), stride, most_back)
        kept_front, kept_back = kept_front[blk], kept_back[blk]
        sending = jnp.concatenate(
            [tail(own_front, kept_front, most_front), tail(own_back, kept_back, most_back)]
        )
        arrived = lax.ppermute(
            jnp.take(sources, sending, axis=0, mode="clip"),
            "blk",
            [(i, i ^ stride) for i in range(shards)],
        )
        so_far = sources.shape[0]
        own_front = jnp.where(stream_ids < kept_front, own_front, so_far + stream_ids - kept_front)
        own_back = jnp.where(stream_ids < kept_back, own_back, so_far + most_front + stream_ids - kept_back)
        sources = jnp.concatenate([sources, arrived], axis=0)

    total_ids = jnp.arange(2 * stream_ids.shape[0] + slots // 4, dtype=jnp.int32)
    double = ((0, 0), (0, total_ids.shape[0] - stream_ids.shape[0]))
    lengths = fronts + backs
    codes = jnp.where(
        total_ids < fronts[:, None], jnp.pad(front, double), moved(jnp.pad(back, double), fronts)
    )
    own_fronts = fronts[blk]
    order = jnp.where(
        total_ids < own_fronts,
        jnp.pad(own_front, double[1]),
        moved(jnp.pad(own_back, double[1])[None], own_fronts[None])[0],
    )
    tiles2a = gathered(jnp.take(sources, order[:late_from], axis=0, mode="clip"))
    tiles2b = gathered(jnp.take(sources, order[late_from:held], axis=0, mode="clip"))
    chunk = slots // 4
    misplaced = jnp.stack([jnp.max(fronts) - late_from, jnp.max(lengths) - held])
    misplaced = lax.pmax(misplaced, "ffn")

    rows_f = tokens.astype(jnp.float32)
    center = jnp.mean(rows_f, axis=1, keepdims=True)
    spread = jnp.mean((rows_f - center) ** 2, axis=1, keepdims=True)
    normed = ((rows_f - center) / jnp.sqrt(spread + 1e-05) * ln_gain + ln_bias).astype(jnp.bfloat16)
    normed_blocks = normed.reshape(token_rows, second_blocks, side).transpose(1, 0, 2)
    normed_blocks = jnp.pad(normed_blocks, ((0, 1), (0, 0), (0, 0)))
    normed_blocks, misplaced = lax.optimization_barrier((normed_blocks, misplaced))
    some_late = jnp.max(misplaced) > 0

    (total,) = tile_pass(
        first_kernel,
        index1[:, :opening] // first_blocks,
        index1[:, :opening] % first_blocks,
        slot_ids[:opening] < count1[:, None],
        ffn,
        normed_blocks,
        tiles1,
        [fc1_bias.reshape(first_blocks, 1, side)],
        [fixed((first_blocks, 1, side))],
        [jax.ShapeDtypeStruct((first_blocks, token_rows, side), jnp.float32)],
        first_blocks,
    )
    (hidden,) = tile_pass(
        hidden_kernel,
        index1[:, opening:] // first_blocks,
        index1[:, opening:] % first_blocks,
        slot_ids[opening:] < count1[:, None],
        ffn,
        normed_blocks,
        tiles2a,
        [total],
        [fixed(total.shape)],
        [jax.ShapeDtypeStruct((first_blocks + 1, token_rows, side), jnp.bfloat16)],
        first_blocks,
    )

    def second_pass(places, live, tiles):
        return tile_pass(
            partial_kernel,
            places // second_blocks,
            places % second_blocks,
            live,
            ffn,
            hidden,
            tiles,
            [],
            [],
            [
                jax.ShapeDtypeStruct((second_blocks, token_rows, side), jnp.float32),
                jax.ShapeDtypeStruct((token_rows, width), jnp.bfloat16),
            ],
            second_blocks,
            steps=2,
            group=4,
            scratch=False,
        )

    def own_cols(value):
        return lax.dynamic_slice_in_dim(value, ffn * share, share, 1).astype(jnp.float32)

    def from_others(partial_value):
        branch = jnp.zeros((token_rows, share), jnp.float32)
        for shift in range(1, ffn_size):
            to = lax.rem(ffn + shift, ffn_size)
            arrived = lax.ppermute(
                lax.dynamic_slice_in_dim(partial_value, to * share, share, 1),
                "ffn",
                [(i, (i + shift) % ffn_size) for i in range(ffn_size)],
            )
            branch = branch + arrived.astype(jnp.float32)
        return branch

    in_front = total_ids < fronts[:, None]
    in_second = (total_ids >= left1[:, None]) & (total_ids < lengths[:, None])
    total, partial_value = second_pass(codes[:, :late_from], in_second[:, :late_from], tiles2a)
    last_codes = codes[:, late_from:held]
    last_own = (in_second & ~in_front)[:, late_from:held]
    branch = from_others(partial_value)

    def with_late(branch):
        _, late = second_pass(last_codes, (in_second & in_front)[:, late_from:held], tiles2b)
        branch = branch + from_others(late) + own_cols(late)

        def one_more(number, branch):
            at = held + number * chunk
            here = jnp.take(sources, lax.dynamic_slice_in_dim(order, at, chunk), axis=0, mode="clip")
            part = [lax.dynamic_slice_in_dim(v, at, chunk, 1) for v in (codes, in_second)]
            _, extra = second_pass(*part, gathered(here))
            return branch + from_others(extra) + own_cols(extra)

        return lax.fori_loop(0, (misplaced[1] + chunk - 1) // chunk, one_more, branch)

    if not aligned:
        branch = lax.cond(some_late, with_late, lambda branch: branch, branch)
        more, _ = second_pass(last_codes, last_own, tiles2b)
        own = (total + more).transpose(1, 0, 2).reshape(token_rows, width)
        return (own_cols(tokens) + own_cols(own) + branch + fc2_bias).astype(jnp.bfloat16)

    share_blocks = share // side
    last_rows, last_cols = last_codes // second_blocks, last_codes % second_blocks % share_blocks
    last_plan = planned(last_rows, last_cols, last_own, share_blocks, first_blocks, 2, 4)
    last_plan, branch = lax.optimization_barrier((last_plan, branch))
    last_pass = functools.partial(
        tile_pass,
        result_kernel,
        last_rows,
        last_cols,
        last_own,
        ffn,
        hidden,
        tiles2b,
        more_specs=[
            pl.BlockSpec(
                (share_blocks, token_rows, side),
                lambda i, fields, counts, at: (at[0], 0, 0),
                pipeline_mode=pl.Buffered(1),
            ),
            pl.BlockSpec(
                (token_rows, share),
                lambda i, fields, counts, at: (0, at[0]),
                pipeline_mode=pl.Buffered(1),
            ),
            fixed((token_rows, share)),
            fixed((1, share)),
        ],
        out_shapes=[jax.ShapeDtypeStruct((token_rows, share), jnp.bfloat16)],
        blocks=share_blocks,
        steps=2,
        group=4,
        vmem=LAST_VMEM_BYTES,
        plan=last_plan,
    )

    def finished(branch):
        return last_pass(more=[total, tokens, branch, fc2_bias.reshape(1, share)])[0]

    return lax.cond(some_late, lambda branch: finished(with_late(branch)), finished, branch)


def solution(mesh):
    placed = (
        P("blk", None),
        P(),
        P(),
        P("blk", "ffn", None, None, None),
        P("blk", "ffn", None),
        P("blk", "ffn"),
        P("ffn"),
        P("blk", "ffn", None, None, None),
        P("blk", "ffn", None),
        P("blk", "ffn"),
        P("ffn"),
    )
    return jax.shard_map(
        functools.partial(on_device, ffn_size=mesh.shape["ffn"]),
        mesh=mesh,
        in_specs=placed,
        out_specs=P("blk", "ffn"),
        check_vma=False,
    )
```

```python
import functools

import jax
import jax.numpy as jnp
from jax import lax
from jax.experimental import pallas as pl
from jax.experimental.pallas import tpu as pltpu
from jax.sharding import PartitionSpec as P

UNROLL = 4
VMEM_BYTES = 56 * 1024 * 1024
LAST_VMEM_BYTES = 36 * 1024 * 1024


def group_kernel(group, size, zero_row, row_ref, col_ref, field_ref, count_ref, fill_ref, open_ref):
    step, steps = pl.program_id(0), pl.num_programs(0)
    listed = row_ref.shape[0] // steps

    def field(number, at):
        return (number * steps + step) * size + at

    def clear(at, carry):
        field_ref[field(0, at)] = 0
        for g in range(group):
            field_ref[field(1 + g, at)] = 0
            field_ref[field(1 + group + g, at)] = zero_row
        return carry

    def no_group(c, carry):
        fill_ref[c] = 0
        open_ref[c] = 0
        return carry

    def place(tile, groups):
        col = col_ref[step * listed + tile]
        held = jnp.maximum(col, 0)
        filled = fill_ref[held]
        opens = (col >= 0) & (filled == 0)
        at = jnp.where(opens, groups, open_ref[held])

        @pl.when(col >= 0)
        def _():
            open_ref[held] = at
            fill_ref[held] = jnp.where(filled == group - 1, 0, filled + 1)
            field_ref[field(0, at)] = col
            field_ref[field(1 + filled, at)] = tile
            field_ref[field(1 + group + filled, at)] = row_ref[step * listed + tile]

        return groups + opens.astype(jnp.int32)

    lax.fori_loop(0, size, clear, 0)
    lax.fori_loop(0, fill_ref.shape[0], no_group, 0)
    count_ref[step] = lax.fori_loop(0, listed, place, jnp.int32(0))


def group_up(rows, cols, live, blocks, zero_row, group):
    steps, listed = rows.shape
    most = (listed + (group - 1) * min(blocks, listed)) // group
    size = -(-most // UNROLL) * UNROLL
    smem = pl.BlockSpec(memory_space=pltpu.SMEM)
    return pl.pallas_call(
        functools.partial(group_kernel, group, size, zero_row),
        out_shape=[
            jax.ShapeDtypeStruct(((2 * group + 1) * steps * size,), jnp.int32),
            jax.ShapeDtypeStruct((steps,), jnp.int32),
        ],
        grid=(steps,),
        in_specs=[smem, smem],
        out_specs=[smem, smem],
        scratch_shapes=[pltpu.SMEM((blocks,), jnp.int32), pltpu.SMEM((blocks,), jnp.int32)],
        cost_estimate=pl.CostEstimate(flops=0, bytes_accessed=16 * steps * listed, transcendentals=0),
    )(rows.reshape(-1), jnp.where(live, cols, -1).reshape(-1))


def add_block(field_ref, count_ref, x_ref, w_ref, acc, group):
    step, steps = pl.program_id(0), pl.num_programs(0)
    w_ref = w_ref.reshape(-1, *w_ref.shape[2:])
    fields = 2 * group + 1
    size = field_ref.shape[0] // (fields * steps)

    def one(at):
        col, *parts = (field_ref[(f * steps + step) * size + at] for f in range(fields))
        left = jnp.concatenate([x_ref[row] for row in parts[group:]], axis=1)
        right = jnp.concatenate([w_ref[tile] for tile in parts[:group]], axis=0)
        acc[col] += jnp.dot(left, right, preferred_element_type=jnp.float32)

    def several(turn, carry):
        for u in range(UNROLL):
            one(turn * UNROLL + u)
        return carry

    lax.fori_loop(0, lax.div(count_ref[step] + UNROLL - 1, jnp.int32(UNROLL)), several, 0)


def for_blocks(count, work):
    def turn(c, carry):
        work(c)
        return carry

    lax.fori_loop(0, count, turn, 0)


def columns(c, width):
    return pl.ds(pl.multiple_of(c * width, width), width)


def at_start(work):
    pl.when(pl.program_id(0) == 0)(work)


def at_end(work):
    pl.when(pl.program_id(0) == pl.num_programs(0) - 1)(work)


def first_kernel(group, field_ref, count_ref, at_ref, x_ref, w_ref, bias_ref, sum_ref):
    @at_start
    def _():
        def fill(c):
            sum_ref[c] = jnp.broadcast_to(bias_ref[c], sum_ref.shape[1:])

        for_blocks(sum_ref.shape[0], fill)

    add_block(field_ref, count_ref, x_ref, w_ref, sum_ref, group)


def hidden_kernel(group, field_ref, count_ref, at_ref, x_ref, w_ref, sum_ref, out_ref, acc):
    blocks = acc.shape[0]

    @at_start
    def _():
        def fill(c):
            acc[c] = sum_ref[c]

        for_blocks(blocks, fill)

    add_block(field_ref, count_ref, x_ref, w_ref, acc, group)

    @at_end
    def _():
        def finish(c):
            out_ref[c] = jnp.maximum(acc[c], 0.0).astype(out_ref.dtype)

        for_blocks(blocks, finish)
        out_ref[blocks] = jnp.zeros(out_ref.shape[1:], out_ref.dtype)


def partial_kernel(group, field_ref, count_ref, at_ref, x_ref, w_ref, sum_ref, out_ref):
    blocks, width = sum_ref.shape[0], sum_ref.shape[2]

    @at_start
    def _():
        def fill(c):
            sum_ref[c] = jnp.zeros(sum_ref.shape[1:], sum_ref.dtype)

        for_blocks(blocks, fill)

    add_block(field_ref, count_ref, x_ref, w_ref, sum_ref, group)

    @at_end
    def _():
        def finish(c):
            out_ref[:, columns(c, width)] = sum_ref[c].astype(out_ref.dtype)

        for_blocks(blocks, finish)


def result_kernel(
    group, field_ref, count_ref, at_ref,
    x_ref, w_ref, sum_ref, token_ref, other_ref, bias_ref, out_ref, acc,
):
    blocks, width = acc.shape[0], acc.shape[2]

    @at_start
    def _():
        def fill(c):
            acc[c] = sum_ref[c]

        for_blocks(blocks, fill)

    add_block(field_ref, count_ref, x_ref, w_ref, acc, group)

    @at_end
    def _():
        def finish(c):
            cols = columns(c, width)
            value = token_ref[:, cols].astype(jnp.float32) + (acc[c] + other_ref[:, cols])
            out_ref[:, cols] = (value + bias_ref[:, cols]).astype(out_ref.dtype)

        for_blocks(blocks, finish)


def fixed(shape):
    return pl.BlockSpec(shape, lambda i, *_: (0,) * len(shape), pipeline_mode=pl.Buffered(1))


def planned(rows, cols, live, blocks, zero_row, steps, group):
    steps = steps if rows.shape[0] % steps == 0 else 1
    return group_up(*(v.reshape(steps, -1) for v in (rows, cols, live)), blocks, zero_row, group)


def tile_pass(
    kernel, rows, cols, live, at, x, tiles, more, more_specs, out_shapes, blocks,
    steps=4, group=2, scratch=True, vmem=VMEM_BYTES, plan=None,
):
    shards, slots = rows.shape
    side, tokens = tiles.shape[-1], x.shape[1]
    steps = steps if shards % steps == 0 else 1
    if plan is None:
        plan = planned(rows, cols, live, blocks, x.shape[0] - 1, steps, group)
    fields, counts = plan
    return pl.pallas_call(
        functools.partial(kernel, group),
        out_shape=out_shapes,
        grid_spec=pltpu.PrefetchScalarGridSpec(
            num_scalar_prefetch=3,
            grid=(steps,),
            in_specs=[
                fixed(x.shape),
                pl.BlockSpec((shards // steps, slots, side, side), lambda i, *_: (i, 0, 0, 0)),
                *more_specs,
            ],
            out_specs=[
                pl.BlockSpec(o.shape, lambda i, *_, rank=len(o.shape): (0,) * rank) for o in out_shapes
            ],
            scratch_shapes=[pltpu.VMEM((blocks, tokens, side), jnp.float32)] if scratch else [],
        ),
        compiler_params=pltpu.CompilerParams(vmem_limit_bytes=vmem),
        cost_estimate=pl.CostEstimate(
            flops=4 * shards * slots * tokens * side * side,
            bytes_accessed=shards * slots * side * side * 2,
            transcendentals=0,
        ),
    )(fields, counts, at.reshape(1), x, tiles, *more)


def swapped(values, stride):
    return values.reshape(-1, 2, stride, *values.shape[1:])[:, ::-1].reshape(values.shape)


def moved(values, by):
    ids = jnp.arange(values.shape[1], dtype=jnp.int32)
    hit = (ids[:, None] - by[:, None, None]) == ids
    return jnp.sum(jnp.where(hit, values[:, None, :], 0), axis=2)


def on_device(
    tokens,
    ln_gain,
    ln_bias,
    fc1_tiles,
    fc1_index,
    fc1_count,
    fc1_bias,
    fc2_tiles,
    fc2_index,
    fc2_count,
    fc2_bias,
    ffn_size,
):
    side = fc1_tiles.shape[-1]
    slots = fc1_tiles.shape[2]
    shards = lax.axis_size("blk")
    token_rows, width = tokens.shape
    first_blocks = fc1_bias.shape[0] // side
    second_blocks = width // side
    share = width // ffn_size
    blk, ffn = lax.axis_index("blk"), lax.axis_index("ffn")
    aligned = share % side == 0
    opening = slots * 4 // 5
    rest = slots - opening
    held = slots
    late_from = held - slots // 3
    levels = [
        (stride, max(slots // most, 1), max(slots // least, 1))
        for stride, most, least in ((1, 6, 8), (2, 12, 16), (4, 16, 24))
        if shards % (2 * stride) == 0
    ]
    slot_ids = jnp.arange(slots, dtype=jnp.int32)
    stream_ids = jnp.arange(rest + slots, dtype=jnp.int32)

    def gathered(value):
        return lax.all_gather(value, "blk", axis=0, tiled=True).reshape(shards, -1, side, side)

    tiles1 = gathered(fc1_tiles[0, 0, :opening])
    meta = jnp.concatenate([fc1_index[:, 0], fc2_index[:, 0], fc1_count, fc2_count], axis=1)
    meta = lax.all_gather(meta, "blk", axis=0, tiled=True)
    index1, index2 = meta[:, :slots], meta[:, slots : 2 * slots]
    count1, count2 = meta[:, 2 * slots], meta[:, 2 * slots + 1]
    left1 = jnp.maximum(count1 - opening, 0)

    def in_own_share(index):
        if not aligned:
            return jnp.zeros(index.shape, jnp.bool_)
        return index % second_blocks // (share // side) == ffn

    def streams(index, count, left, first_values, values):
        live = slot_ids < count[:, None]
        own = in_own_share(index)
        front, back = live & ~own, live & own
        front_place = left[:, None] + jnp.cumsum(front.astype(jnp.int32), axis=1) - 1
        back_place = jnp.cumsum(back.astype(jnp.int32), axis=1) - 1

        def placed(mask, place):
            hit = mask[:, None, :] & (place[:, None, :] == stream_ids[:, None])
            return jnp.sum(jnp.where(hit, values[:, None, :], 0), axis=2)

        first = jnp.where(stream_ids < left[:, None], jnp.pad(first_values, ((0, 0), (0, slots))), 0)
        return (
            first + placed(front, front_place),
            placed(back, back_place),
            left + jnp.sum(front.astype(jnp.int32), axis=1),
            jnp.sum(back.astype(jnp.int32), axis=1),
        )

    front, back, fronts, backs = streams(
        index2, count2, left1, jnp.zeros((shards, rest), jnp.int32), index2
    )
    own_left = jnp.maximum(fc1_count[:, 0] - opening, 0)
    own_front, own_back, _, _ = streams(
        fc2_index[:, 0], fc2_count[:, 0], own_left, jnp.arange(rest, dtype=jnp.int32)[None], rest + slot_ids[None]
    )
    own_front, own_back = own_front[0], own_back[0]
    sources = jnp.concatenate([fc1_tiles[0, 0, opening:], fc2_tiles[0, 0]], axis=0)

    def evened(values, numbers, fixed_numbers, stride, most):
        partners = swapped(numbers, stride)
        sent = jnp.clip((numbers - partners) // 2, 0, jnp.minimum(most, numbers - fixed_numbers))
        kept = numbers - sent
        got = swapped(sent, stride)
        arrived = moved(swapped(values, stride), kept - (partners - got))
        return jnp.where(stream_ids < kept[:, None], values, arrived), kept, kept + got

    def tail(stream, kept, most):
        return lax.dynamic_slice_in_dim(jnp.pad(stream, (0, most)), kept, most)

    for stride, most_front, most_back in levels:
        front, kept_front, fronts = evened(front, fronts, left1, stride, most_front)
        back, kept_back, backs = evened(back, backs, jnp.zeros_like(backs), stride, most_back)
        kept_front, kept_back = kept_front[blk], kept_back[blk]
        sending = jnp.concatenate(
            [tail(own_front, kept_front, most_front), tail(own_back, kept_back, most_back)]
        )
        arrived = lax.ppermute(
            jnp.take(sources, sending, axis=0, mode="clip"),
            "blk",
            [(i, i ^ stride) for i in range(shards)],
        )
        so_far = sources.shape[0]
        own_front = jnp.where(stream_ids < kept_front, own_front, so_far + stream_ids - kept_front)
        own_back = jnp.where(stream_ids < kept_back, own_back, so_far + most_front + stream_ids - kept_back)
        sources = jnp.concatenate([sources, arrived], axis=0)

    total_ids = jnp.arange(2 * stream_ids.shape[0] + slots // 4, dtype=jnp.int32)
    double = ((0, 0), (0, total_ids.shape[0] - stream_ids.shape[0]))
    lengths = fronts + backs
    codes = jnp.where(
        total_ids < fronts[:, None], jnp.pad(front, double), moved(jnp.pad(back, double), fronts)
    )
    own_fronts = fronts[blk]
    order = jnp.where(
        total_ids < own_fronts,
        jnp.pad(own_front, double[1]),
        moved(jnp.pad(own_back, double[1])[None], own_fronts[None])[0],
    )
    tiles2a = gathered(jnp.take(sources, order[:late_from], axis=0, mode="clip"))
    tiles2b = gathered(jnp.take(sources, order[late_from:held], axis=0, mode="clip"))
    misplaced = jnp.stack([jnp.max(fronts) - late_from, jnp.max(lengths) - held, jnp.max(lengths)])
    misplaced = lax.pmax(misplaced, "ffn")

    rows_f = tokens.astype(jnp.float32)
    center = jnp.mean(rows_f, axis=1, keepdims=True)
    spread = jnp.mean((rows_f - center) ** 2, axis=1, keepdims=True)
    normed = ((rows_f - center) / jnp.sqrt(spread + 1e-05) * ln_gain + ln_bias).astype(jnp.bfloat16)
    normed_blocks = normed.reshape(token_rows, second_blocks, side).transpose(1, 0, 2)
    normed_blocks = jnp.pad(normed_blocks, ((0, 1), (0, 0), (0, 0)))
    normed_blocks, misplaced = lax.optimization_barrier((normed_blocks, misplaced))
    some_late = jnp.max(misplaced[:2]) > 0

    (total,) = tile_pass(
        first_kernel,
        index1[:, :opening] // first_blocks,
        index1[:, :opening] % first_blocks,
        slot_ids[:opening] < count1[:, None],
        ffn,
        normed_blocks,
        tiles1,
        [fc1_bias.reshape(first_blocks, 1, side)],
        [fixed((first_blocks, 1, side))],
        [jax.ShapeDtypeStruct((first_blocks, token_rows, side), jnp.float32)],
        first_blocks,
        scratch=False,
    )
    (hidden,) = tile_pass(
        hidden_kernel,
        index1[:, opening:] // first_blocks,
        index1[:, opening:] % first_blocks,
        slot_ids[opening:] < count1[:, None],
        ffn,
        normed_blocks,
        tiles2a,
        [total],
        [fixed(total.shape)],
        [jax.ShapeDtypeStruct((first_blocks + 1, token_rows, side), jnp.bfloat16)],
        first_blocks,
    )

    def second_pass(places, live, tiles, steps=2, group=4):
        return tile_pass(
            partial_kernel,
            places // second_blocks,
            places % second_blocks,
            live,
            ffn,
            hidden,
            tiles,
            [],
            [],
            [
                jax.ShapeDtypeStruct((second_blocks, token_rows, side), jnp.float32),
                jax.ShapeDtypeStruct((token_rows, width), jnp.bfloat16),
            ],
            second_blocks,
            steps=steps,
            group=group,
            scratch=False,
        )

    def own_cols(value):
        return lax.dynamic_slice_in_dim(value, ffn * share, share, 1).astype(jnp.float32)

    def from_others(partial_value):
        branch = jnp.zeros((token_rows, share), jnp.float32)
        for shift in range(1, ffn_size):
            to = lax.rem(ffn + shift, ffn_size)
            arrived = lax.ppermute(
                lax.dynamic_slice_in_dim(partial_value, to * share, share, 1),
                "ffn",
                [(i, (i + shift) % ffn_size) for i in range(ffn_size)],
            )
            branch = branch + arrived.astype(jnp.float32)
        return branch

    in_front = total_ids < fronts[:, None]
    in_second = (total_ids >= left1[:, None]) & (total_ids < lengths[:, None])
    total, partial_value = second_pass(codes[:, :late_from], in_second[:, :late_from], tiles2a)
    last_codes = codes[:, late_from:held]
    last_own = (in_second & ~in_front)[:, late_from:held]
    branch = from_others(partial_value)

    def with_late(branch):
        chunk = slots // 4
        start = jnp.where(misplaced[0] > 0, late_from, held)
        late = in_second & (in_front | (total_ids >= held))

        def one_more(number, branch):
            at = start + number * chunk
            here = jnp.take(sources, lax.dynamic_slice_in_dim(order, at, chunk), axis=0, mode="clip")
            part = [lax.dynamic_slice_in_dim(v, at, chunk, 1) for v in (codes, late)]
            _, extra = second_pass(*part, gathered(here), steps=1, group=1)
            return branch + from_others(extra) + own_cols(extra)

        return lax.fori_loop(0, (misplaced[2] - start + chunk - 1) // chunk, one_more, branch)

    if not aligned:
        branch = lax.cond(some_late, with_late, lambda branch: branch, branch)
        more, _ = second_pass(last_codes, last_own, tiles2b)
        own = (total + more).transpose(1, 0, 2).reshape(token_rows, width)
        return (own_cols(tokens) + own_cols(own) + branch + fc2_bias).astype(jnp.bfloat16)

    share_blocks = share // side
    last_rows, last_cols = last_codes // second_blocks, last_codes % second_blocks % share_blocks
    last_plan = planned(last_rows, last_cols, last_own, share_blocks, first_blocks, 2, 4)
    bias_row = fc2_bias.reshape(1, share)
    last_plan, branch, bias_row = lax.optimization_barrier((last_plan, branch, bias_row))
    last_pass = functools.partial(
        tile_pass,
        result_kernel,
        last_rows,
        last_cols,
        last_own,
        ffn,
        hidden,
        tiles2b,
        more_specs=[
            pl.BlockSpec(
                (share_blocks, token_rows, side),
                lambda i, fields, counts, at: (at[0], 0, 0),
                pipeline_mode=pl.Buffered(1),
            ),
            pl.BlockSpec(
                (token_rows, share),
                lambda i, fields, counts, at: (0, at[0]),
                pipeline_mode=pl.Buffered(1),
            ),
            fixed((token_rows, share)),
            fixed((1, share)),
        ],
        out_shapes=[jax.ShapeDtypeStruct((token_rows, share), jnp.bfloat16)],
        blocks=share_blocks,
        steps=2,
        group=4,
        vmem=LAST_VMEM_BYTES,
        plan=last_plan,
    )

    def finished(branch):
        return last_pass(more=[total, tokens, branch, bias_row])[0]

    return lax.cond(some_late, lambda branch: finished(with_late(branch)), finished, branch)


def solution(mesh):
    placed = (
        P("blk", None),
        P(),
        P(),
        P("blk", "ffn", None, None, None),
        P("blk", "ffn", None),
        P("blk", "ffn"),
        P("ffn"),
        P("blk", "ffn", None, None, None),
        P("blk", "ffn", None),
        P("blk", "ffn"),
        P("ffn"),
    )
    return jax.shard_map(
        functools.partial(on_device, ffn_size=mesh.shape["ffn"]),
        mesh=mesh,
        in_specs=placed,
        out_specs=P("blk", "ffn"),
        check_vma=False,
    )
```

```python
import functools

import jax
import jax.numpy as jnp
from jax import lax
from jax.experimental import pallas as pl
from jax.experimental.pallas import tpu as pltpu
from jax.sharding import PartitionSpec as P

UNROLL = 4
VMEM_BYTES = 56 * 1024 * 1024
LAST_VMEM_BYTES = 36 * 1024 * 1024


def group_kernel(group, size, zero_row, row_ref, col_ref, field_ref, count_ref, fill_ref, open_ref):
    step, steps = pl.program_id(0), pl.num_programs(0)
    listed = row_ref.shape[0] // steps

    def field(number, at):
        return (number * steps + step) * size + at

    def clear(at, carry):
        field_ref[field(0, at)] = 0
        for g in range(group):
            field_ref[field(1 + g, at)] = 0
            field_ref[field(1 + group + g, at)] = zero_row
        return carry

    def no_group(c, carry):
        fill_ref[c] = 0
        open_ref[c] = 0
        return carry

    def place(tile, groups):
        col = col_ref[step * listed + tile]
        held = jnp.maximum(col, 0)
        filled = fill_ref[held]
        opens = (col >= 0) & (filled == 0)
        at = jnp.where(opens, groups, open_ref[held])

        @pl.when(col >= 0)
        def _():
            open_ref[held] = at
            fill_ref[held] = jnp.where(filled == group - 1, 0, filled + 1)
            field_ref[field(0, at)] = col
            field_ref[field(1 + filled, at)] = tile
            field_ref[field(1 + group + filled, at)] = row_ref[step * listed + tile]

        return groups + opens.astype(jnp.int32)

    lax.fori_loop(0, size, clear, 0)
    lax.fori_loop(0, fill_ref.shape[0], no_group, 0)
    count_ref[step] = lax.fori_loop(0, listed, place, jnp.int32(0))


def group_up(rows, cols, live, blocks, zero_row, group):
    steps, listed = rows.shape
    most = (listed + (group - 1) * min(blocks, listed)) // group
    size = -(-most // UNROLL) * UNROLL
    smem = pl.BlockSpec(memory_space=pltpu.SMEM)
    return pl.pallas_call(
        functools.partial(group_kernel, group, size, zero_row),
        out_shape=[
            jax.ShapeDtypeStruct(((2 * group + 1) * steps * size,), jnp.int32),
            jax.ShapeDtypeStruct((steps,), jnp.int32),
        ],
        grid=(steps,),
        in_specs=[smem, smem],
        out_specs=[smem, smem],
        scratch_shapes=[pltpu.SMEM((blocks,), jnp.int32), pltpu.SMEM((blocks,), jnp.int32)],
        cost_estimate=pl.CostEstimate(flops=0, bytes_accessed=16 * steps * listed, transcendentals=0),
    )(rows.reshape(-1), jnp.where(live, cols, -1).reshape(-1))


def add_block(field_ref, count_ref, x_ref, w_ref, acc, group):
    step, steps = pl.program_id(0), pl.num_programs(0)
    w_ref = w_ref.reshape(-1, *w_ref.shape[2:])
    fields = 2 * group + 1
    size = field_ref.shape[0] // (fields * steps)

    def one(at):
        col, *parts = (field_ref[(f * steps + step) * size + at] for f in range(fields))
        left = jnp.concatenate([x_ref[row] for row in parts[group:]], axis=1)
        right = jnp.concatenate([w_ref[tile] for tile in parts[:group]], axis=0)
        acc[col] += jnp.dot(left, right, preferred_element_type=jnp.float32)

    def several(turn, carry):
        for u in range(UNROLL):
            one(turn * UNROLL + u)
        return carry

    lax.fori_loop(0, lax.div(count_ref[step] + UNROLL - 1, jnp.int32(UNROLL)), several, 0)


def for_blocks(count, work):
    def turn(c, carry):
        work(c)
        return carry

    lax.fori_loop(0, count, turn, 0)


def columns(c, width):
    return pl.ds(pl.multiple_of(c * width, width), width)


def at_start(work):
    pl.when(pl.program_id(0) == 0)(work)


def at_end(work):
    pl.when(pl.program_id(0) == pl.num_programs(0) - 1)(work)


def first_kernel(group, field_ref, count_ref, at_ref, x_ref, w_ref, bias_ref, sum_ref):
    @at_start
    def _():
        def fill(c):
            sum_ref[c] = jnp.broadcast_to(bias_ref[c], sum_ref.shape[1:])

        for_blocks(sum_ref.shape[0], fill)

    add_block(field_ref, count_ref, x_ref, w_ref, sum_ref, group)


def hidden_kernel(group, field_ref, count_ref, at_ref, x_ref, w_ref, sum_ref, out_ref, acc):
    blocks = acc.shape[0]

    @at_start
    def _():
        def fill(c):
            acc[c] = sum_ref[c]

        for_blocks(blocks, fill)

    add_block(field_ref, count_ref, x_ref, w_ref, acc, group)

    @at_end
    def _():
        def finish(c):
            out_ref[c] = jnp.maximum(acc[c], 0.0).astype(out_ref.dtype)

        for_blocks(blocks, finish)
        out_ref[blocks] = jnp.zeros(out_ref.shape[1:], out_ref.dtype)


def partial_kernel(group, field_ref, count_ref, at_ref, x_ref, w_ref, sum_ref, out_ref):
    blocks, width = sum_ref.shape[0], sum_ref.shape[2]

    @at_start
    def _():
        def fill(c):
            sum_ref[c] = jnp.zeros(sum_ref.shape[1:], sum_ref.dtype)

        for_blocks(blocks, fill)

    add_block(field_ref, count_ref, x_ref, w_ref, sum_ref, group)

    @at_end
    def _():
        def finish(c):
            out_ref[:, columns(c, width)] = sum_ref[c].astype(out_ref.dtype)

        for_blocks(blocks, finish)


def result_kernel(
    group, field_ref, count_ref, at_ref,
    x_ref, w_ref, sum_ref, token_ref, other_ref, bias_ref, out_ref, acc,
):
    blocks, width = acc.shape[0], acc.shape[2]

    @at_start
    def _():
        def fill(c):
            acc[c] = sum_ref[c]

        for_blocks(blocks, fill)

    add_block(field_ref, count_ref, x_ref, w_ref, acc, group)

    @at_end
    def _():
        def finish(c):
            cols = columns(c, width)
            value = token_ref[:, cols].astype(jnp.float32) + (acc[c] + other_ref[:, cols])
            out_ref[:, cols] = (value + bias_ref[:, cols]).astype(out_ref.dtype)

        for_blocks(blocks, finish)


def fixed(shape):
    return pl.BlockSpec(shape, lambda i, *_: (0,) * len(shape), pipeline_mode=pl.Buffered(1))


def planned(rows, cols, live, blocks, zero_row, steps, group):
    steps = steps if rows.shape[0] % steps == 0 else 1
    return group_up(*(v.reshape(steps, -1) for v in (rows, cols, live)), blocks, zero_row, group)


def tile_pass(
    kernel, rows, cols, live, at, x, tiles, more, more_specs, out_shapes, blocks,
    steps=4, group=2, scratch=True, vmem=VMEM_BYTES, plan=None,
):
    shards, slots = rows.shape
    side, tokens = tiles.shape[-1], x.shape[1]
    steps = steps if shards % steps == 0 else 1
    if plan is None:
        plan = planned(rows, cols, live, blocks, x.shape[0] - 1, steps, group)
    fields, counts = plan
    return pl.pallas_call(
        functools.partial(kernel, group),
        out_shape=out_shapes,
        grid_spec=pltpu.PrefetchScalarGridSpec(
            num_scalar_prefetch=3,
            grid=(steps,),
            in_specs=[
                fixed(x.shape),
                pl.BlockSpec((shards // steps, slots, side, side), lambda i, *_: (i, 0, 0, 0)),
                *more_specs,
            ],
            out_specs=[
                pl.BlockSpec(o.shape, lambda i, *_, rank=len(o.shape): (0,) * rank) for o in out_shapes
            ],
            scratch_shapes=[pltpu.VMEM((blocks, tokens, side), jnp.float32)] if scratch else [],
        ),
        compiler_params=pltpu.CompilerParams(vmem_limit_bytes=vmem),
        cost_estimate=pl.CostEstimate(
            flops=4 * shards * slots * tokens * side * side,
            bytes_accessed=shards * slots * side * side * 2,
            transcendentals=0,
        ),
    )(fields, counts, at.reshape(1), x, tiles, *more)


def swapped(values, stride):
    return values.reshape(-1, 2, stride, *values.shape[1:])[:, ::-1].reshape(values.shape)


def moved(values, by):
    ids = jnp.arange(values.shape[1], dtype=jnp.int32)
    hit = (ids[:, None] - by[:, None, None]) == ids
    return jnp.sum(jnp.where(hit, values[:, None, :], 0), axis=2)


def on_device(
    tokens,
    ln_gain,
    ln_bias,
    fc1_tiles,
    fc1_index,
    fc1_count,
    fc1_bias,
    fc2_tiles,
    fc2_index,
    fc2_count,
    fc2_bias,
    ffn_size,
):
    side = fc1_tiles.shape[-1]
    slots = fc1_tiles.shape[2]
    shards = lax.axis_size("blk")
    token_rows, width = tokens.shape
    first_blocks = fc1_bias.shape[0] // side
    second_blocks = width // side
    share = width // ffn_size
    blk, ffn = lax.axis_index("blk"), lax.axis_index("ffn")
    aligned = share % side == 0
    opening = slots * 5 // 7
    rest = slots - opening
    held = slots + slots // 100
    late_from = held - slots // 3
    levels = [
        (stride, slots // most, max(slots // least, 1))
        for stride, most, least in ((1, 6, 8), (2, 16, 16), (4, 32, 16), (8, slots + 1, 16))
        if shards % (2 * stride) == 0
    ]
    slot_ids = jnp.arange(slots, dtype=jnp.int32)
    stream_ids = jnp.arange(rest + slots, dtype=jnp.int32)

    def gathered(value):
        return lax.all_gather(value, "blk", axis=0, tiled=True).reshape(shards, -1, side, side)

    tiles1 = gathered(fc1_tiles[0, 0, :opening])
    meta = jnp.concatenate([fc1_index[:, 0], fc2_index[:, 0], fc1_count, fc2_count], axis=1)
    meta = lax.all_gather(meta, "blk", axis=0, tiled=True)
    index1, index2 = meta[:, :slots], meta[:, slots : 2 * slots]
    count1, count2 = meta[:, 2 * slots], meta[:, 2 * slots + 1]
    left1 = jnp.maximum(count1 - opening, 0)

    def in_own_share(index):
        if not aligned:
            return jnp.zeros(index.shape, jnp.bool_)
        return index % second_blocks // (share // side) == ffn

    def streams(index, count, left, first_values, values):
        live = slot_ids < count[:, None]
        own = in_own_share(index)
        front, back = live & ~own, live & own
        front_place = left[:, None] + jnp.cumsum(front.astype(jnp.int32), axis=1) - 1
        back_place = jnp.cumsum(back.astype(jnp.int32), axis=1) - 1

        def placed(mask, place):
            hit = mask[:, None, :] & (place[:, None, :] == stream_ids[:, None])
            return jnp.sum(jnp.where(hit, values[:, None, :], 0), axis=2)

        first = jnp.where(stream_ids < left[:, None], jnp.pad(first_values, ((0, 0), (0, slots))), 0)
        return (
            first + placed(front, front_place),
            placed(back, back_place),
            left + jnp.sum(front.astype(jnp.int32), axis=1),
            jnp.sum(back.astype(jnp.int32), axis=1),
        )

    front, back, fronts, backs = streams(
        index2, count2, left1, jnp.zeros((shards, rest), jnp.int32), index2
    )
    own_left = jnp.maximum(fc1_count[:, 0] - opening, 0)
    own_front, own_back, _, _ = streams(
        fc2_index[:, 0], fc2_count[:, 0], own_left, jnp.arange(rest, dtype=jnp.int32)[None], rest + slot_ids[None]
    )
    own_front, own_back = own_front[0], own_back[0]
    sources = jnp.concatenate([fc1_tiles[0, 0, opening:], fc2_tiles[0, 0]], axis=0)

    def evened(values, numbers, fixed_numbers, weights, stride, most):
        partners = swapped(numbers, stride)
        excess = (weights - swapped(weights, stride)) // 2
        room = jnp.minimum(most, stream_ids.shape[0] - partners)
        sent = jnp.clip(excess, 0, jnp.minimum(room, numbers - fixed_numbers))
        kept = numbers - sent
        got = swapped(sent, stride)
        arrived = moved(swapped(values, stride), kept - (partners - got))
        return jnp.where(stream_ids < kept[:, None], values, arrived), kept, kept + got

    def tail(stream, kept, most):
        return lax.dynamic_slice_in_dim(jnp.pad(stream, (0, most)), kept, most)

    for stride, most_front, most_back in levels:
        front, kept_front, fronts = evened(front, fronts, left1, fronts, stride, most_front)
        back, kept_back, backs = evened(
            back, backs, jnp.zeros_like(backs), fronts + backs, stride, most_back
        )
        kept_front, kept_back = kept_front[blk], kept_back[blk]
        sending = jnp.concatenate(
            [tail(own_front, kept_front, most_front), tail(own_back, kept_back, most_back)]
        )
        arrived = lax.ppermute(
            jnp.take(sources, sending, axis=0, mode="clip"),
            "blk",
            [(i, i ^ stride) for i in range(shards)],
        )
        so_far = sources.shape[0]
        own_front = jnp.where(stream_ids < kept_front, own_front, so_far + stream_ids - kept_front)
        own_back = jnp.where(stream_ids < kept_back, own_back, so_far + most_front + stream_ids - kept_back)
        sources = jnp.concatenate([sources, arrived], axis=0)

    total_ids = jnp.arange(2 * stream_ids.shape[0] + slots // 4, dtype=jnp.int32)
    double = ((0, 0), (0, total_ids.shape[0] - stream_ids.shape[0]))
    lengths = fronts + backs
    codes = jnp.where(
        total_ids < fronts[:, None], jnp.pad(front, double), moved(jnp.pad(back, double), fronts)
    )
    own_fronts = fronts[blk]
    order = jnp.where(
        total_ids < own_fronts,
        jnp.pad(own_front, double[1]),
        moved(jnp.pad(own_back, double[1])[None], own_fronts[None])[0],
    )
    tiles2a = gathered(jnp.take(sources, order[:late_from], axis=0, mode="clip"))
    tiles2b = gathered(jnp.take(sources, order[late_from:held], axis=0, mode="clip"))
    misplaced = jnp.stack([jnp.max(fronts) - late_from, jnp.max(lengths) - held, jnp.max(lengths)])
    misplaced = lax.pmax(misplaced, "ffn")

    rows_f = tokens.astype(jnp.float32)
    center = jnp.mean(rows_f, axis=1, keepdims=True)
    spread = jnp.mean((rows_f - center) ** 2, axis=1, keepdims=True)
    normed = ((rows_f - center) / jnp.sqrt(spread + 1e-05) * ln_gain + ln_bias).astype(jnp.bfloat16)
    normed_blocks = normed.reshape(token_rows, second_blocks, side).transpose(1, 0, 2)
    normed_blocks = jnp.pad(normed_blocks, ((0, 1), (0, 0), (0, 0)))
    normed_blocks, misplaced = lax.optimization_barrier((normed_blocks, misplaced))
    some_late = jnp.max(misplaced[:2]) > 0

    (total,) = tile_pass(
        first_kernel,
        index1[:, :opening] // first_blocks,
        index1[:, :opening] % first_blocks,
        slot_ids[:opening] < count1[:, None],
        ffn,
        normed_blocks,
        tiles1,
        [fc1_bias.reshape(first_blocks, 1, side)],
        [fixed((first_blocks, 1, side))],
        [jax.ShapeDtypeStruct((first_blocks, token_rows, side), jnp.float32)],
        first_blocks,
        scratch=False,
    )
    (hidden,) = tile_pass(
        hidden_kernel,
        index1[:, opening:] // first_blocks,
        index1[:, opening:] % first_blocks,
        slot_ids[opening:] < count1[:, None],
        ffn,
        normed_blocks,
        tiles2a,
        [total],
        [fixed(total.shape)],
        [jax.ShapeDtypeStruct((first_blocks + 1, token_rows, side), jnp.bfloat16)],
        first_blocks,
    )

    def second_pass(places, live, tiles, steps=2, group=4):
        return tile_pass(
            partial_kernel,
            places // second_blocks,
            places % second_blocks,
            live,
            ffn,
            hidden,
            tiles,
            [],
            [],
            [
                jax.ShapeDtypeStruct((second_blocks, token_rows, side), jnp.float32),
                jax.ShapeDtypeStruct((token_rows, width), jnp.bfloat16),
            ],
            second_blocks,
            steps=steps,
            group=group,
            scratch=False,
        )

    def own_cols(value):
        return lax.dynamic_slice_in_dim(value, ffn * share, share, 1).astype(jnp.float32)

    def from_others(partial_value):
        branch = jnp.zeros((token_rows, share), jnp.float32)
        for shift in range(1, ffn_size):
            to = lax.rem(ffn + shift, ffn_size)
            arrived = lax.ppermute(
                lax.dynamic_slice_in_dim(partial_value, to * share, share, 1),
                "ffn",
                [(i, (i + shift) % ffn_size) for i in range(ffn_size)],
            )
            branch = branch + arrived.astype(jnp.float32)
        return branch

    in_front = total_ids < fronts[:, None]
    in_second = (total_ids >= left1[:, None]) & (total_ids < lengths[:, None])
    total, partial_value = second_pass(codes[:, :late_from], in_second[:, :late_from], tiles2a)
    last_codes = codes[:, late_from:held]
    last_own = (in_second & ~in_front)[:, late_from:held]
    branch = from_others(partial_value)

    def with_late(branch):
        chunk = slots // 4
        start = jnp.where(misplaced[0] > 0, late_from, held)
        late = in_second & (in_front | (total_ids >= held))

        def one_more(number, branch):
            at = start + number * chunk
            here = jnp.take(sources, lax.dynamic_slice_in_dim(order, at, chunk), axis=0, mode="clip")
            part = [lax.dynamic_slice_in_dim(v, at, chunk, 1) for v in (codes, late)]
            _, extra = second_pass(*part, gathered(here), steps=1, group=1)
            return branch + from_others(extra) + own_cols(extra)

        return lax.fori_loop(0, (misplaced[2] - start + chunk - 1) // chunk, one_more, branch)

    if not aligned:
        branch = lax.cond(some_late, with_late, lambda branch: branch, branch)
        more, _ = second_pass(last_codes, last_own, tiles2b)
        own = (total + more).transpose(1, 0, 2).reshape(token_rows, width)
        return (own_cols(tokens) + own_cols(own) + branch + fc2_bias).astype(jnp.bfloat16)

    share_blocks = share // side
    last_rows, last_cols = last_codes // second_blocks, last_codes % second_blocks % share_blocks
    last_plan = planned(last_rows, last_cols, last_own, share_blocks, first_blocks, 2, 4)
    bias_row = fc2_bias.reshape(1, share)
    last_plan, branch, bias_row = lax.optimization_barrier((last_plan, branch, bias_row))
    last_pass = functools.partial(
        tile_pass,
        result_kernel,
        last_rows,
        last_cols,
        last_own,
        ffn,
        hidden,
        tiles2b,
        more_specs=[
            pl.BlockSpec(
                (share_blocks, token_rows, side),
                lambda i, fields, counts, at: (at[0], 0, 0),
                pipeline_mode=pl.Buffered(1),
            ),
            pl.BlockSpec(
                (token_rows, share),
                lambda i, fields, counts, at: (0, at[0]),
                pipeline_mode=pl.Buffered(1),
            ),
            fixed((token_rows, share)),
            fixed((1, share)),
        ],
        out_shapes=[jax.ShapeDtypeStruct((token_rows, share), jnp.bfloat16)],
        blocks=share_blocks,
        steps=2,
        group=4,
        vmem=LAST_VMEM_BYTES,
        plan=last_plan,
    )

    def finished(branch):
        return last_pass(more=[total, tokens, branch, bias_row])[0]

    return lax.cond(some_late, lambda branch: finished(with_late(branch)), finished, branch)


def solution(mesh):
    placed = (
        P("blk", None),
        P(),
        P(),
        P("blk", "ffn", None, None, None),
        P("blk", "ffn", None),
        P("blk", "ffn"),
        P("ffn"),
        P("blk", "ffn", None, None, None),
        P("blk", "ffn", None),
        P("blk", "ffn"),
        P("ffn"),
    )
    return jax.shard_map(
        functools.partial(on_device, ffn_size=mesh.shape["ffn"]),
        mesh=mesh,
        in_specs=placed,
        out_specs=P("blk", "ffn"),
        check_vma=False,
    )
```

```python
import functools

import jax
import jax.numpy as jnp
from jax import lax
from jax.experimental import pallas as pl
from jax.experimental.pallas import tpu as pltpu
from jax.sharding import PartitionSpec as P

UNROLL = 4
VMEM_BYTES = 56 * 1024 * 1024
LAST_VMEM_BYTES = 36 * 1024 * 1024


def group_kernel(group, size, zero_row, row_ref, col_ref, field_ref, count_ref, fill_ref, open_ref):
    step, steps = pl.program_id(0), pl.num_programs(0)
    listed = row_ref.shape[0] // steps

    def field(number, at):
        return (number * steps + step) * size + at

    def clear(at, carry):
        field_ref[field(0, at)] = 0
        for g in range(group):
            field_ref[field(1 + g, at)] = 0
            field_ref[field(1 + group + g, at)] = zero_row
        return carry

    def no_group(c, carry):
        fill_ref[c] = 0
        open_ref[c] = 0
        return carry

    def place(tile, groups):
        col = col_ref[step * listed + tile]
        held = jnp.maximum(col, 0)
        filled = fill_ref[held]
        opens = (col >= 0) & (filled == 0)
        at = jnp.where(opens, groups, open_ref[held])

        @pl.when(col >= 0)
        def _():
            open_ref[held] = at
            fill_ref[held] = jnp.where(filled == group - 1, 0, filled + 1)
            field_ref[field(0, at)] = col
            field_ref[field(1 + filled, at)] = tile
            field_ref[field(1 + group + filled, at)] = row_ref[step * listed + tile]

        return groups + opens.astype(jnp.int32)

    lax.fori_loop(0, size, clear, 0)
    lax.fori_loop(0, fill_ref.shape[0], no_group, 0)
    count_ref[step] = lax.fori_loop(0, listed, place, jnp.int32(0))


def group_up(rows, cols, live, blocks, zero_row, group):
    steps, listed = rows.shape
    most = (listed + (group - 1) * min(blocks, listed)) // group
    size = -(-most // UNROLL) * UNROLL
    smem = pl.BlockSpec(memory_space=pltpu.SMEM)
    return pl.pallas_call(
        functools.partial(group_kernel, group, size, zero_row),
        out_shape=[
            jax.ShapeDtypeStruct(((2 * group + 1) * steps * size,), jnp.int32),
            jax.ShapeDtypeStruct((steps,), jnp.int32),
        ],
        grid=(steps,),
        in_specs=[smem, smem],
        out_specs=[smem, smem],
        scratch_shapes=[pltpu.SMEM((blocks,), jnp.int32), pltpu.SMEM((blocks,), jnp.int32)],
        cost_estimate=pl.CostEstimate(flops=0, bytes_accessed=16 * steps * listed, transcendentals=0),
    )(rows.reshape(-1), jnp.where(live, cols, -1).reshape(-1))


def add_block(field_ref, count_ref, x_ref, w_ref, acc, group):
    step, steps = pl.program_id(0), pl.num_programs(0)
    w_ref = w_ref.reshape(-1, *w_ref.shape[2:])
    fields = 2 * group + 1
    size = field_ref.shape[0] // (fields * steps)

    def one(at):
        col, *parts = (field_ref[(f * steps + step) * size + at] for f in range(fields))
        left = jnp.concatenate([x_ref[row] for row in parts[group:]], axis=1)
        right = jnp.concatenate([w_ref[tile] for tile in parts[:group]], axis=0)
        acc[col] += jnp.dot(left, right, preferred_element_type=jnp.float32)

    def several(turn, carry):
        for u in range(UNROLL):
            one(turn * UNROLL + u)
        return carry

    lax.fori_loop(0, lax.div(count_ref[step] + UNROLL - 1, jnp.int32(UNROLL)), several, 0)


def for_blocks(count, work):
    def turn(c, carry):
        work(c)
        return carry

    lax.fori_loop(0, count, turn, 0)


def columns(c, width):
    return pl.ds(pl.multiple_of(c * width, width), width)


def at_start(work):
    pl.when(pl.program_id(0) == 0)(work)


def at_end(work):
    pl.when(pl.program_id(0) == pl.num_programs(0) - 1)(work)


def first_kernel(group, field_ref, count_ref, at_ref, x_ref, w_ref, bias_ref, sum_ref):
    @at_start
    def _():
        def fill(c):
            sum_ref[c] = jnp.broadcast_to(bias_ref[c], sum_ref.shape[1:])

        for_blocks(sum_ref.shape[0], fill)

    add_block(field_ref, count_ref, x_ref, w_ref, sum_ref, group)


def hidden_kernel(group, field_ref, count_ref, at_ref, x_ref, w_ref, sum_ref, out_ref, acc):
    blocks = acc.shape[0]

    @at_start
    def _():
        def fill(c):
            acc[c] = sum_ref[c]

        for_blocks(blocks, fill)

    add_block(field_ref, count_ref, x_ref, w_ref, acc, group)

    @at_end
    def _():
        def finish(c):
            out_ref[c] = jnp.maximum(acc[c], 0.0).astype(out_ref.dtype)

        for_blocks(blocks, finish)
        out_ref[blocks] = jnp.zeros(out_ref.shape[1:], out_ref.dtype)


def partial_kernel(group, field_ref, count_ref, at_ref, x_ref, w_ref, sum_ref, out_ref):
    blocks, width = sum_ref.shape[0], sum_ref.shape[2]

    @at_start
    def _():
        def fill(c):
            sum_ref[c] = jnp.zeros(sum_ref.shape[1:], sum_ref.dtype)

        for_blocks(blocks, fill)

    add_block(field_ref, count_ref, x_ref, w_ref, sum_ref, group)

    @at_end
    def _():
        def finish(c):
            out_ref[:, columns(c, width)] = sum_ref[c].astype(out_ref.dtype)

        for_blocks(blocks, finish)


def result_kernel(
    group, field_ref, count_ref, at_ref,
    x_ref, w_ref, sum_ref, token_ref, other_ref, bias_ref, out_ref, acc,
):
    blocks, width = acc.shape[0], acc.shape[2]

    @at_start
    def _():
        def fill(c):
            acc[c] = sum_ref[c]

        for_blocks(blocks, fill)

    add_block(field_ref, count_ref, x_ref, w_ref, acc, group)

    @at_end
    def _():
        def finish(c):
            cols = columns(c, width)
            value = token_ref[:, cols].astype(jnp.float32) + (acc[c] + other_ref[:, cols])
            out_ref[:, cols] = (value + bias_ref[:, cols]).astype(out_ref.dtype)

        for_blocks(blocks, finish)


def fixed(shape):
    return pl.BlockSpec(shape, lambda i, *_: (0,) * len(shape), pipeline_mode=pl.Buffered(1))


def planned(rows, cols, live, blocks, zero_row, steps, group):
    steps = steps if rows.shape[0] % steps == 0 else 1
    return group_up(*(v.reshape(steps, -1) for v in (rows, cols, live)), blocks, zero_row, group)


def tile_pass(
    kernel, rows, cols, live, at, x, tiles, more, more_specs, out_shapes, blocks,
    steps=4, group=2, scratch=True, vmem=VMEM_BYTES, plan=None,
):
    shards, slots = rows.shape
    side, tokens = tiles.shape[-1], x.shape[1]
    steps = steps if shards % steps == 0 else 1
    if plan is None:
        plan = planned(rows, cols, live, blocks, x.shape[0] - 1, steps, group)
    fields, counts = plan
    return pl.pallas_call(
        functools.partial(kernel, group),
        out_shape=out_shapes,
        grid_spec=pltpu.PrefetchScalarGridSpec(
            num_scalar_prefetch=3,
            grid=(steps,),
            in_specs=[
                fixed(x.shape),
                pl.BlockSpec((shards // steps, slots, side, side), lambda i, *_: (i, 0, 0, 0)),
                *more_specs,
            ],
            out_specs=[
                pl.BlockSpec(o.shape, lambda i, *_, rank=len(o.shape): (0,) * rank) for o in out_shapes
            ],
            scratch_shapes=[pltpu.VMEM((blocks, tokens, side), jnp.float32)] if scratch else [],
        ),
        compiler_params=pltpu.CompilerParams(vmem_limit_bytes=vmem),
        cost_estimate=pl.CostEstimate(
            flops=4 * shards * slots * tokens * side * side,
            bytes_accessed=shards * slots * side * side * 2,
            transcendentals=0,
        ),
    )(fields, counts, at.reshape(1), x, tiles, *more)


def layout_kernel(
    levels, capacity, index_ref, own_ref, count_ref, left_ref, at_ref,
    code_ref, front_count_ref, length_ref, order_ref, send_ref,
    place_ref, source_ref, fronts, backs, sent_ref,
):
    shards = count_ref.shape[0]
    slots = index_ref.shape[0] // shards
    total = order_ref.shape[0]
    me = at_ref[0]

    def times(count, work):
        def turn(i, carry):
            work(i)
            return carry

        lax.fori_loop(0, count, turn, 0)

    def spot(back, shard, i):
        return (back * shards + shard) * capacity + i

    def build(shard):
        left = left_ref[shard]

        def first(i):
            place_ref[spot(0, shard, i)] = 0
            source_ref[spot(0, shard, i)] = i

        def second(slot, carry):
            front, back = carry
            own = own_ref[shard * slots + slot]
            at = spot(own, shard, jnp.where(own == 1, back, front))
            place_ref[at] = index_ref[shard * slots + slot]
            source_ref[at] = capacity - slots + slot
            return front + 1 - own, back + own

        times(left, first)
        fronts[shard], backs[shard] = lax.fori_loop(0, count_ref[shard], second, (left, jnp.int32(0)))

    def even(back, stride, most, so_far, send_at):
        numbers = backs if back else fronts

        def weight(shard):
            return fronts[shard] + backs[shard] if back else fronts[shard]

        def decide(shard):
            partner = shard ^ stride
            excess = lax.div(jnp.maximum(weight(shard) - weight(partner), 0), jnp.int32(2))
            spare = numbers[shard] if back else numbers[shard] - left_ref[shard]
            room = jnp.minimum(most, capacity - numbers[partner])
            sent_ref[shard] = jnp.minimum(excess, jnp.minimum(room, spare))

        def hand_over(shard):
            partner, sent = shard ^ stride, sent_ref[shard]
            here, there = numbers[shard] - sent, numbers[partner]

            def one(i):
                old, new = spot(back, shard, here + i), spot(back, partner, there + i)
                place_ref[new] = place_ref[old]

                @pl.when(shard == me)
                def _():
                    send_ref[send_at + i] = source_ref[old]

                source_ref[new] = so_far + i

            times(sent, one)

        def settle(shard):
            numbers[shard] = numbers[shard] - sent_ref[shard] + sent_ref[shard ^ stride]

        for work in (decide, hand_over, settle):
            times(shards, work)

    def lay_out(shard):
        front, back = fronts[shard], backs[shard]
        front_count_ref[shard] = front
        length_ref[shard] = front + back

        def copy(back, start):
            def one(i):
                code_ref[shard * total + start + i] = place_ref[spot(back, shard, i)]

                @pl.when(shard == me)
                def _():
                    order_ref[start + i] = source_ref[spot(back, shard, i)]

            return one

        times(front, copy(0, 0))
        times(back, copy(1, front))

    def clear(ref):
        def one(i):
            ref[i] = 0

        times(ref.shape[0], one)

    clear(order_ref)
    clear(send_ref)
    times(shards, build)
    so_far, send_at = capacity, 0
    for stride, most_front, most_back in levels:
        for back, most in ((0, most_front), (1, most_back)):
            if most:
                even(back, stride, most, so_far, send_at)
            so_far, send_at = so_far + most, send_at + most
    times(shards, lay_out)


def laid_out(levels, capacity, total, index, own, count, left, blk):
    shards, slots = index.shape
    smem = pl.BlockSpec(memory_space=pltpu.SMEM)
    sizes = [shards * total, shards, shards, total, sum(front + back for _, front, back in levels)]
    scratch = [2 * shards * capacity, 2 * shards * capacity, shards, shards, shards]
    return pl.pallas_call(
        functools.partial(layout_kernel, levels, capacity),
        out_shape=[jax.ShapeDtypeStruct((size,), jnp.int32) for size in sizes],
        in_specs=[smem] * 5,
        out_specs=[smem] * 5,
        scratch_shapes=[pltpu.SMEM((size,), jnp.int32) for size in scratch],
        cost_estimate=pl.CostEstimate(flops=0, bytes_accessed=16 * shards * slots, transcendentals=0),
    )(index.reshape(-1), own.reshape(-1), count, left, blk.reshape(1))


def on_device(
    tokens,
    ln_gain,
    ln_bias,
    fc1_tiles,
    fc1_index,
    fc1_count,
    fc1_bias,
    fc2_tiles,
    fc2_index,
    fc2_count,
    fc2_bias,
    ffn_size,
):
    side = fc1_tiles.shape[-1]
    slots = fc1_tiles.shape[2]
    shards = lax.axis_size("blk")
    token_rows, width = tokens.shape
    first_blocks = fc1_bias.shape[0] // side
    second_blocks = width // side
    share = width // ffn_size
    blk, ffn = lax.axis_index("blk"), lax.axis_index("ffn")
    aligned = share % side == 0
    opening = slots * 5 // 7
    rest = slots - opening
    held = slots + slots // 100
    late_from = held - slots // 3
    levels = [
        (stride, slots // most, max(slots // least, 1))
        for stride, most, least in ((1, 6, 8), (2, 16, 16), (4, 32, 16), (8, slots + 1, 16))
        if shards % (2 * stride) == 0
    ]
    slot_ids = jnp.arange(slots, dtype=jnp.int32)

    def gathered(value):
        return lax.all_gather(value, "blk", axis=0, tiled=True).reshape(shards, -1, side, side)

    tiles1 = gathered(fc1_tiles[0, 0, :opening])
    meta = jnp.concatenate([fc1_index[:, 0], fc2_index[:, 0], fc1_count, fc2_count], axis=1)
    meta = lax.all_gather(meta, "blk", axis=0, tiled=True)
    index1, index2 = meta[:, :slots], meta[:, slots : 2 * slots]
    count1, count2 = meta[:, 2 * slots], meta[:, 2 * slots + 1]
    left1 = jnp.maximum(count1 - opening, 0)

    def in_own_share(index):
        if not aligned:
            return jnp.zeros(index.shape, jnp.bool_)
        return index % second_blocks // (share // side) == ffn

    capacity = rest + slots
    total_ids = jnp.arange(2 * capacity + slots // 4, dtype=jnp.int32)
    codes, fronts, lengths, order, sends = laid_out(
        levels, capacity, total_ids.shape[0], index2, in_own_share(index2).astype(jnp.int32), count2, left1, blk
    )
    codes = codes.reshape(shards, -1)
    sources = jnp.concatenate([fc1_tiles[0, 0, opening:], fc2_tiles[0, 0]], axis=0)
    for stride, most_front, most_back in levels:
        sending, sends = sends[: most_front + most_back], sends[most_front + most_back :]
        arrived = lax.ppermute(
            jnp.take(sources, sending, axis=0, mode="clip"),
            "blk",
            [(i, i ^ stride) for i in range(shards)],
        )
        sources = jnp.concatenate([sources, arrived], axis=0)

    tiles2a = gathered(jnp.take(sources, order[:late_from], axis=0, mode="clip"))
    tiles2b = gathered(jnp.take(sources, order[late_from:held], axis=0, mode="clip"))
    misplaced = jnp.stack([jnp.max(fronts) - late_from, jnp.max(lengths) - held, jnp.max(lengths)])
    misplaced = lax.pmax(misplaced, "ffn")

    rows_f = tokens.astype(jnp.float32)
    center = jnp.mean(rows_f, axis=1, keepdims=True)
    spread = jnp.mean((rows_f - center) ** 2, axis=1, keepdims=True)
    normed = ((rows_f - center) / jnp.sqrt(spread + 1e-05) * ln_gain + ln_bias).astype(jnp.bfloat16)
    normed_blocks = normed.reshape(token_rows, second_blocks, side).transpose(1, 0, 2)
    normed_blocks = jnp.pad(normed_blocks, ((0, 1), (0, 0), (0, 0)))
    normed_blocks, misplaced = lax.optimization_barrier((normed_blocks, misplaced))
    some_late = jnp.max(misplaced[:2]) > 0

    (total,) = tile_pass(
        first_kernel,
        index1[:, :opening] // first_blocks,
        index1[:, :opening] % first_blocks,
        slot_ids[:opening] < count1[:, None],
        ffn,
        normed_blocks,
        tiles1,
        [fc1_bias.reshape(first_blocks, 1, side)],
        [fixed((first_blocks, 1, side))],
        [jax.ShapeDtypeStruct((first_blocks, token_rows, side), jnp.float32)],
        first_blocks,
        scratch=False,
    )
    (hidden,) = tile_pass(
        hidden_kernel,
        index1[:, opening:] // first_blocks,
        index1[:, opening:] % first_blocks,
        slot_ids[opening:] < count1[:, None],
        ffn,
        normed_blocks,
        tiles2a,
        [total],
        [fixed(total.shape)],
        [jax.ShapeDtypeStruct((first_blocks + 1, token_rows, side), jnp.bfloat16)],
        first_blocks,
    )

    def second_pass(places, live, tiles, steps=2, group=4):
        return tile_pass(
            partial_kernel,
            places // second_blocks,
            places % second_blocks,
            live,
            ffn,
            hidden,
            tiles,
            [],
            [],
            [
                jax.ShapeDtypeStruct((second_blocks, token_rows, side), jnp.float32),
                jax.ShapeDtypeStruct((token_rows, width), jnp.bfloat16),
            ],
            second_blocks,
            steps=steps,
            group=group,
            scratch=False,
        )

    def own_cols(value):
        return lax.dynamic_slice_in_dim(value, ffn * share, share, 1).astype(jnp.float32)

    def from_others(partial_value):
        branch = jnp.zeros((token_rows, share), jnp.float32)
        for shift in range(1, ffn_size):
            to = lax.rem(ffn + shift, ffn_size)
            arrived = lax.ppermute(
                lax.dynamic_slice_in_dim(partial_value, to * share, share, 1),
                "ffn",
                [(i, (i + shift) % ffn_size) for i in range(ffn_size)],
            )
            branch = branch + arrived.astype(jnp.float32)
        return branch

    in_front = total_ids < fronts[:, None]
    in_second = (total_ids >= left1[:, None]) & (total_ids < lengths[:, None])
    total, partial_value = second_pass(codes[:, :late_from], in_second[:, :late_from], tiles2a)
    last_codes = codes[:, late_from:held]
    last_own = (in_second & ~in_front)[:, late_from:held]
    branch = from_others(partial_value)

    def with_late(branch):
        chunk = slots // 4
        start = jnp.where(misplaced[0] > 0, late_from, held)
        late = in_second & (in_front | (total_ids >= held))

        def one_more(number, branch):
            at = start + number * chunk
            here = jnp.take(sources, lax.dynamic_slice_in_dim(order, at, chunk), axis=0, mode="clip")
            part = [lax.dynamic_slice_in_dim(v, at, chunk, 1) for v in (codes, late)]
            _, extra = second_pass(*part, gathered(here), steps=1, group=1)
            return branch + from_others(extra) + own_cols(extra)

        return lax.fori_loop(0, (misplaced[2] - start + chunk - 1) // chunk, one_more, branch)

    if not aligned:
        branch = lax.cond(some_late, with_late, lambda branch: branch, branch)
        more, _ = second_pass(last_codes, last_own, tiles2b)
        own = (total + more).transpose(1, 0, 2).reshape(token_rows, width)
        return (own_cols(tokens) + own_cols(own) + branch + fc2_bias).astype(jnp.bfloat16)

    share_blocks = share // side
    last_rows, last_cols = last_codes // second_blocks, last_codes % second_blocks % share_blocks
    last_plan = planned(last_rows, last_cols, last_own, share_blocks, first_blocks, 2, 4)
    bias_row = fc2_bias.reshape(1, share)
    last_plan, branch, bias_row = lax.optimization_barrier((last_plan, branch, bias_row))
    last_pass = functools.partial(
        tile_pass,
        result_kernel,
        last_rows,
        last_cols,
        last_own,
        ffn,
        hidden,
        tiles2b,
        more_specs=[
            pl.BlockSpec(
                (share_blocks, token_rows, side),
                lambda i, fields, counts, at: (at[0], 0, 0),
                pipeline_mode=pl.Buffered(1),
            ),
            pl.BlockSpec(
                (token_rows, share),
                lambda i, fields, counts, at: (0, at[0]),
                pipeline_mode=pl.Buffered(1),
            ),
            fixed((token_rows, share)),
            fixed((1, share)),
        ],
        out_shapes=[jax.ShapeDtypeStruct((token_rows, share), jnp.bfloat16)],
        blocks=share_blocks,
        steps=2,
        group=4,
        vmem=LAST_VMEM_BYTES,
        plan=last_plan,
    )

    def finished(branch):
        return last_pass(more=[total, tokens, branch, bias_row])[0]

    return lax.cond(some_late, lambda branch: finished(with_late(branch)), finished, branch)


def solution(mesh):
    placed = (
        P("blk", None),
        P(),
        P(),
        P("blk", "ffn", None, None, None),
        P("blk", "ffn", None),
        P("blk", "ffn"),
        P("ffn"),
        P("blk", "ffn", None, None, None),
        P("blk", "ffn", None),
        P("blk", "ffn"),
        P("ffn"),
    )
    return jax.shard_map(
        functools.partial(on_device, ffn_size=mesh.shape["ffn"]),
        mesh=mesh,
        in_specs=placed,
        out_specs=P("blk", "ffn"),
        check_vma=False,
    )
```

```python
import functools

import jax
import jax.numpy as jnp
from jax import lax
from jax.experimental import pallas as pl
from jax.experimental.pallas import tpu as pltpu
from jax.sharding import PartitionSpec as P

UNROLL = 8
VMEM_BYTES = 56 * 1024 * 1024
LAST_VMEM_BYTES = 26 * 1024 * 1024


def group_kernel(group, size, zero_row, row_ref, col_ref, field_ref, count_ref, fill_ref, open_ref):
    step, steps = pl.program_id(0), pl.num_programs(0)
    listed = row_ref.shape[0] // steps

    def field(number, at):
        return (number * steps + step) * size + at

    def clear(at, carry):
        field_ref[field(0, at)] = 0
        for g in range(group):
            field_ref[field(1 + g, at)] = 0
            field_ref[field(1 + group + g, at)] = zero_row
        return carry

    def no_group(c, carry):
        fill_ref[c] = 0
        open_ref[c] = 0
        return carry

    def place(tile, groups):
        col = col_ref[step * listed + tile]
        held = jnp.maximum(col, 0)
        filled = fill_ref[held]
        opens = (col >= 0) & (filled == 0)
        at = jnp.where(opens, groups, open_ref[held])

        @pl.when(col >= 0)
        def _():
            open_ref[held] = at
            fill_ref[held] = jnp.where(filled == group - 1, 0, filled + 1)
            field_ref[field(0, at)] = col
            field_ref[field(1 + filled, at)] = tile
            field_ref[field(1 + group + filled, at)] = row_ref[step * listed + tile]

        return groups + opens.astype(jnp.int32)

    lax.fori_loop(0, size, clear, 0)
    lax.fori_loop(0, fill_ref.shape[0], no_group, 0)
    count_ref[step] = lax.fori_loop(0, listed, place, jnp.int32(0))


def group_up(rows, cols, live, blocks, zero_row, group):
    steps, listed = rows.shape
    most = (listed + (group - 1) * min(blocks, listed)) // group
    size = -(-most // UNROLL) * UNROLL
    smem = pl.BlockSpec(memory_space=pltpu.SMEM)
    return pl.pallas_call(
        functools.partial(group_kernel, group, size, zero_row),
        out_shape=[
            jax.ShapeDtypeStruct(((2 * group + 1) * steps * size,), jnp.int32),
            jax.ShapeDtypeStruct((steps,), jnp.int32),
        ],
        grid=(steps,),
        in_specs=[smem, smem],
        out_specs=[smem, smem],
        scratch_shapes=[pltpu.SMEM((blocks,), jnp.int32), pltpu.SMEM((blocks,), jnp.int32)],
        cost_estimate=pl.CostEstimate(flops=0, bytes_accessed=16 * steps * listed, transcendentals=0),
    )(rows.reshape(-1), jnp.where(live, cols, -1).reshape(-1))


def add_block(field_ref, count_ref, x_ref, w_ref, acc, group):
    step, steps = pl.program_id(0), pl.num_programs(0)
    w_ref = w_ref.reshape(-1, *w_ref.shape[2:])
    fields = 2 * group + 1
    size = field_ref.shape[0] // (fields * steps)

    def one(at):
        col, *parts = (field_ref[(f * steps + step) * size + at] for f in range(fields))
        left = jnp.concatenate([x_ref[row] for row in parts[group:]], axis=1)
        right = jnp.concatenate([w_ref[tile] for tile in parts[:group]], axis=0)
        acc[col] += jnp.dot(left, right, preferred_element_type=jnp.float32)

    def several(turn, carry):
        for u in range(UNROLL):
            one(turn * UNROLL + u)
        return carry

    lax.fori_loop(0, lax.div(count_ref[step] + UNROLL - 1, jnp.int32(UNROLL)), several, 0)


def for_blocks(count, work):
    def turn(c, carry):
        work(c)
        return carry

    lax.fori_loop(0, count, turn, 0)


def columns(c, width):
    return pl.ds(pl.multiple_of(c * width, width), width)


def at_start(work):
    pl.when(pl.program_id(0) == 0)(work)


def at_end(work):
    pl.when(pl.program_id(0) == pl.num_programs(0) - 1)(work)


def first_kernel(group, field_ref, count_ref, at_ref, x_ref, w_ref, bias_ref, sum_ref):
    @at_start
    def _():
        def fill(c):
            sum_ref[c] = jnp.broadcast_to(bias_ref[c], sum_ref.shape[1:])

        for_blocks(sum_ref.shape[0], fill)

    add_block(field_ref, count_ref, x_ref, w_ref, sum_ref, group)


def hidden_kernel(group, field_ref, count_ref, at_ref, x_ref, w_ref, sum_ref, out_ref, acc):
    blocks = acc.shape[0]

    @at_start
    def _():
        def fill(c):
            acc[c] = sum_ref[c]

        for_blocks(blocks, fill)

    add_block(field_ref, count_ref, x_ref, w_ref, acc, group)

    @at_end
    def _():
        def finish(c):
            out_ref[c] = jnp.maximum(acc[c], 0.0).astype(out_ref.dtype)

        for_blocks(blocks, finish)
        out_ref[blocks] = jnp.zeros(out_ref.shape[1:], out_ref.dtype)


def partial_kernel(group, field_ref, count_ref, at_ref, x_ref, w_ref, sum_ref, out_ref):
    blocks, width = sum_ref.shape[0], sum_ref.shape[2]

    @at_start
    def _():
        def fill(c):
            sum_ref[c] = jnp.zeros(sum_ref.shape[1:], sum_ref.dtype)

        for_blocks(blocks, fill)

    add_block(field_ref, count_ref, x_ref, w_ref, sum_ref, group)

    @at_end
    def _():
        def finish(c):
            out_ref[:, columns(c, width)] = sum_ref[c].astype(out_ref.dtype)

        for_blocks(blocks, finish)


def result_kernel(
    group, field_ref, count_ref, at_ref,
    x_ref, w_ref, sum_ref, token_ref, other_ref, bias_ref, out_ref, acc,
):
    blocks, width = acc.shape[0], acc.shape[2]

    @at_start
    def _():
        def fill(c):
            acc[c] = sum_ref[c]

        for_blocks(blocks, fill)

    add_block(field_ref, count_ref, x_ref, w_ref, acc, group)

    @at_end
    def _():
        def finish(c):
            cols = columns(c, width)
            value = token_ref[:, cols].astype(jnp.float32) + (acc[c] + other_ref[:, cols])
            out_ref[:, cols] = (value + bias_ref[:, cols]).astype(out_ref.dtype)

        for_blocks(blocks, finish)


def fixed(shape):
    return pl.BlockSpec(shape, lambda i, *_: (0,) * len(shape), pipeline_mode=pl.Buffered(1))


def planned(rows, cols, live, blocks, zero_row, steps, group):
    steps = steps if rows.shape[0] % steps == 0 else 1
    return group_up(*(v.reshape(steps, -1) for v in (rows, cols, live)), blocks, zero_row, group)


def tile_pass(
    kernel, rows, cols, live, at, x, tiles, more, more_specs, out_shapes, blocks,
    steps=4, group=2, scratch=True, vmem=VMEM_BYTES, plan=None,
):
    shards, slots = rows.shape
    side, tokens = tiles.shape[-1], x.shape[1]
    steps = steps if shards % steps == 0 else 1
    if plan is None:
        plan = planned(rows, cols, live, blocks, x.shape[0] - 1, steps, group)
    fields, counts = plan
    return pl.pallas_call(
        functools.partial(kernel, group),
        out_shape=out_shapes,
        grid_spec=pltpu.PrefetchScalarGridSpec(
            num_scalar_prefetch=3,
            grid=(steps,),
            in_specs=[
                fixed(x.shape),
                pl.BlockSpec((shards // steps, slots, side, side), lambda i, *_: (i, 0, 0, 0)),
                *more_specs,
            ],
            out_specs=[
                pl.BlockSpec(o.shape, lambda i, *_, rank=len(o.shape): (0,) * rank) for o in out_shapes
            ],
            scratch_shapes=[pltpu.VMEM((blocks, tokens, side), jnp.float32)] if scratch else [],
        ),
        compiler_params=pltpu.CompilerParams(vmem_limit_bytes=vmem),
        cost_estimate=pl.CostEstimate(
            flops=4 * shards * slots * tokens * side * side,
            bytes_accessed=shards * slots * side * side * 2,
            transcendentals=0,
        ),
    )(fields, counts, at.reshape(1), x, tiles, *more)


def layout_kernel(
    levels, capacity, index_ref, own_ref, count_ref, left_ref, at_ref,
    code_ref, front_count_ref, length_ref, order_ref, send_ref,
    place_ref, source_ref, fronts, backs, sent_ref,
):
    shards = count_ref.shape[0]
    slots = index_ref.shape[0] // shards
    total = order_ref.shape[0]
    me = at_ref[0]

    def times(count, work):
        def turn(i, carry):
            work(i)
            return carry

        lax.fori_loop(0, count, turn, 0)

    def spot(back, shard, i):
        return (back * shards + shard) * capacity + i

    def build(shard):
        left = left_ref[shard]

        def first(i):
            place_ref[spot(0, shard, i)] = 0
            source_ref[spot(0, shard, i)] = i

        def second(slot, carry):
            front, back = carry
            own = own_ref[shard * slots + slot]
            at = spot(own, shard, jnp.where(own == 1, back, front))
            place_ref[at] = index_ref[shard * slots + slot]
            source_ref[at] = capacity - slots + slot
            return front + 1 - own, back + own

        times(left, first)
        fronts[shard], backs[shard] = lax.fori_loop(0, count_ref[shard], second, (left, jnp.int32(0)))

    def even(back, stride, most, so_far, send_at):
        numbers = backs if back else fronts

        def weight(shard):
            return fronts[shard] + backs[shard] if back else fronts[shard]

        def decide(shard):
            partner = shard ^ stride
            excess = lax.div(jnp.maximum(weight(shard) - weight(partner), 0), jnp.int32(2))
            spare = numbers[shard] if back else numbers[shard] - left_ref[shard]
            room = jnp.minimum(most, capacity - numbers[partner])
            sent_ref[shard] = jnp.minimum(excess, jnp.minimum(room, spare))

        def hand_over(shard):
            partner, sent = shard ^ stride, sent_ref[shard]
            here, there = numbers[shard] - sent, numbers[partner]

            def one(i):
                old, new = spot(back, shard, here + i), spot(back, partner, there + i)
                place_ref[new] = place_ref[old]

                @pl.when(shard == me)
                def _():
                    send_ref[send_at + i] = source_ref[old]

                source_ref[new] = so_far + i

            times(sent, one)

        def settle(shard):
            numbers[shard] = numbers[shard] - sent_ref[shard] + sent_ref[shard ^ stride]

        for work in (decide, hand_over, settle):
            times(shards, work)

    def lay_out(shard):
        front, back = fronts[shard], backs[shard]
        front_count_ref[shard] = front
        length_ref[shard] = front + back

        def copy(back, start):
            def one(i):
                code_ref[shard * total + start + i] = place_ref[spot(back, shard, i)]

                @pl.when(shard == me)
                def _():
                    order_ref[start + i] = source_ref[spot(back, shard, i)]

            return one

        times(front, copy(0, 0))
        times(back, copy(1, front))

    def clear(ref):
        def one(i):
            ref[i] = 0

        times(ref.shape[0], one)

    clear(order_ref)
    clear(send_ref)
    times(shards, build)
    so_far, send_at = capacity, 0
    for stride, most_front, most_back in levels:
        for back, most in ((0, most_front), (1, most_back)):
            if most:
                even(back, stride, most, so_far, send_at)
            so_far, send_at = so_far + most, send_at + most
    times(shards, lay_out)


def laid_out(levels, capacity, total, index, own, count, left, blk):
    shards, slots = index.shape
    smem = pl.BlockSpec(memory_space=pltpu.SMEM)
    sizes = [shards * total, shards, shards, total, sum(front + back for _, front, back in levels)]
    scratch = [2 * shards * capacity, 2 * shards * capacity, shards, shards, shards]
    return pl.pallas_call(
        functools.partial(layout_kernel, levels, capacity),
        out_shape=[jax.ShapeDtypeStruct((size,), jnp.int32) for size in sizes],
        in_specs=[smem] * 5,
        out_specs=[smem] * 5,
        scratch_shapes=[pltpu.SMEM((size,), jnp.int32) for size in scratch],
        cost_estimate=pl.CostEstimate(flops=0, bytes_accessed=16 * shards * slots, transcendentals=0),
    )(index.reshape(-1), own.reshape(-1), count, left, blk.reshape(1))


def on_device(
    tokens,
    ln_gain,
    ln_bias,
    fc1_tiles,
    fc1_index,
    fc1_count,
    fc1_bias,
    fc2_tiles,
    fc2_index,
    fc2_count,
    fc2_bias,
    ffn_size,
):
    side = fc1_tiles.shape[-1]
    slots = fc1_tiles.shape[2]
    shards = lax.axis_size("blk")
    token_rows, width = tokens.shape
    first_blocks = fc1_bias.shape[0] // side
    second_blocks = width // side
    share = width // ffn_size
    blk, ffn = lax.axis_index("blk"), lax.axis_index("ffn")
    aligned = share % side == 0
    opening = slots * 5 // 7
    rest = slots - opening
    held = slots + slots // 100
    late_from = held - slots // 3
    levels = [
        (stride, slots // most, max(slots // least, 1))
        for stride, most, least in ((1, 6, 8), (2, 16, 16), (4, 32, 16), (8, slots + 1, 16))
        if shards % (2 * stride) == 0
    ]
    slot_ids = jnp.arange(slots, dtype=jnp.int32)

    def gathered(value):
        return lax.all_gather(value, "blk", axis=0, tiled=True).reshape(shards, -1, side, side)

    tiles1 = gathered(fc1_tiles[0, 0, :opening])
    meta = jnp.concatenate([fc1_index[:, 0], fc2_index[:, 0], fc1_count, fc2_count], axis=1)
    meta = lax.all_gather(meta, "blk", axis=0, tiled=True)
    index1, index2 = meta[:, :slots], meta[:, slots : 2 * slots]
    count1, count2 = meta[:, 2 * slots], meta[:, 2 * slots + 1]
    left1 = jnp.maximum(count1 - opening, 0)

    def in_own_share(index):
        if not aligned:
            return jnp.zeros(index.shape, jnp.bool_)
        return index % second_blocks // (share // side) == ffn

    capacity = rest + slots
    total_ids = jnp.arange(2 * capacity + slots // 4, dtype=jnp.int32)
    codes, fronts, lengths, order, sends = laid_out(
        levels, capacity, total_ids.shape[0], index2, in_own_share(index2).astype(jnp.int32), count2, left1, blk
    )
    codes = codes.reshape(shards, -1)
    sources = jnp.concatenate([fc1_tiles[0, 0, opening:], fc2_tiles[0, 0]], axis=0)
    for stride, most_front, most_back in levels:
        sending, sends = sends[: most_front + most_back], sends[most_front + most_back :]
        arrived = lax.ppermute(
            jnp.take(sources, sending, axis=0, mode="clip"),
            "blk",
            [(i, i ^ stride) for i in range(shards)],
        )
        sources = jnp.concatenate([sources, arrived], axis=0)

    tiles2a = gathered(jnp.take(sources, order[:late_from], axis=0, mode="clip"))
    tiles2b = gathered(jnp.take(sources, order[late_from:held], axis=0, mode="clip"))
    misplaced = jnp.stack([jnp.max(fronts) - late_from, jnp.max(lengths) - held, jnp.max(lengths)])
    misplaced = lax.pmax(misplaced, "ffn")

    rows_f = tokens.astype(jnp.float32)
    center = jnp.mean(rows_f, axis=1, keepdims=True)
    spread = jnp.mean((rows_f - center) ** 2, axis=1, keepdims=True)
    normed = ((rows_f - center) / jnp.sqrt(spread + 1e-05) * ln_gain + ln_bias).astype(jnp.bfloat16)
    normed_blocks = normed.reshape(token_rows, second_blocks, side).transpose(1, 0, 2)
    normed_blocks = jnp.pad(normed_blocks, ((0, 1), (0, 0), (0, 0)))
    normed_blocks, misplaced = lax.optimization_barrier((normed_blocks, misplaced))
    some_late = jnp.max(misplaced[:2]) > 0

    (total,) = tile_pass(
        first_kernel,
        index1[:, :opening] // first_blocks,
        index1[:, :opening] % first_blocks,
        slot_ids[:opening] < count1[:, None],
        ffn,
        normed_blocks,
        tiles1,
        [fc1_bias.reshape(first_blocks, 1, side)],
        [fixed((first_blocks, 1, side))],
        [jax.ShapeDtypeStruct((first_blocks, token_rows, side), jnp.float32)],
        first_blocks,
        scratch=False,
    )
    (hidden,) = tile_pass(
        hidden_kernel,
        index1[:, opening:] // first_blocks,
        index1[:, opening:] % first_blocks,
        slot_ids[opening:] < count1[:, None],
        ffn,
        normed_blocks,
        tiles2a,
        [total],
        [fixed(total.shape)],
        [jax.ShapeDtypeStruct((first_blocks + 1, token_rows, side), jnp.bfloat16)],
        first_blocks,
    )

    def second_pass(places, live, tiles, steps=2, group=4):
        return tile_pass(
            partial_kernel,
            places // second_blocks,
            places % second_blocks,
            live,
            ffn,
            hidden,
            tiles,
            [],
            [],
            [
                jax.ShapeDtypeStruct((second_blocks, token_rows, side), jnp.float32),
                jax.ShapeDtypeStruct((token_rows, width), jnp.bfloat16),
            ],
            second_blocks,
            steps=steps,
            group=group,
            scratch=False,
        )

    def own_cols(value):
        return lax.dynamic_slice_in_dim(value, ffn * share, share, 1).astype(jnp.float32)

    def from_others(partial_value):
        branch = jnp.zeros((token_rows, share), jnp.float32)
        for shift in range(1, ffn_size):
            to = lax.rem(ffn + shift, ffn_size)
            arrived = lax.ppermute(
                lax.dynamic_slice_in_dim(partial_value, to * share, share, 1),
                "ffn",
                [(i, (i + shift) % ffn_size) for i in range(ffn_size)],
            )
            branch = branch + arrived.astype(jnp.float32)
        return branch

    in_front = total_ids < fronts[:, None]
    in_second = (total_ids >= left1[:, None]) & (total_ids < lengths[:, None])
    total, partial_value = second_pass(codes[:, :late_from], in_second[:, :late_from], tiles2a)
    last_codes = codes[:, late_from:held]
    last_own = (in_second & ~in_front)[:, late_from:held]
    branch = from_others(partial_value)

    def with_late(branch):
        chunk = slots // 4
        start = jnp.where(misplaced[0] > 0, late_from, held)
        late = in_second & (in_front | (total_ids >= held))

        def one_more(number, branch):
            at = start + number * chunk
            here = jnp.take(sources, lax.dynamic_slice_in_dim(order, at, chunk), axis=0, mode="clip")
            part = [lax.dynamic_slice_in_dim(v, at, chunk, 1) for v in (codes, late)]
            _, extra = second_pass(*part, gathered(here), steps=1, group=1)
            return branch + from_others(extra) + own_cols(extra)

        return lax.fori_loop(0, (misplaced[2] - start + chunk - 1) // chunk, one_more, branch)

    if not aligned:
        branch = lax.cond(some_late, with_late, lambda branch: branch, branch)
        more, _ = second_pass(last_codes, last_own, tiles2b)
        own = (total + more).transpose(1, 0, 2).reshape(token_rows, width)
        return (own_cols(tokens) + own_cols(own) + branch + fc2_bias).astype(jnp.bfloat16)

    share_blocks = share // side
    last_rows, last_cols = last_codes // second_blocks, last_codes % second_blocks % share_blocks
    last_plan = planned(last_rows, last_cols, last_own, share_blocks, first_blocks, 4, 4)
    bias_row = fc2_bias.reshape(1, share)
    last_plan, branch, bias_row = lax.optimization_barrier((last_plan, branch, bias_row))
    last_pass = functools.partial(
        tile_pass,
        result_kernel,
        last_rows,
        last_cols,
        last_own,
        ffn,
        hidden,
        tiles2b,
        more_specs=[
            pl.BlockSpec(
                (share_blocks, token_rows, side),
                lambda i, fields, counts, at: (at[0], 0, 0),
                pipeline_mode=pl.Buffered(1),
            ),
            pl.BlockSpec(
                (token_rows, share),
                lambda i, fields, counts, at: (0, at[0]),
                pipeline_mode=pl.Buffered(1),
            ),
            fixed((token_rows, share)),
            fixed((1, share)),
        ],
        out_shapes=[jax.ShapeDtypeStruct((token_rows, share), jnp.bfloat16)],
        blocks=share_blocks,
        steps=4,
        group=4,
        vmem=LAST_VMEM_BYTES,
        plan=last_plan,
    )

    def finished(branch):
        return last_pass(more=[total, tokens, branch, bias_row])[0]

    return lax.cond(some_late, lambda branch: finished(with_late(branch)), finished, branch)


def solution(mesh):
    placed = (
        P("blk", None),
        P(),
        P(),
        P("blk", "ffn", None, None, None),
        P("blk", "ffn", None),
        P("blk", "ffn"),
        P("ffn"),
        P("blk", "ffn", None, None, None),
        P("blk", "ffn", None),
        P("blk", "ffn"),
        P("ffn"),
    )
    return jax.shard_map(
        functools.partial(on_device, ffn_size=mesh.shape["ffn"]),
        mesh=mesh,
        in_specs=placed,
        out_specs=P("blk", "ffn"),
        check_vma=False,
    )
```

```python
import functools

import jax
import jax.numpy as jnp
from jax import lax
from jax.experimental import pallas as pl
from jax.experimental.pallas import tpu as pltpu
from jax.sharding import PartitionSpec as P

UNROLL = 8
VMEM_BYTES = 56 * 1024 * 1024
LAST_VMEM_BYTES = 26 * 1024 * 1024


def group_kernel(group, size, zero_row, row_ref, col_ref, field_ref, count_ref, fill_ref, open_ref):
    step, steps = pl.program_id(0), pl.num_programs(0)
    listed = row_ref.shape[0] // steps

    def field(number, at):
        return (number * steps + step) * size + at

    def clear(at, carry):
        field_ref[field(0, at)] = 0
        for g in range(group):
            field_ref[field(1 + g, at)] = 0
            field_ref[field(1 + group + g, at)] = zero_row
        return carry

    def no_group(c, carry):
        fill_ref[c] = 0
        open_ref[c] = 0
        return carry

    def place(tile, groups):
        col = col_ref[step * listed + tile]
        held = jnp.maximum(col, 0)
        filled = fill_ref[held]
        opens = (col >= 0) & (filled == 0)
        at = jnp.where(opens, groups, open_ref[held])

        @pl.when(col >= 0)
        def _():
            open_ref[held] = at
            fill_ref[held] = jnp.where(filled == group - 1, 0, filled + 1)
            field_ref[field(0, at)] = col
            field_ref[field(1 + filled, at)] = tile
            field_ref[field(1 + group + filled, at)] = row_ref[step * listed + tile]

        return groups + opens.astype(jnp.int32)

    lax.fori_loop(0, size, clear, 0)
    lax.fori_loop(0, fill_ref.shape[0], no_group, 0)
    count_ref[step] = lax.fori_loop(0, listed, place, jnp.int32(0))


def group_up(rows, cols, live, blocks, zero_row, group):
    steps, listed = rows.shape
    most = (listed + (group - 1) * min(blocks, listed)) // group
    size = -(-most // UNROLL) * UNROLL
    smem = pl.BlockSpec(memory_space=pltpu.SMEM)
    return pl.pallas_call(
        functools.partial(group_kernel, group, size, zero_row),
        out_shape=[
            jax.ShapeDtypeStruct(((2 * group + 1) * steps * size,), jnp.int32),
            jax.ShapeDtypeStruct((steps,), jnp.int32),
        ],
        grid=(steps,),
        in_specs=[smem, smem],
        out_specs=[smem, smem],
        scratch_shapes=[pltpu.SMEM((blocks,), jnp.int32), pltpu.SMEM((blocks,), jnp.int32)],
        cost_estimate=pl.CostEstimate(flops=0, bytes_accessed=16 * steps * listed, transcendentals=0),
    )(rows.reshape(-1), jnp.where(live, cols, -1).reshape(-1))


def add_block(field_ref, count_ref, x_ref, w_ref, acc, group):
    step, steps = pl.program_id(0), pl.num_programs(0)
    w_ref = w_ref.reshape(-1, *w_ref.shape[2:])
    fields = 2 * group + 1
    size = field_ref.shape[0] // (fields * steps)

    def one(at):
        col, *parts = (field_ref[(f * steps + step) * size + at] for f in range(fields))
        left = jnp.concatenate([x_ref[row] for row in parts[group:]], axis=1)
        right = jnp.concatenate([w_ref[tile] for tile in parts[:group]], axis=0)
        acc[col] += jnp.dot(left, right, preferred_element_type=jnp.float32)

    def several(turn, carry):
        for u in range(UNROLL):
            one(turn * UNROLL + u)
        return carry

    lax.fori_loop(0, lax.div(count_ref[step] + UNROLL - 1, jnp.int32(UNROLL)), several, 0)


def for_blocks(count, work):
    def turn(c, carry):
        work(c)
        return carry

    lax.fori_loop(0, count, turn, 0)


def columns(c, width):
    return pl.ds(pl.multiple_of(c * width, width), width)


def at_start(work):
    pl.when(pl.program_id(0) == 0)(work)


def at_end(work):
    pl.when(pl.program_id(0) == pl.num_programs(0) - 1)(work)


def first_kernel(group, field_ref, count_ref, at_ref, x_ref, w_ref, bias_ref, sum_ref):
    @at_start
    def _():
        def fill(c):
            sum_ref[c] = jnp.broadcast_to(bias_ref[c], sum_ref.shape[1:])

        for_blocks(sum_ref.shape[0], fill)

    add_block(field_ref, count_ref, x_ref, w_ref, sum_ref, group)


def hidden_kernel(group, field_ref, count_ref, at_ref, x_ref, w_ref, sum_ref, out_ref, acc):
    blocks = acc.shape[0]

    @at_start
    def _():
        def fill(c):
            acc[c] = sum_ref[c]

        for_blocks(blocks, fill)

    add_block(field_ref, count_ref, x_ref, w_ref, acc, group)

    @at_end
    def _():
        def finish(c):
            out_ref[c] = jnp.maximum(acc[c], 0.0).astype(out_ref.dtype)

        for_blocks(blocks, finish)
        out_ref[blocks] = jnp.zeros(out_ref.shape[1:], out_ref.dtype)


def partial_kernel(group, field_ref, count_ref, at_ref, x_ref, w_ref, sum_ref, out_ref):
    blocks, width = sum_ref.shape[0], sum_ref.shape[2]

    @at_start
    def _():
        def fill(c):
            sum_ref[c] = jnp.zeros(sum_ref.shape[1:], sum_ref.dtype)

        for_blocks(blocks, fill)

    add_block(field_ref, count_ref, x_ref, w_ref, sum_ref, group)

    @at_end
    def _():
        def finish(c):
            out_ref[:, columns(c, width)] = sum_ref[c].astype(out_ref.dtype)

        for_blocks(blocks, finish)


def result_kernel(
    group, field_ref, count_ref, at_ref,
    x_ref, w_ref, sum_ref, token_ref, other_ref, bias_ref, out_ref, acc,
):
    blocks, width = acc.shape[0], acc.shape[2]

    @at_start
    def _():
        def fill(c):
            acc[c] = sum_ref[c]

        for_blocks(blocks, fill)

    add_block(field_ref, count_ref, x_ref, w_ref, acc, group)

    @at_end
    def _():
        def finish(c):
            cols = columns(c, width)
            value = token_ref[:, cols].astype(jnp.float32) + (acc[c] + other_ref[:, cols])
            out_ref[:, cols] = (value + bias_ref[:, cols]).astype(out_ref.dtype)

        for_blocks(blocks, finish)


def fixed(shape):
    return pl.BlockSpec(shape, lambda i, *_: (0,) * len(shape), pipeline_mode=pl.Buffered(1))


def planned(rows, cols, live, blocks, zero_row, steps, group):
    steps = steps if rows.shape[0] % steps == 0 else 1
    return group_up(*(v.reshape(steps, -1) for v in (rows, cols, live)), blocks, zero_row, group)


def tile_pass(
    kernel, rows, cols, live, at, x, tiles, more, more_specs, out_shapes, blocks,
    steps=4, group=2, scratch=True, vmem=VMEM_BYTES, plan=None,
):
    shards, slots = rows.shape
    side, tokens = tiles.shape[-1], x.shape[1]
    steps = steps if shards % steps == 0 else 1
    if plan is None:
        plan = planned(rows, cols, live, blocks, x.shape[0] - 1, steps, group)
    fields, counts = plan
    return pl.pallas_call(
        functools.partial(kernel, group),
        out_shape=out_shapes,
        grid_spec=pltpu.PrefetchScalarGridSpec(
            num_scalar_prefetch=3,
            grid=(steps,),
            in_specs=[
                fixed(x.shape),
                pl.BlockSpec((shards // steps, slots, side, side), lambda i, *_: (i, 0, 0, 0)),
                *more_specs,
            ],
            out_specs=[
                pl.BlockSpec(o.shape, lambda i, *_, rank=len(o.shape): (0,) * rank) for o in out_shapes
            ],
            scratch_shapes=[pltpu.VMEM((blocks, tokens, side), jnp.float32)] if scratch else [],
        ),
        compiler_params=pltpu.CompilerParams(vmem_limit_bytes=vmem),
        cost_estimate=pl.CostEstimate(
            flops=4 * shards * slots * tokens * side * side,
            bytes_accessed=shards * slots * side * side * 2,
            transcendentals=0,
        ),
    )(fields, counts, at.reshape(1), x, tiles, *more)


def layout_kernel(
    levels, capacity, index_ref, own_ref, count_ref, left_ref, at_ref,
    code_ref, front_count_ref, length_ref, order_ref, send_ref,
    place_ref, source_ref, late_place_ref, late_source_ref, fronts, backs, kept_fronts, kept_backs, sent_ref,
):
    late_room = late_place_ref.shape[0] // (2 * count_ref.shape[0])
    shards = count_ref.shape[0]
    slots = index_ref.shape[0] // shards
    total = order_ref.shape[0]
    me = at_ref[0]

    def times(count, work):
        def turn(i, carry):
            work(i)
            return carry

        lax.fori_loop(0, count, turn, 0)

    def spot(back, shard, i):
        return (back * shards + shard) * capacity + i

    def build(shard):
        left = left_ref[shard]

        def first(i):
            place_ref[spot(0, shard, i)] = 0
            source_ref[spot(0, shard, i)] = i

        def second(slot, carry):
            front, back = carry
            own = own_ref[shard * slots + slot]
            at = spot(own, shard, jnp.where(own == 1, back, front))
            place_ref[at] = index_ref[shard * slots + slot]
            source_ref[at] = capacity - slots + slot
            return front + 1 - own, back + own

        times(left, first)
        front, back = lax.fori_loop(0, count_ref[shard], second, (left, jnp.int32(0)))
        fronts[shard], backs[shard] = front, back
        kept_fronts[shard], kept_backs[shard] = front, back

    def late_spot(back, shard, i):
        return (back * shards + shard) * late_room + i

    def even(level, back, stride, most, so_far, send_at):
        numbers, kept = (backs, kept_backs) if back else (fronts, kept_fronts)

        def weight(shard):
            return fronts[shard] + backs[shard] if back else fronts[shard]

        def decide(shard):
            partner = shard ^ stride
            excess = lax.div(jnp.maximum(weight(shard) - weight(partner), 0), jnp.int32(2))
            spare = kept[shard] if back else kept[shard] - left_ref[shard]
            room = jnp.minimum(most, capacity - numbers[partner])
            sent_ref[shard] = jnp.minimum(excess, jnp.minimum(room, spare))

        def hand_over(shard):
            partner, sent = shard ^ stride, sent_ref[shard]
            here, there = kept[shard] - sent, numbers[partner]
            there_late = there - kept[partner]

            def one(i):
                old = spot(back, shard, here + i)

                @pl.when(shard == me)
                def _():
                    send_ref[send_at + i] = source_ref[old]

                if level == 0:
                    new = spot(back, partner, there + i)
                    place_ref[new] = place_ref[old]
                    source_ref[new] = so_far + i
                else:
                    new = late_spot(back, partner, there_late + i)
                    late_place_ref[new] = place_ref[old]
                    late_source_ref[new] = so_far + i

            times(sent, one)

        def settle(shard):
            got = sent_ref[shard ^ stride]
            numbers[shard] = numbers[shard] - sent_ref[shard] + got
            kept[shard] = kept[shard] - sent_ref[shard] + (got if level == 0 else 0)

        for work in (decide, hand_over, settle):
            times(shards, work)

    def lay_out(shard):
        front, back = fronts[shard], backs[shard]
        front_count_ref[shard] = front
        length_ref[shard] = front + back

        def copy(count, places, sources, at, start):
            def one(i):
                code_ref[shard * total + start + i] = places[at + i]

                @pl.when(shard == me)
                def _():
                    order_ref[start + i] = sources[at + i]

            times(count, one)

        for back, start, number, kept in ((0, 0, front, kept_fronts[shard]), (1, front, back, kept_backs[shard])):
            copy(kept, place_ref, source_ref, spot(back, shard, 0), start)
            copy(number - kept, late_place_ref, late_source_ref, late_spot(back, shard, 0), start + kept)

    def clear(ref):
        def one(i):
            ref[i] = 0

        times(ref.shape[0], one)

    clear(order_ref)
    clear(send_ref)
    times(shards, build)
    so_far, send_at = capacity, 0
    for level, (stride, most_front, most_back) in enumerate(levels):
        for back, most in ((0, most_front), (1, most_back)):
            if most:
                even(level, back, stride, most, so_far, send_at)
            so_far, send_at = so_far + most, send_at + most
    times(shards, lay_out)


def laid_out(levels, capacity, total, index, own, count, left, blk):
    shards, slots = index.shape
    smem = pl.BlockSpec(memory_space=pltpu.SMEM)
    sizes = [shards * total, shards, shards, total, sum(front + back for _, front, back in levels)]
    late_room = max(sum(front + back for _, front, back in levels[1:]), 1)
    scratch = [2 * shards * capacity] * 2 + [2 * shards * late_room] * 2 + [shards] * 5
    return pl.pallas_call(
        functools.partial(layout_kernel, levels, capacity),
        out_shape=[jax.ShapeDtypeStruct((size,), jnp.int32) for size in sizes],
        in_specs=[smem] * 5,
        out_specs=[smem] * 5,
        scratch_shapes=[pltpu.SMEM((size,), jnp.int32) for size in scratch],
        cost_estimate=pl.CostEstimate(flops=0, bytes_accessed=16 * shards * slots, transcendentals=0),
    )(index.reshape(-1), own.reshape(-1), count, left, blk.reshape(1))


def on_device(
    tokens,
    ln_gain,
    ln_bias,
    fc1_tiles,
    fc1_index,
    fc1_count,
    fc1_bias,
    fc2_tiles,
    fc2_index,
    fc2_count,
    fc2_bias,
    ffn_size,
):
    side = fc1_tiles.shape[-1]
    slots = fc1_tiles.shape[2]
    shards = lax.axis_size("blk")
    token_rows, width = tokens.shape
    first_blocks = fc1_bias.shape[0] // side
    second_blocks = width // side
    share = width // ffn_size
    blk, ffn = lax.axis_index("blk"), lax.axis_index("ffn")
    aligned = share % side == 0
    opening = slots * 5 // 7
    rest = slots - opening
    held = slots + slots // 100
    late_from = held - slots // 3
    levels = [
        (stride, slots // most, max(slots // least, 1))
        for stride, most, least in ((1, 6, 8), (2, 16, 16), (4, 32, 16), (8, slots + 1, 16))
        if shards % (2 * stride) == 0
    ]
    slot_ids = jnp.arange(slots, dtype=jnp.int32)

    def gathered(value):
        return lax.all_gather(value, "blk", axis=0, tiled=True).reshape(shards, -1, side, side)

    tiles1 = gathered(fc1_tiles[0, 0, :opening])
    meta = jnp.concatenate([fc1_index[:, 0], fc2_index[:, 0], fc1_count, fc2_count], axis=1)
    meta = lax.all_gather(meta, "blk", axis=0, tiled=True)
    index1, index2 = meta[:, :slots], meta[:, slots : 2 * slots]
    count1, count2 = meta[:, 2 * slots], meta[:, 2 * slots + 1]
    left1 = jnp.maximum(count1 - opening, 0)

    def in_own_share(index):
        if not aligned:
            return jnp.zeros(index.shape, jnp.bool_)
        return index % second_blocks // (share // side) == ffn

    capacity = rest + slots
    total_ids = jnp.arange(2 * capacity + slots // 4, dtype=jnp.int32)
    codes, fronts, lengths, order, sends = laid_out(
        levels, capacity, total_ids.shape[0], index2, in_own_share(index2).astype(jnp.int32), count2, left1, blk
    )
    codes = codes.reshape(shards, -1)
    sources = jnp.concatenate([fc1_tiles[0, 0, opening:], fc2_tiles[0, 0]], axis=0)
    arrived = []
    for level, (stride, most_front, most_back) in enumerate(levels):
        sending, sends = sends[: most_front + most_back], sends[most_front + most_back :]
        arrived.append(
            lax.ppermute(
                jnp.take(sources, sending, axis=0, mode="clip"),
                "blk",
                [(i, i ^ stride) for i in range(shards)],
            )
        )
        if level == 0:
            sources = jnp.concatenate([sources, arrived.pop()], axis=0)
    sources = jnp.concatenate([sources, *arrived], axis=0)

    tiles2a = gathered(jnp.take(sources, order[:late_from], axis=0, mode="clip"))
    tiles2b = gathered(jnp.take(sources, order[late_from:held], axis=0, mode="clip"))
    misplaced = jnp.stack([jnp.max(fronts) - late_from, jnp.max(lengths) - held, jnp.max(lengths)])
    misplaced = lax.pmax(misplaced, "ffn")

    rows_f = tokens.astype(jnp.float32)
    center = jnp.mean(rows_f, axis=1, keepdims=True)
    spread = jnp.mean((rows_f - center) ** 2, axis=1, keepdims=True)
    normed = ((rows_f - center) / jnp.sqrt(spread + 1e-05) * ln_gain + ln_bias).astype(jnp.bfloat16)
    normed_blocks = normed.reshape(token_rows, second_blocks, side).transpose(1, 0, 2)
    normed_blocks = jnp.pad(normed_blocks, ((0, 1), (0, 0), (0, 0)))
    normed_blocks, misplaced = lax.optimization_barrier((normed_blocks, misplaced))
    some_late = jnp.max(misplaced[:2]) > 0

    (total,) = tile_pass(
        first_kernel,
        index1[:, :opening] // first_blocks,
        index1[:, :opening] % first_blocks,
        slot_ids[:opening] < count1[:, None],
        ffn,
        normed_blocks,
        tiles1,
        [fc1_bias.reshape(first_blocks, 1, side)],
        [fixed((first_blocks, 1, side))],
        [jax.ShapeDtypeStruct((first_blocks, token_rows, side), jnp.float32)],
        first_blocks,
        scratch=False,
    )
    (hidden,) = tile_pass(
        hidden_kernel,
        index1[:, opening:] // first_blocks,
        index1[:, opening:] % first_blocks,
        slot_ids[opening:] < count1[:, None],
        ffn,
        normed_blocks,
        tiles2a,
        [total],
        [fixed(total.shape)],
        [jax.ShapeDtypeStruct((first_blocks + 1, token_rows, side), jnp.bfloat16)],
        first_blocks,
    )

    def second_pass(places, live, tiles, steps=2, group=4):
        return tile_pass(
            partial_kernel,
            places // second_blocks,
            places % second_blocks,
            live,
            ffn,
            hidden,
            tiles,
            [],
            [],
            [
                jax.ShapeDtypeStruct((second_blocks, token_rows, side), jnp.float32),
                jax.ShapeDtypeStruct((token_rows, width), jnp.bfloat16),
            ],
            second_blocks,
            steps=steps,
            group=group,
            scratch=False,
        )

    def own_cols(value):
        return lax.dynamic_slice_in_dim(value, ffn * share, share, 1).astype(jnp.float32)

    def from_others(partial_value):
        branch = jnp.zeros((token_rows, share), jnp.float32)
        for shift in range(1, ffn_size):
            to = lax.rem(ffn + shift, ffn_size)
            arrived = lax.ppermute(
                lax.dynamic_slice_in_dim(partial_value, to * share, share, 1),
                "ffn",
                [(i, (i + shift) % ffn_size) for i in range(ffn_size)],
            )
            branch = branch + arrived.astype(jnp.float32)
        return branch

    in_front = total_ids < fronts[:, None]
    in_second = (total_ids >= left1[:, None]) & (total_ids < lengths[:, None])
    total, partial_value = second_pass(codes[:, :late_from], in_second[:, :late_from], tiles2a)
    last_codes = codes[:, late_from:held]
    last_own = (in_second & ~in_front)[:, late_from:held]
    branch = from_others(partial_value)

    def with_late(branch):
        chunk = slots // 4
        start = jnp.where(misplaced[0] > 0, late_from, held)
        late = in_second & (in_front | (total_ids >= held))

        def one_more(number, branch):
            at = start + number * chunk
            here = jnp.take(sources, lax.dynamic_slice_in_dim(order, at, chunk), axis=0, mode="clip")
            part = [lax.dynamic_slice_in_dim(v, at, chunk, 1) for v in (codes, late)]
            _, extra = second_pass(*part, gathered(here), steps=1, group=1)
            return branch + from_others(extra) + own_cols(extra)

        return lax.fori_loop(0, (misplaced[2] - start + chunk - 1) // chunk, one_more, branch)

    if not aligned:
        branch = lax.cond(some_late, with_late, lambda branch: branch, branch)
        more, _ = second_pass(last_codes, last_own, tiles2b)
        own = (total + more).transpose(1, 0, 2).reshape(token_rows, width)
        return (own_cols(tokens) + own_cols(own) + branch + fc2_bias).astype(jnp.bfloat16)

    share_blocks = share // side
    last_rows, last_cols = last_codes // second_blocks, last_codes % second_blocks % share_blocks
    last_plan = planned(last_rows, last_cols, last_own, share_blocks, first_blocks, 4, 4)
    bias_row = fc2_bias.reshape(1, share)
    last_plan, branch, bias_row = lax.optimization_barrier((last_plan, branch, bias_row))
    last_pass = functools.partial(
        tile_pass,
        result_kernel,
        last_rows,
        last_cols,
        last_own,
        ffn,
        hidden,
        tiles2b,
        more_specs=[
            pl.BlockSpec(
                (share_blocks, token_rows, side),
                lambda i, fields, counts, at: (at[0], 0, 0),
                pipeline_mode=pl.Buffered(1),
            ),
            pl.BlockSpec(
                (token_rows, share),
                lambda i, fields, counts, at: (0, at[0]),
                pipeline_mode=pl.Buffered(1),
            ),
            fixed((token_rows, share)),
            fixed((1, share)),
        ],
        out_shapes=[jax.ShapeDtypeStruct((token_rows, share), jnp.bfloat16)],
        blocks=share_blocks,
        steps=4,
        group=4,
        vmem=LAST_VMEM_BYTES,
        plan=last_plan,
    )

    def finished(branch):
        return last_pass(more=[total, tokens, branch, bias_row])[0]

    return lax.cond(some_late, lambda branch: finished(with_late(branch)), finished, branch)


def solution(mesh):
    placed = (
        P("blk", None),
        P(),
        P(),
        P("blk", "ffn", None, None, None),
        P("blk", "ffn", None),
        P("blk", "ffn"),
        P("ffn"),
        P("blk", "ffn", None, None, None),
        P("blk", "ffn", None),
        P("blk", "ffn"),
        P("ffn"),
    )
    return jax.shard_map(
        functools.partial(on_device, ffn_size=mesh.shape["ffn"]),
        mesh=mesh,
        in_specs=placed,
        out_specs=P("blk", "ffn"),
        check_vma=False,
    )
```

```python
import functools

import jax
import jax.numpy as jnp
from jax import lax
from jax.experimental import pallas as pl
from jax.experimental.pallas import tpu as pltpu
from jax.sharding import PartitionSpec as P

UNROLL = 8
VMEM_BYTES = 56 * 1024 * 1024
LAST_VMEM_BYTES = 26 * 1024 * 1024


def group_kernel(group, size, zero_row, row_ref, col_ref, field_ref, count_ref, fill_ref, open_ref):
    step, steps = pl.program_id(0), pl.num_programs(0)
    listed = row_ref.shape[0] // steps

    def field(number, at):
        return (number * steps + step) * size + at

    def clear(at, carry):
        field_ref[field(0, at)] = 0
        for g in range(group):
            field_ref[field(1 + g, at)] = 0
            field_ref[field(1 + group + g, at)] = zero_row
        return carry

    def no_group(c, carry):
        fill_ref[c] = 0
        open_ref[c] = 0
        return carry

    def place(tile, groups):
        col = col_ref[step * listed + tile]
        held = jnp.maximum(col, 0)
        filled = fill_ref[held]
        opens = (col >= 0) & (filled == 0)
        at = jnp.where(opens, groups, open_ref[held])

        @pl.when(col >= 0)
        def _():
            open_ref[held] = at
            fill_ref[held] = jnp.where(filled == group - 1, 0, filled + 1)
            field_ref[field(0, at)] = col
            field_ref[field(1 + filled, at)] = tile
            field_ref[field(1 + group + filled, at)] = row_ref[step * listed + tile]

        return groups + opens.astype(jnp.int32)

    lax.fori_loop(0, size, clear, 0)
    lax.fori_loop(0, fill_ref.shape[0], no_group, 0)
    count_ref[step] = lax.fori_loop(0, listed, place, jnp.int32(0))


def group_up(rows, cols, live, blocks, zero_row, group):
    steps, listed = rows.shape
    most = (listed + (group - 1) * min(blocks, listed)) // group
    size = -(-most // UNROLL) * UNROLL
    smem = pl.BlockSpec(memory_space=pltpu.SMEM)
    return pl.pallas_call(
        functools.partial(group_kernel, group, size, zero_row),
        out_shape=[
            jax.ShapeDtypeStruct(((2 * group + 1) * steps * size,), jnp.int32),
            jax.ShapeDtypeStruct((steps,), jnp.int32),
        ],
        grid=(steps,),
        in_specs=[smem, smem],
        out_specs=[smem, smem],
        scratch_shapes=[pltpu.SMEM((blocks,), jnp.int32), pltpu.SMEM((blocks,), jnp.int32)],
        cost_estimate=pl.CostEstimate(flops=0, bytes_accessed=16 * steps * listed, transcendentals=0),
    )(rows.reshape(-1), jnp.where(live, cols, -1).reshape(-1))


def add_block(field_ref, count_ref, x_ref, w_ref, acc, group):
    step, steps = pl.program_id(0), pl.num_programs(0)
    w_ref = w_ref.reshape(-1, *w_ref.shape[2:])
    fields = 2 * group + 1
    size = field_ref.shape[0] // (fields * steps)

    def one(at):
        col, *parts = (field_ref[(f * steps + step) * size + at] for f in range(fields))
        left = jnp.concatenate([x_ref[row] for row in parts[group:]], axis=1)
        right = jnp.concatenate([w_ref[tile] for tile in parts[:group]], axis=0)
        acc[col] += jnp.dot(left, right, preferred_element_type=jnp.float32)

    def several(turn, carry):
        for u in range(UNROLL):
            one(turn * UNROLL + u)
        return carry

    lax.fori_loop(0, lax.div(count_ref[step] + UNROLL - 1, jnp.int32(UNROLL)), several, 0)


def for_blocks(count, work):
    def turn(c, carry):
        work(c)
        return carry

    lax.fori_loop(0, count, turn, 0)


def columns(c, width):
    return pl.ds(pl.multiple_of(c * width, width), width)


def at_start(work):
    pl.when(pl.program_id(0) == 0)(work)


def at_end(work):
    pl.when(pl.program_id(0) == pl.num_programs(0) - 1)(work)


def first_kernel(group, field_ref, count_ref, at_ref, x_ref, w_ref, bias_ref, sum_ref):
    @at_start
    def _():
        def fill(c):
            sum_ref[c] = jnp.broadcast_to(bias_ref[c], sum_ref.shape[1:])

        for_blocks(sum_ref.shape[0], fill)

    add_block(field_ref, count_ref, x_ref, w_ref, sum_ref, group)


def hidden_kernel(group, field_ref, count_ref, at_ref, x_ref, w_ref, sum_ref, out_ref, acc):
    blocks = acc.shape[0]

    @at_start
    def _():
        def fill(c):
            acc[c] = sum_ref[c]

        for_blocks(blocks, fill)

    add_block(field_ref, count_ref, x_ref, w_ref, acc, group)

    @at_end
    def _():
        def finish(c):
            out_ref[c] = jnp.maximum(acc[c], 0.0).astype(out_ref.dtype)

        for_blocks(blocks, finish)
        out_ref[blocks] = jnp.zeros(out_ref.shape[1:], out_ref.dtype)


def partial_kernel(group, field_ref, count_ref, at_ref, x_ref, w_ref, sum_ref, out_ref):
    blocks, width = sum_ref.shape[0], sum_ref.shape[2]

    @at_start
    def _():
        def fill(c):
            sum_ref[c] = jnp.zeros(sum_ref.shape[1:], sum_ref.dtype)

        for_blocks(blocks, fill)

    add_block(field_ref, count_ref, x_ref, w_ref, sum_ref, group)

    @at_end
    def _():
        def finish(c):
            out_ref[:, columns(c, width)] = sum_ref[c].astype(out_ref.dtype)

        for_blocks(blocks, finish)


def result_kernel(
    group, field_ref, count_ref, at_ref,
    x_ref, w_ref, sum_ref, token_ref, other_ref, bias_ref, out_ref, acc,
):
    blocks, width = acc.shape[0], acc.shape[2]

    @at_start
    def _():
        def fill(c):
            acc[c] = sum_ref[c]

        for_blocks(blocks, fill)

    add_block(field_ref, count_ref, x_ref, w_ref, acc, group)

    @at_end
    def _():
        def finish(c):
            cols = columns(c, width)
            value = token_ref[:, cols].astype(jnp.float32) + (acc[c] + other_ref[:, cols])
            out_ref[:, cols] = (value + bias_ref[:, cols]).astype(out_ref.dtype)

        for_blocks(blocks, finish)


def fixed(shape):
    return pl.BlockSpec(shape, lambda i, *_: (0,) * len(shape), pipeline_mode=pl.Buffered(1))


def planned(rows, cols, live, blocks, zero_row, steps, group):
    steps = steps if rows.shape[0] % steps == 0 else 1
    return group_up(*(v.reshape(steps, -1) for v in (rows, cols, live)), blocks, zero_row, group)


def tile_pass(
    kernel, rows, cols, live, at, x, tiles, more, more_specs, out_shapes, blocks,
    steps=4, group=2, scratch=True, vmem=VMEM_BYTES, plan=None,
):
    shards, slots = rows.shape
    side, tokens = tiles.shape[-1], x.shape[1]
    steps = steps if shards % steps == 0 else 1
    if plan is None:
        plan = planned(rows, cols, live, blocks, x.shape[0] - 1, steps, group)
    fields, counts = plan
    return pl.pallas_call(
        functools.partial(kernel, group),
        out_shape=out_shapes,
        grid_spec=pltpu.PrefetchScalarGridSpec(
            num_scalar_prefetch=3,
            grid=(steps,),
            in_specs=[
                fixed(x.shape),
                pl.BlockSpec((shards // steps, slots, side, side), lambda i, *_: (i, 0, 0, 0)),
                *more_specs,
            ],
            out_specs=[
                pl.BlockSpec(o.shape, lambda i, *_, rank=len(o.shape): (0,) * rank) for o in out_shapes
            ],
            scratch_shapes=[pltpu.VMEM((blocks, tokens, side), jnp.float32)] if scratch else [],
        ),
        compiler_params=pltpu.CompilerParams(vmem_limit_bytes=vmem),
        cost_estimate=pl.CostEstimate(
            flops=4 * shards * slots * tokens * side * side,
            bytes_accessed=shards * slots * side * side * 2,
            transcendentals=0,
        ),
    )(fields, counts, at.reshape(1), x, tiles, *more)


def layout_kernel(
    levels, capacity, index_ref, own_ref, count_ref, left_ref, at_ref,
    code_ref, front_count_ref, length_ref, order_ref, send_ref,
    place_ref, source_ref, late_place_ref, late_source_ref, fronts, backs, kept_fronts, kept_backs, sent_ref,
):
    late_room = late_place_ref.shape[0] // (2 * count_ref.shape[0])
    shards = count_ref.shape[0]
    slots = index_ref.shape[0] // shards
    total = order_ref.shape[0]
    me = at_ref[0]

    def times(count, work):
        def turn(i, carry):
            work(i)
            return carry

        lax.fori_loop(0, count, turn, 0)

    def spot(back, shard, i):
        return (back * shards + shard) * capacity + i

    def build(shard):
        left = left_ref[shard]

        def first(i):
            place_ref[spot(0, shard, i)] = 0
            source_ref[spot(0, shard, i)] = i

        def second(slot, carry):
            front, back = carry
            own = own_ref[shard * slots + slot]
            at = spot(own, shard, jnp.where(own == 1, back, front))
            place_ref[at] = index_ref[shard * slots + slot]
            source_ref[at] = capacity - slots + slot
            return front + 1 - own, back + own

        times(left, first)
        front, back = lax.fori_loop(0, count_ref[shard], second, (left, jnp.int32(0)))
        fronts[shard], backs[shard] = front, back
        kept_fronts[shard], kept_backs[shard] = front, back

    def late_spot(back, shard, i):
        return (back * shards + shard) * late_room + i

    def even(level, back, stride, most, so_far, send_at):
        numbers, kept = (backs, kept_backs) if back else (fronts, kept_fronts)

        def weight(shard):
            return fronts[shard] + backs[shard] if back else fronts[shard]

        def decide(shard):
            partner = shard ^ stride
            excess = lax.div(jnp.maximum(weight(shard) - weight(partner), 0), jnp.int32(2))
            spare = kept[shard] if back else kept[shard] - left_ref[shard]
            room = jnp.minimum(most, capacity - numbers[partner])
            sent_ref[shard] = jnp.minimum(excess, jnp.minimum(room, spare))

        def hand_over(shard):
            partner, sent = shard ^ stride, sent_ref[shard]
            here, there = kept[shard] - sent, numbers[partner]
            there_late = there - kept[partner]

            def one(i):
                old = spot(back, shard, here + i)

                @pl.when(shard == me)
                def _():
                    send_ref[send_at + i] = source_ref[old]

                if level == 0:
                    new = spot(back, partner, there + i)
                    place_ref[new] = place_ref[old]
                    source_ref[new] = so_far + i
                else:
                    new = late_spot(back, partner, there_late + i)
                    late_place_ref[new] = place_ref[old]
                    late_source_ref[new] = so_far + i

            times(sent, one)

        def settle(shard):
            got = sent_ref[shard ^ stride]
            numbers[shard] = numbers[shard] - sent_ref[shard] + got
            kept[shard] = kept[shard] - sent_ref[shard] + (got if level == 0 else 0)

        for work in (decide, hand_over, settle):
            times(shards, work)

    def lay_out(shard):
        front, back = fronts[shard], backs[shard]
        front_count_ref[shard] = front
        length_ref[shard] = front + back

        def copy(count, places, sources, at, start):
            def one(i):
                code_ref[shard * total + start + i] = places[at + i]

                @pl.when(shard == me)
                def _():
                    order_ref[start + i] = sources[at + i]

            times(count, one)

        for back, start, number, kept in ((0, 0, front, kept_fronts[shard]), (1, front, back, kept_backs[shard])):
            copy(kept, place_ref, source_ref, spot(back, shard, 0), start)
            copy(number - kept, late_place_ref, late_source_ref, late_spot(back, shard, 0), start + kept)

    def clear(ref):
        def one(i):
            ref[i] = 0

        times(ref.shape[0], one)

    clear(order_ref)
    clear(send_ref)
    times(shards, build)
    so_far, send_at = capacity, 0
    for level, (stride, most_front, most_back) in enumerate(levels):
        for back, most in ((0, most_front), (1, most_back)):
            if most:
                even(level, back, stride, most, so_far, send_at)
            so_far, send_at = so_far + most, send_at + most
    times(shards, lay_out)


def laid_out(levels, capacity, total, index, own, count, left, blk):
    shards, slots = index.shape
    smem = pl.BlockSpec(memory_space=pltpu.SMEM)
    sizes = [shards * total, shards, shards, total, sum(front + back for _, front, back in levels)]
    late_room = max(sum(front + back for _, front, back in levels[1:]), 1)
    scratch = [2 * shards * capacity] * 2 + [2 * shards * late_room] * 2 + [shards] * 5
    return pl.pallas_call(
        functools.partial(layout_kernel, levels, capacity),
        out_shape=[jax.ShapeDtypeStruct((size,), jnp.int32) for size in sizes],
        in_specs=[smem] * 5,
        out_specs=[smem] * 5,
        scratch_shapes=[pltpu.SMEM((size,), jnp.int32) for size in scratch],
        cost_estimate=pl.CostEstimate(flops=0, bytes_accessed=16 * shards * slots, transcendentals=0),
    )(index.reshape(-1), own.reshape(-1), count, left, blk.reshape(1))


def on_device(
    tokens,
    ln_gain,
    ln_bias,
    fc1_tiles,
    fc1_index,
    fc1_count,
    fc1_bias,
    fc2_tiles,
    fc2_index,
    fc2_count,
    fc2_bias,
    ffn_size,
):
    side = fc1_tiles.shape[-1]
    slots = fc1_tiles.shape[2]
    shards = lax.axis_size("blk")
    token_rows, width = tokens.shape
    first_blocks = fc1_bias.shape[0] // side
    second_blocks = width // side
    share = width // ffn_size
    blk, ffn = lax.axis_index("blk"), lax.axis_index("ffn")
    aligned = share % side == 0
    opening = slots * 7 // 11
    rest = slots - opening
    held = slots + slots // 14
    late_from = held - slots // 3
    levels = [
        (stride, slots // most, max(slots // least, 1))
        for stride, most, least in ((1, 4, 5), (2, 14, 16), (4, 25, 16), (8, 50, 16))
        if shards % (2 * stride) == 0
    ]
    slot_ids = jnp.arange(slots, dtype=jnp.int32)

    def gathered(value):
        return lax.all_gather(value, "blk", axis=0, tiled=True).reshape(shards, -1, side, side)

    tiles1 = gathered(fc1_tiles[0, 0, :opening])
    meta = jnp.concatenate([fc1_index[:, 0], fc2_index[:, 0], fc1_count, fc2_count], axis=1)
    meta = lax.all_gather(meta, "blk", axis=0, tiled=True)
    index1, index2 = meta[:, :slots], meta[:, slots : 2 * slots]
    count1, count2 = meta[:, 2 * slots], meta[:, 2 * slots + 1]
    left1 = jnp.maximum(count1 - opening, 0)

    def in_own_share(index):
        if not aligned:
            return jnp.zeros(index.shape, jnp.bool_)
        return index % second_blocks // (share // side) == ffn

    capacity = rest + slots
    total_ids = jnp.arange(2 * capacity + slots // 4, dtype=jnp.int32)
    codes, fronts, lengths, order, sends = laid_out(
        levels, capacity, total_ids.shape[0], index2, in_own_share(index2).astype(jnp.int32), count2, left1, blk
    )
    codes = codes.reshape(shards, -1)
    sources = jnp.concatenate([fc1_tiles[0, 0, opening:], fc2_tiles[0, 0]], axis=0)
    arrived = []
    for level, (stride, most_front, most_back) in enumerate(levels):
        sending, sends = sends[: most_front + most_back], sends[most_front + most_back :]
        arrived.append(
            lax.ppermute(
                jnp.take(sources, sending, axis=0, mode="clip"),
                "blk",
                [(i, i ^ stride) for i in range(shards)],
            )
        )
        if level == 0:
            sources = jnp.concatenate([sources, arrived.pop()], axis=0)
    sources = jnp.concatenate([sources, *arrived], axis=0)

    tiles2a = gathered(jnp.take(sources, order[:late_from], axis=0, mode="clip"))
    tiles2b = gathered(jnp.take(sources, order[late_from:held], axis=0, mode="clip"))
    misplaced = jnp.stack([jnp.max(fronts) - late_from, jnp.max(lengths) - held, jnp.max(lengths)])
    misplaced = lax.pmax(misplaced, "ffn")

    rows_f = tokens.astype(jnp.float32)
    center = jnp.mean(rows_f, axis=1, keepdims=True)
    spread = jnp.mean((rows_f - center) ** 2, axis=1, keepdims=True)
    normed = ((rows_f - center) / jnp.sqrt(spread + 1e-05) * ln_gain + ln_bias).astype(jnp.bfloat16)
    normed_blocks = normed.reshape(token_rows, second_blocks, side).transpose(1, 0, 2)
    normed_blocks = jnp.pad(normed_blocks, ((0, 1), (0, 0), (0, 0)))
    normed_blocks, misplaced = lax.optimization_barrier((normed_blocks, misplaced))
    some_late = jnp.max(misplaced[:2]) > 0

    (total,) = tile_pass(
        first_kernel,
        index1[:, :opening] // first_blocks,
        index1[:, :opening] % first_blocks,
        slot_ids[:opening] < count1[:, None],
        ffn,
        normed_blocks,
        tiles1,
        [fc1_bias.reshape(first_blocks, 1, side)],
        [fixed((first_blocks, 1, side))],
        [jax.ShapeDtypeStruct((first_blocks, token_rows, side), jnp.float32)],
        first_blocks,
        scratch=False,
    )
    (hidden,) = tile_pass(
        hidden_kernel,
        index1[:, opening:] // first_blocks,
        index1[:, opening:] % first_blocks,
        slot_ids[opening:] < count1[:, None],
        ffn,
        normed_blocks,
        tiles2a,
        [total],
        [fixed(total.shape)],
        [jax.ShapeDtypeStruct((first_blocks + 1, token_rows, side), jnp.bfloat16)],
        first_blocks,
    )

    def second_pass(places, live, tiles, steps=2, group=4):
        return tile_pass(
            partial_kernel,
            places // second_blocks,
            places % second_blocks,
            live,
            ffn,
            hidden,
            tiles,
            [],
            [],
            [
                jax.ShapeDtypeStruct((second_blocks, token_rows, side), jnp.float32),
                jax.ShapeDtypeStruct((token_rows, width), jnp.bfloat16),
            ],
            second_blocks,
            steps=steps,
            group=group,
            scratch=False,
        )

    def own_cols(value):
        return lax.dynamic_slice_in_dim(value, ffn * share, share, 1).astype(jnp.float32)

    def from_others(partial_value):
        branch = jnp.zeros((token_rows, share), jnp.float32)
        for shift in range(1, ffn_size):
            to = lax.rem(ffn + shift, ffn_size)
            arrived = lax.ppermute(
                lax.dynamic_slice_in_dim(partial_value, to * share, share, 1),
                "ffn",
                [(i, (i + shift) % ffn_size) for i in range(ffn_size)],
            )
            branch = branch + arrived.astype(jnp.float32)
        return branch

    in_front = total_ids < fronts[:, None]
    in_second = (total_ids >= left1[:, None]) & (total_ids < lengths[:, None])
    total, partial_value = second_pass(codes[:, :late_from], in_second[:, :late_from], tiles2a)
    last_codes = codes[:, late_from:held]
    last_own = (in_second & ~in_front)[:, late_from:held]
    branch = from_others(partial_value)

    def with_late(branch):
        chunk = slots // 4
        start = jnp.where(misplaced[0] > 0, late_from, held)
        late = in_second & (in_front | (total_ids >= held))

        def one_more(number, branch):
            at = start + number * chunk
            here = jnp.take(sources, lax.dynamic_slice_in_dim(order, at, chunk), axis=0, mode="clip")
            part = [lax.dynamic_slice_in_dim(v, at, chunk, 1) for v in (codes, late)]
            _, extra = second_pass(*part, gathered(here), steps=1, group=1)
            return branch + from_others(extra) + own_cols(extra)

        return lax.fori_loop(0, (misplaced[2] - start + chunk - 1) // chunk, one_more, branch)

    if not aligned:
        branch = lax.cond(some_late, with_late, lambda branch: branch, branch)
        more, _ = second_pass(last_codes, last_own, tiles2b)
        own = (total + more).transpose(1, 0, 2).reshape(token_rows, width)
        return (own_cols(tokens) + own_cols(own) + branch + fc2_bias).astype(jnp.bfloat16)

    share_blocks = share // side
    last_rows, last_cols = last_codes // second_blocks, last_codes % second_blocks % share_blocks
    last_plan = planned(last_rows, last_cols, last_own, share_blocks, first_blocks, 4, 4)
    bias_row = fc2_bias.reshape(1, share)
    last_plan, branch, bias_row = lax.optimization_barrier((last_plan, branch, bias_row))
    last_pass = functools.partial(
        tile_pass,
        result_kernel,
        last_rows,
        last_cols,
        last_own,
        ffn,
        hidden,
        tiles2b,
        more_specs=[
            pl.BlockSpec(
                (share_blocks, token_rows, side),
                lambda i, fields, counts, at: (at[0], 0, 0),
                pipeline_mode=pl.Buffered(1),
            ),
            pl.BlockSpec(
                (token_rows, share),
                lambda i, fields, counts, at: (0, at[0]),
                pipeline_mode=pl.Buffered(1),
            ),
            fixed((token_rows, share)),
            fixed((1, share)),
        ],
        out_shapes=[jax.ShapeDtypeStruct((token_rows, share), jnp.bfloat16)],
        blocks=share_blocks,
        steps=4,
        group=4,
        vmem=LAST_VMEM_BYTES,
        plan=last_plan,
    )

    def finished(branch):
        return last_pass(more=[total, tokens, branch, bias_row])[0]

    return lax.cond(some_late, lambda branch: finished(with_late(branch)), finished, branch)


def solution(mesh):
    placed = (
        P("blk", None),
        P(),
        P(),
        P("blk", "ffn", None, None, None),
        P("blk", "ffn", None),
        P("blk", "ffn"),
        P("ffn"),
        P("blk", "ffn", None, None, None),
        P("blk", "ffn", None),
        P("blk", "ffn"),
        P("ffn"),
    )
    return jax.shard_map(
        functools.partial(on_device, ffn_size=mesh.shape["ffn"]),
        mesh=mesh,
        in_specs=placed,
        out_specs=P("blk", "ffn"),
        check_vma=False,
    )
```

```python
import functools

import jax
import jax.numpy as jnp
from jax import lax
from jax.experimental import pallas as pl
from jax.experimental.pallas import tpu as pltpu
from jax.sharding import PartitionSpec as P

UNROLL = 8
VMEM_BYTES = 56 * 1024 * 1024
LAST_VMEM_BYTES = 36 * 1024 * 1024


def group_kernel(group, size, zero_row, row_ref, col_ref, field_ref, count_ref, fill_ref, open_ref):
    step, steps = pl.program_id(0), pl.num_programs(0)
    listed = row_ref.shape[0] // steps

    def field(number, at):
        return (number * steps + step) * size + at

    def clear(at, carry):
        field_ref[field(0, at)] = 0
        for g in range(group):
            field_ref[field(1 + g, at)] = 0
            field_ref[field(1 + group + g, at)] = zero_row
        return carry

    def no_group(c, carry):
        fill_ref[c] = 0
        open_ref[c] = 0
        return carry

    def place(tile, groups):
        col = col_ref[step * listed + tile]
        held = jnp.maximum(col, 0)
        filled = fill_ref[held]
        opens = (col >= 0) & (filled == 0)
        at = jnp.where(opens, groups, open_ref[held])

        @pl.when(col >= 0)
        def _():
            open_ref[held] = at
            fill_ref[held] = jnp.where(filled == group - 1, 0, filled + 1)
            field_ref[field(0, at)] = col
            field_ref[field(1 + filled, at)] = tile
            field_ref[field(1 + group + filled, at)] = row_ref[step * listed + tile]

        return groups + opens.astype(jnp.int32)

    lax.fori_loop(0, size, clear, 0)
    lax.fori_loop(0, fill_ref.shape[0], no_group, 0)
    count_ref[step] = lax.fori_loop(0, listed, place, jnp.int32(0))


def group_up(rows, cols, live, blocks, zero_row, group):
    steps, listed = rows.shape
    most = (listed + (group - 1) * min(blocks, listed)) // group
    size = -(-most // UNROLL) * UNROLL
    smem = pl.BlockSpec(memory_space=pltpu.SMEM)
    return pl.pallas_call(
        functools.partial(group_kernel, group, size, zero_row),
        out_shape=[
            jax.ShapeDtypeStruct(((2 * group + 1) * steps * size,), jnp.int32),
            jax.ShapeDtypeStruct((steps,), jnp.int32),
        ],
        grid=(steps,),
        in_specs=[smem, smem],
        out_specs=[smem, smem],
        scratch_shapes=[pltpu.SMEM((blocks,), jnp.int32), pltpu.SMEM((blocks,), jnp.int32)],
        cost_estimate=pl.CostEstimate(flops=0, bytes_accessed=16 * steps * listed, transcendentals=0),
    )(rows.reshape(-1), jnp.where(live, cols, -1).reshape(-1))


def add_block(field_ref, count_ref, x_ref, w_ref, acc, group):
    step, steps = pl.program_id(0), pl.num_programs(0)
    w_ref = w_ref.reshape(-1, *w_ref.shape[2:])
    fields = 2 * group + 1
    size = field_ref.shape[0] // (fields * steps)

    def one(at):
        col, *parts = (field_ref[(f * steps + step) * size + at] for f in range(fields))
        left = jnp.concatenate([x_ref[row] for row in parts[group:]], axis=1)
        right = jnp.concatenate([w_ref[tile] for tile in parts[:group]], axis=0)
        acc[col] += jnp.dot(left, right, preferred_element_type=jnp.float32)

    def several(turn, carry):
        for u in range(UNROLL):
            one(turn * UNROLL + u)
        return carry

    lax.fori_loop(0, lax.div(count_ref[step] + UNROLL - 1, jnp.int32(UNROLL)), several, 0)


def for_blocks(count, work):
    def turn(c, carry):
        work(c)
        return carry

    lax.fori_loop(0, count, turn, 0)


def columns(c, width):
    return pl.ds(pl.multiple_of(c * width, width), width)


def at_start(work):
    pl.when(pl.program_id(0) == 0)(work)


def at_end(work):
    pl.when(pl.program_id(0) == pl.num_programs(0) - 1)(work)


def first_kernel(group, field_ref, count_ref, at_ref, x_ref, w_ref, bias_ref, sum_ref):
    @at_start
    def _():
        def fill(c):
            sum_ref[c] = jnp.broadcast_to(bias_ref[c], sum_ref.shape[1:])

        for_blocks(sum_ref.shape[0], fill)

    add_block(field_ref, count_ref, x_ref, w_ref, sum_ref, group)


def hidden_kernel(group, field_ref, count_ref, at_ref, x_ref, w_ref, sum_ref, out_ref, acc):
    blocks = acc.shape[0]

    @at_start
    def _():
        def fill(c):
            acc[c] = sum_ref[c]

        for_blocks(blocks, fill)

    add_block(field_ref, count_ref, x_ref, w_ref, acc, group)

    @at_end
    def _():
        def finish(c):
            out_ref[c] = jnp.maximum(acc[c], 0.0).astype(out_ref.dtype)

        for_blocks(blocks, finish)
        out_ref[blocks] = jnp.zeros(out_ref.shape[1:], out_ref.dtype)


def partial_kernel(group, field_ref, count_ref, at_ref, x_ref, w_ref, sum_ref, out_ref):
    blocks, width = sum_ref.shape[0], sum_ref.shape[2]

    @at_start
    def _():
        def fill(c):
            sum_ref[c] = jnp.zeros(sum_ref.shape[1:], sum_ref.dtype)

        for_blocks(blocks, fill)

    add_block(field_ref, count_ref, x_ref, w_ref, sum_ref, group)

    @at_end
    def _():
        def finish(c):
            out_ref[:, columns(c, width)] = sum_ref[c].astype(out_ref.dtype)

        for_blocks(blocks, finish)


def result_kernel(
    group, field_ref, count_ref, at_ref,
    x_ref, w_ref, sum_ref, token_ref, other_ref, bias_ref, out_ref, acc,
):
    blocks, width = acc.shape[0], acc.shape[2]

    @at_start
    def _():
        def fill(c):
            acc[c] = sum_ref[c]

        for_blocks(blocks, fill)

    add_block(field_ref, count_ref, x_ref, w_ref, acc, group)

    @at_end
    def _():
        def finish(c):
            cols = columns(c, width)
            value = token_ref[:, cols].astype(jnp.float32) + (acc[c] + other_ref[:, cols])
            out_ref[:, cols] = (value + bias_ref[:, cols]).astype(out_ref.dtype)

        for_blocks(blocks, finish)


def fixed(shape):
    return pl.BlockSpec(shape, lambda i, *_: (0,) * len(shape), pipeline_mode=pl.Buffered(1))


def planned(rows, cols, live, blocks, zero_row, steps, group):
    steps = steps if rows.shape[0] % steps == 0 else 1
    return group_up(*(v.reshape(steps, -1) for v in (rows, cols, live)), blocks, zero_row, group)


def tile_pass(
    kernel, rows, cols, live, at, x, tiles, more, more_specs, out_shapes, blocks,
    steps=4, group=2, scratch=True, vmem=VMEM_BYTES, plan=None,
):
    shards, slots = rows.shape
    side, tokens = tiles.shape[-1], x.shape[1]
    steps = steps if shards % steps == 0 else 1
    if plan is None:
        plan = planned(rows, cols, live, blocks, x.shape[0] - 1, steps, group)
    fields, counts = plan
    return pl.pallas_call(
        functools.partial(kernel, group),
        out_shape=out_shapes,
        grid_spec=pltpu.PrefetchScalarGridSpec(
            num_scalar_prefetch=3,
            grid=(steps,),
            in_specs=[
                fixed(x.shape),
                pl.BlockSpec((shards // steps, slots, side, side), lambda i, *_: (i, 0, 0, 0)),
                *more_specs,
            ],
            out_specs=[
                pl.BlockSpec(o.shape, lambda i, *_, rank=len(o.shape): (0,) * rank) for o in out_shapes
            ],
            scratch_shapes=[pltpu.VMEM((blocks, tokens, side), jnp.float32)] if scratch else [],
        ),
        compiler_params=pltpu.CompilerParams(vmem_limit_bytes=vmem),
        cost_estimate=pl.CostEstimate(
            flops=4 * shards * slots * tokens * side * side,
            bytes_accessed=shards * slots * side * side * 2,
            transcendentals=0,
        ),
    )(fields, counts, at.reshape(1), x, tiles, *more)


def layout_kernel(
    levels, capacity, index_ref, own_ref, count_ref, left_ref, at_ref,
    code_ref, front_count_ref, length_ref, order_ref, send_ref,
    place_ref, source_ref, late_place_ref, late_source_ref, fronts, backs, kept_fronts, kept_backs, sent_ref,
):
    late_room = late_place_ref.shape[0] // (2 * count_ref.shape[0])
    shards = count_ref.shape[0]
    slots = index_ref.shape[0] // shards
    total = order_ref.shape[0]
    me = at_ref[0]

    def times(count, work):
        def turn(i, carry):
            work(i)
            return carry

        lax.fori_loop(0, count, turn, 0)

    def spot(back, shard, i):
        return (back * shards + shard) * capacity + i

    def build(shard):
        left = left_ref[shard]

        def first(i):
            place_ref[spot(0, shard, i)] = 0
            source_ref[spot(0, shard, i)] = i

        def second(slot, carry):
            front, back = carry
            own = own_ref[shard * slots + slot]
            at = spot(own, shard, jnp.where(own == 1, back, front))
            place_ref[at] = index_ref[shard * slots + slot]
            source_ref[at] = capacity - slots + slot
            return front + 1 - own, back + own

        times(left, first)
        front, back = lax.fori_loop(0, count_ref[shard], second, (left, jnp.int32(0)))
        fronts[shard], backs[shard] = front, back
        kept_fronts[shard], kept_backs[shard] = front, back

    def late_spot(back, shard, i):
        return (back * shards + shard) * late_room + i

    def even(level, back, stride, most, so_far, send_at):
        numbers, kept = (backs, kept_backs) if back else (fronts, kept_fronts)

        def weight(shard):
            return fronts[shard] + backs[shard] if back else fronts[shard]

        def decide(shard):
            partner = shard ^ stride
            excess = lax.div(jnp.maximum(weight(shard) - weight(partner), 0), jnp.int32(2))
            spare = kept[shard] if back else kept[shard] - left_ref[shard]
            room = jnp.minimum(most, capacity - numbers[partner])
            sent_ref[shard] = jnp.minimum(excess, jnp.minimum(room, spare))

        def hand_over(shard):
            partner, sent = shard ^ stride, sent_ref[shard]
            here, there = kept[shard] - sent, numbers[partner]
            there_late = there - kept[partner]

            def one(i):
                old = spot(back, shard, here + i)

                @pl.when(shard == me)
                def _():
                    send_ref[send_at + i] = source_ref[old]

                if level == 0:
                    new = spot(back, partner, there + i)
                    place_ref[new] = place_ref[old]
                    source_ref[new] = so_far + i
                else:
                    new = late_spot(back, partner, there_late + i)
                    late_place_ref[new] = place_ref[old]
                    late_source_ref[new] = so_far + i

            times(sent, one)

        def settle(shard):
            got = sent_ref[shard ^ stride]
            numbers[shard] = numbers[shard] - sent_ref[shard] + got
            kept[shard] = kept[shard] - sent_ref[shard] + (got if level == 0 else 0)

        for work in (decide, hand_over, settle):
            times(shards, work)

    def lay_out(shard):
        front, back = fronts[shard], backs[shard]
        front_count_ref[shard] = front
        length_ref[shard] = front + back

        def copy(count, places, sources, at, start):
            def one(i):
                code_ref[shard * total + start + i] = places[at + i]

                @pl.when(shard == me)
                def _():
                    order_ref[start + i] = sources[at + i]

            times(count, one)

        for back, start, number, kept in ((0, 0, front, kept_fronts[shard]), (1, front, back, kept_backs[shard])):
            copy(kept, place_ref, source_ref, spot(back, shard, 0), start)
            copy(number - kept, late_place_ref, late_source_ref, late_spot(back, shard, 0), start + kept)

    def clear(ref):
        def one(i):
            ref[i] = 0

        times(ref.shape[0], one)

    clear(order_ref)
    clear(send_ref)
    times(shards, build)
    so_far, send_at = capacity, 0
    for level, (stride, most_front, most_back) in enumerate(levels):
        for back, most in ((0, most_front), (1, most_back)):
            if most:
                even(level, back, stride, most, so_far, send_at)
            so_far, send_at = so_far + most, send_at + most
    times(shards, lay_out)


def laid_out(levels, capacity, total, index, own, count, left, blk):
    shards, slots = index.shape
    smem = pl.BlockSpec(memory_space=pltpu.SMEM)
    sizes = [shards * total, shards, shards, total, sum(front + back for _, front, back in levels)]
    late_room = max(sum(front + back for _, front, back in levels[1:]), 1)
    scratch = [2 * shards * capacity] * 2 + [2 * shards * late_room] * 2 + [shards] * 5
    return pl.pallas_call(
        functools.partial(layout_kernel, levels, capacity),
        out_shape=[jax.ShapeDtypeStruct((size,), jnp.int32) for size in sizes],
        in_specs=[smem] * 5,
        out_specs=[smem] * 5,
        scratch_shapes=[pltpu.SMEM((size,), jnp.int32) for size in scratch],
        cost_estimate=pl.CostEstimate(flops=0, bytes_accessed=16 * shards * slots, transcendentals=0),
    )(index.reshape(-1), own.reshape(-1), count, left, blk.reshape(1))


def on_device(
    tokens,
    ln_gain,
    ln_bias,
    fc1_tiles,
    fc1_index,
    fc1_count,
    fc1_bias,
    fc2_tiles,
    fc2_index,
    fc2_count,
    fc2_bias,
    ffn_size,
):
    side = fc1_tiles.shape[-1]
    slots = fc1_tiles.shape[2]
    shards = lax.axis_size("blk")
    token_rows, width = tokens.shape
    first_blocks = fc1_bias.shape[0] // side
    second_blocks = width // side
    share = width // ffn_size
    blk, ffn = lax.axis_index("blk"), lax.axis_index("ffn")
    aligned = share % side == 0
    opening = slots * 7 // 11
    rest = slots - opening
    held = slots + slots // 14
    late_from = held - slots * 8 // 25
    levels = [
        (stride, slots // most, max(slots // least, 1))
        for stride, most, least in ((1, 4, 5), (2, 14, 16), (4, 25, 16), (8, 50, 16))
        if shards % (2 * stride) == 0
    ]
    slot_ids = jnp.arange(slots, dtype=jnp.int32)

    def gathered(value):
        return lax.all_gather(value, "blk", axis=0, tiled=True).reshape(shards, -1, side, side)

    tiles1 = gathered(fc1_tiles[0, 0, :opening])
    meta = jnp.concatenate([fc1_index[:, 0], fc2_index[:, 0], fc1_count, fc2_count], axis=1)
    meta = lax.all_gather(meta, "blk", axis=0, tiled=True)
    index1, index2 = meta[:, :slots], meta[:, slots : 2 * slots]
    count1, count2 = meta[:, 2 * slots], meta[:, 2 * slots + 1]
    left1 = jnp.maximum(count1 - opening, 0)

    def in_own_share(index):
        if not aligned:
            return jnp.zeros(index.shape, jnp.bool_)
        return index % second_blocks // (share // side) == ffn

    capacity = rest + slots
    total_ids = jnp.arange(2 * capacity + slots // 4, dtype=jnp.int32)
    codes, fronts, lengths, order, sends = laid_out(
        levels, capacity, total_ids.shape[0], index2, in_own_share(index2).astype(jnp.int32), count2, left1, blk
    )
    codes = codes.reshape(shards, -1)
    sources = jnp.concatenate([fc1_tiles[0, 0, opening:], fc2_tiles[0, 0]], axis=0)
    arrived = []
    for level, (stride, most_front, most_back) in enumerate(levels):
        sending, sends = sends[: most_front + most_back], sends[most_front + most_back :]
        arrived.append(
            lax.ppermute(
                jnp.take(sources, sending, axis=0, mode="clip"),
                "blk",
                [(i, i ^ stride) for i in range(shards)],
            )
        )
        if level == 0:
            sources = jnp.concatenate([sources, arrived.pop()], axis=0)
    sources = jnp.concatenate([sources, *arrived], axis=0)

    tiles2a = gathered(jnp.take(sources, order[:late_from], axis=0, mode="clip"))
    tiles2b = gathered(jnp.take(sources, order[late_from:held], axis=0, mode="clip"))
    misplaced = jnp.stack([jnp.max(fronts) - late_from, jnp.max(lengths) - held, jnp.max(lengths)])
    misplaced = lax.pmax(misplaced, "ffn")

    rows_f = tokens.astype(jnp.float32)
    center = jnp.mean(rows_f, axis=1, keepdims=True)
    spread = jnp.mean((rows_f - center) ** 2, axis=1, keepdims=True)
    normed = ((rows_f - center) / jnp.sqrt(spread + 1e-05) * ln_gain + ln_bias).astype(jnp.bfloat16)
    normed_blocks = normed.reshape(token_rows, second_blocks, side).transpose(1, 0, 2)
    normed_blocks = jnp.pad(normed_blocks, ((0, 1), (0, 0), (0, 0)))
    normed_blocks, misplaced = lax.optimization_barrier((normed_blocks, misplaced))
    some_late = jnp.max(misplaced[:2]) > 0

    (total,) = tile_pass(
        first_kernel,
        index1[:, :opening] // first_blocks,
        index1[:, :opening] % first_blocks,
        slot_ids[:opening] < count1[:, None],
        ffn,
        normed_blocks,
        tiles1,
        [fc1_bias.reshape(first_blocks, 1, side)],
        [fixed((first_blocks, 1, side))],
        [jax.ShapeDtypeStruct((first_blocks, token_rows, side), jnp.float32)],
        first_blocks,
        scratch=False,
    )
    (hidden,) = tile_pass(
        hidden_kernel,
        index1[:, opening:] // first_blocks,
        index1[:, opening:] % first_blocks,
        slot_ids[opening:] < count1[:, None],
        ffn,
        normed_blocks,
        tiles2a,
        [total],
        [fixed(total.shape)],
        [jax.ShapeDtypeStruct((first_blocks + 1, token_rows, side), jnp.bfloat16)],
        first_blocks,
    )

    def second_pass(places, live, tiles, steps=2, group=4):
        return tile_pass(
            partial_kernel,
            places // second_blocks,
            places % second_blocks,
            live,
            ffn,
            hidden,
            tiles,
            [],
            [],
            [
                jax.ShapeDtypeStruct((second_blocks, token_rows, side), jnp.float32),
                jax.ShapeDtypeStruct((token_rows, width), jnp.bfloat16),
            ],
            second_blocks,
            steps=steps,
            group=group,
            scratch=False,
        )

    def own_cols(value):
        return lax.dynamic_slice_in_dim(value, ffn * share, share, 1).astype(jnp.float32)

    def from_others(partial_value):
        branch = jnp.zeros((token_rows, share), jnp.float32)
        for shift in range(1, ffn_size):
            to = lax.rem(ffn + shift, ffn_size)
            arrived = lax.ppermute(
                lax.dynamic_slice_in_dim(partial_value, to * share, share, 1),
                "ffn",
                [(i, (i + shift) % ffn_size) for i in range(ffn_size)],
            )
            branch = branch + arrived.astype(jnp.float32)
        return branch

    in_front = total_ids < fronts[:, None]
    in_second = (total_ids >= left1[:, None]) & (total_ids < lengths[:, None])
    total, partial_value = second_pass(codes[:, :late_from], in_second[:, :late_from], tiles2a)
    last_codes = codes[:, late_from:held]
    last_own = (in_second & ~in_front)[:, late_from:held]
    branch = from_others(partial_value)

    def with_late(branch):
        chunk = slots // 4
        start = jnp.where(misplaced[0] > 0, late_from, held)
        late = in_second & (in_front | (total_ids >= held))

        def one_more(number, branch):
            at = start + number * chunk
            here = jnp.take(sources, lax.dynamic_slice_in_dim(order, at, chunk), axis=0, mode="clip")
            part = [lax.dynamic_slice_in_dim(v, at, chunk, 1) for v in (codes, late)]
            _, extra = second_pass(*part, gathered(here), steps=1, group=1)
            return branch + from_others(extra) + own_cols(extra)

        return lax.fori_loop(0, (misplaced[2] - start + chunk - 1) // chunk, one_more, branch)

    if not aligned:
        branch = lax.cond(some_late, with_late, lambda branch: branch, branch)
        more, _ = second_pass(last_codes, last_own, tiles2b)
        own = (total + more).transpose(1, 0, 2).reshape(token_rows, width)
        return (own_cols(tokens) + own_cols(own) + branch + fc2_bias).astype(jnp.bfloat16)

    share_blocks = share // side
    last_rows, last_cols = last_codes // second_blocks, last_codes % second_blocks % share_blocks
    last_plan = planned(last_rows, last_cols, last_own, share_blocks, first_blocks, 2, 4)
    bias_row = fc2_bias.reshape(1, share)
    last_plan, branch, bias_row = lax.optimization_barrier((last_plan, branch, bias_row))
    last_pass = functools.partial(
        tile_pass,
        result_kernel,
        last_rows,
        last_cols,
        last_own,
        ffn,
        hidden,
        tiles2b,
        more_specs=[
            pl.BlockSpec(
                (share_blocks, token_rows, side),
                lambda i, fields, counts, at: (at[0], 0, 0),
                pipeline_mode=pl.Buffered(1),
            ),
            pl.BlockSpec(
                (token_rows, share),
                lambda i, fields, counts, at: (0, at[0]),
                pipeline_mode=pl.Buffered(1),
            ),
            fixed((token_rows, share)),
            fixed((1, share)),
        ],
        out_shapes=[jax.ShapeDtypeStruct((token_rows, share), jnp.bfloat16)],
        blocks=share_blocks,
        steps=2,
        group=4,
        vmem=LAST_VMEM_BYTES,
        plan=last_plan,
    )

    def finished(branch):
        return last_pass(more=[total, tokens, branch, bias_row])[0]

    return lax.cond(some_late, lambda branch: finished(with_late(branch)), finished, branch)


def solution(mesh):
    placed = (
        P("blk", None),
        P(),
        P(),
        P("blk", "ffn", None, None, None),
        P("blk", "ffn", None),
        P("blk", "ffn"),
        P("ffn"),
        P("blk", "ffn", None, None, None),
        P("blk", "ffn", None),
        P("blk", "ffn"),
        P("ffn"),
    )
    return jax.shard_map(
        functools.partial(on_device, ffn_size=mesh.shape["ffn"]),
        mesh=mesh,
        in_specs=placed,
        out_specs=P("blk", "ffn"),
        check_vma=False,
    )
```

```python
import functools

import jax
import jax.numpy as jnp
from jax import lax
from jax.experimental import pallas as pl
from jax.experimental.pallas import tpu as pltpu
from jax.sharding import PartitionSpec as P

UNROLL = 8
VMEM_BYTES = 56 * 1024 * 1024
LAST_VMEM_BYTES = 26 * 1024 * 1024


def group_kernel(group, size, zero_row, row_ref, col_ref, field_ref, count_ref, fill_ref, open_ref):
    step, steps = pl.program_id(0), pl.num_programs(0)
    listed = row_ref.shape[0] // steps

    def field(number, at):
        return (number * steps + step) * size + at

    def clear(at, carry):
        field_ref[field(0, at)] = 0
        for g in range(group):
            field_ref[field(1 + g, at)] = 0
            field_ref[field(1 + group + g, at)] = zero_row
        return carry

    def no_group(c, carry):
        fill_ref[c] = 0
        open_ref[c] = 0
        return carry

    def place(tile, groups):
        col = col_ref[step * listed + tile]
        held = jnp.maximum(col, 0)
        filled = fill_ref[held]
        opens = (col >= 0) & (filled == 0)
        at = jnp.where(opens, groups, open_ref[held])

        @pl.when(col >= 0)
        def _():
            open_ref[held] = at
            fill_ref[held] = jnp.where(filled == group - 1, 0, filled + 1)
            field_ref[field(0, at)] = col
            field_ref[field(1 + filled, at)] = tile
            field_ref[field(1 + group + filled, at)] = row_ref[step * listed + tile]

        return groups + opens.astype(jnp.int32)

    lax.fori_loop(0, size, clear, 0)
    lax.fori_loop(0, fill_ref.shape[0], no_group, 0)
    count_ref[step] = lax.fori_loop(0, listed, place, jnp.int32(0))


def group_up(rows, cols, live, blocks, zero_row, group):
    steps, listed = rows.shape
    most = (listed + (group - 1) * min(blocks, listed)) // group
    size = -(-most // UNROLL) * UNROLL
    smem = pl.BlockSpec(memory_space=pltpu.SMEM)
    return pl.pallas_call(
        functools.partial(group_kernel, group, size, zero_row),
        out_shape=[
            jax.ShapeDtypeStruct(((2 * group + 1) * steps * size,), jnp.int32),
            jax.ShapeDtypeStruct((steps,), jnp.int32),
        ],
        grid=(steps,),
        in_specs=[smem, smem],
        out_specs=[smem, smem],
        scratch_shapes=[pltpu.SMEM((blocks,), jnp.int32), pltpu.SMEM((blocks,), jnp.int32)],
        cost_estimate=pl.CostEstimate(flops=0, bytes_accessed=16 * steps * listed, transcendentals=0),
    )(rows.reshape(-1), jnp.where(live, cols, -1).reshape(-1))


def add_block(field_ref, count_ref, x_ref, w_ref, acc, group):
    step, steps = pl.program_id(0), pl.num_programs(0)
    w_ref = w_ref.reshape(-1, *w_ref.shape[2:])
    fields = 2 * group + 1
    size = field_ref.shape[0] // (fields * steps)

    def one(at):
        col, *parts = (field_ref[(f * steps + step) * size + at] for f in range(fields))
        left = jnp.concatenate([x_ref[row] for row in parts[group:]], axis=1)
        right = jnp.concatenate([w_ref[tile] for tile in parts[:group]], axis=0)
        acc[col] += jnp.dot(left, right, preferred_element_type=jnp.float32)

    def several(turn, carry):
        for u in range(UNROLL):
            one(turn * UNROLL + u)
        return carry

    whole = lax.div(count_ref[step], jnp.int32(UNROLL))
    done = whole * UNROLL

    def few(turn, carry):
        for u in range(UNROLL // 2):
            one(done + turn * (UNROLL // 2) + u)
        return carry

    left_over = count_ref[step] - done + UNROLL // 2 - 1
    lax.fori_loop(0, whole, several, 0)
    lax.fori_loop(0, lax.div(left_over, jnp.int32(UNROLL // 2)), few, 0)


def for_blocks(count, work):
    def turn(c, carry):
        work(c)
        return carry

    lax.fori_loop(0, count, turn, 0)


def columns(c, width):
    return pl.ds(pl.multiple_of(c * width, width), width)


def at_start(work):
    pl.when(pl.program_id(0) == 0)(work)


def at_end(work):
    pl.when(pl.program_id(0) == pl.num_programs(0) - 1)(work)


def first_kernel(group, field_ref, count_ref, at_ref, x_ref, w_ref, bias_ref, sum_ref):
    @at_start
    def _():
        def fill(c):
            sum_ref[c] = jnp.broadcast_to(bias_ref[c], sum_ref.shape[1:])

        for_blocks(sum_ref.shape[0], fill)

    add_block(field_ref, count_ref, x_ref, w_ref, sum_ref, group)


def hidden_kernel(group, field_ref, count_ref, at_ref, x_ref, w_ref, sum_ref, out_ref, acc):
    blocks = acc.shape[0]

    @at_start
    def _():
        def fill(c):
            acc[c] = sum_ref[c]

        for_blocks(blocks, fill)

    add_block(field_ref, count_ref, x_ref, w_ref, acc, group)

    @at_end
    def _():
        def finish(c):
            out_ref[c] = jnp.maximum(acc[c], 0.0).astype(out_ref.dtype)

        for_blocks(blocks, finish)
        out_ref[blocks] = jnp.zeros(out_ref.shape[1:], out_ref.dtype)


def partial_kernel(group, field_ref, count_ref, at_ref, x_ref, w_ref, sum_ref, out_ref):
    blocks, width = sum_ref.shape[0], sum_ref.shape[2]

    @at_start
    def _():
        def fill(c):
            sum_ref[c] = jnp.zeros(sum_ref.shape[1:], sum_ref.dtype)

        for_blocks(blocks, fill)

    add_block(field_ref, count_ref, x_ref, w_ref, sum_ref, group)

    @at_end
    def _():
        def finish(c):
            out_ref[:, columns(c, width)] = sum_ref[c].astype(out_ref.dtype)

        for_blocks(blocks, finish)


def result_kernel(
    group, field_ref, count_ref, at_ref,
    x_ref, w_ref, sum_ref, token_ref, other_ref, bias_ref, out_ref, acc,
):
    blocks, width = acc.shape[0], acc.shape[2]
    part = token_ref.shape[0]
    rows = pl.ds(pl.multiple_of(pl.program_id(0) * part, part), part)

    @at_start
    def _():
        def fill(c):
            acc[c] = jnp.zeros(acc.shape[1:], acc.dtype)

        for_blocks(blocks, fill)

    def add_rows(c):
        cols = columns(c, width)
        value = token_ref[:, cols].astype(jnp.float32) + (sum_ref[c] + other_ref[:, cols])
        acc[c, rows] += value + bias_ref[:, cols]

    for_blocks(blocks, add_rows)
    add_block(field_ref, count_ref, x_ref, w_ref, acc, group)

    @at_end
    def _():
        def finish(c):
            out_ref[:, columns(c, width)] = acc[c].astype(out_ref.dtype)

        for_blocks(blocks, finish)


def fixed(shape):
    return pl.BlockSpec(shape, lambda i, *_: (0,) * len(shape), pipeline_mode=pl.Buffered(1))


def planned(rows, cols, live, blocks, zero_row, steps, group):
    steps = steps if rows.shape[0] % steps == 0 else 1
    return group_up(*(v.reshape(steps, -1) for v in (rows, cols, live)), blocks, zero_row, group)


def tile_pass(
    kernel, rows, cols, live, at, x, tiles, more, more_specs, out_shapes, blocks,
    steps=4, group=2, scratch=True, vmem=VMEM_BYTES, plan=None,
):
    shards, slots = rows.shape
    side, tokens = tiles.shape[-1], x.shape[1]
    steps = steps if shards % steps == 0 else 1
    if plan is None:
        plan = planned(rows, cols, live, blocks, x.shape[0] - 1, steps, group)
    fields, counts = plan
    return pl.pallas_call(
        functools.partial(kernel, group),
        out_shape=out_shapes,
        grid_spec=pltpu.PrefetchScalarGridSpec(
            num_scalar_prefetch=3,
            grid=(steps,),
            in_specs=[
                fixed(x.shape),
                pl.BlockSpec((shards // steps, slots, side, side), lambda i, *_: (i, 0, 0, 0)),
                *more_specs,
            ],
            out_specs=[
                pl.BlockSpec(o.shape, lambda i, *_, rank=len(o.shape): (0,) * rank) for o in out_shapes
            ],
            scratch_shapes=[pltpu.VMEM((blocks, tokens, side), jnp.float32)] if scratch else [],
        ),
        compiler_params=pltpu.CompilerParams(vmem_limit_bytes=vmem),
        cost_estimate=pl.CostEstimate(
            flops=4 * shards * slots * tokens * side * side,
            bytes_accessed=shards * slots * side * side * 2,
            transcendentals=0,
        ),
    )(fields, counts, at.reshape(1), x, tiles, *more)


def layout_kernel(
    levels, capacity, index_ref, own_ref, count_ref, left_ref, at_ref,
    code_ref, front_count_ref, length_ref, order_ref, send_ref,
    place_ref, source_ref, late_place_ref, late_source_ref, fronts, backs, kept_fronts, kept_backs, sent_ref,
):
    late_room = late_place_ref.shape[0] // (2 * count_ref.shape[0])
    shards = count_ref.shape[0]
    slots = index_ref.shape[0] // shards
    total = order_ref.shape[0]
    me = at_ref[0]

    def times(count, work):
        def turn(i, carry):
            work(i)
            return carry

        lax.fori_loop(0, count, turn, 0)

    def spot(back, shard, i):
        return (back * shards + shard) * capacity + i

    def build(shard):
        left = left_ref[shard]

        def first(i):
            place_ref[spot(0, shard, i)] = 0
            source_ref[spot(0, shard, i)] = i

        def second(slot, carry):
            front, back = carry
            own = own_ref[shard * slots + slot]
            at = spot(own, shard, jnp.where(own == 1, back, front))
            place_ref[at] = index_ref[shard * slots + slot]
            source_ref[at] = capacity - slots + slot
            return front + 1 - own, back + own

        times(left, first)
        front, back = lax.fori_loop(0, count_ref[shard], second, (left, jnp.int32(0)))
        fronts[shard], backs[shard] = front, back
        kept_fronts[shard], kept_backs[shard] = front, back

    def late_spot(back, shard, i):
        return (back * shards + shard) * late_room + i

    def even(level, back, stride, most, so_far, send_at):
        numbers, kept = (backs, kept_backs) if back else (fronts, kept_fronts)

        def weight(shard):
            return fronts[shard] + backs[shard] if back else fronts[shard]

        def decide(shard):
            partner = shard ^ stride
            excess = lax.div(jnp.maximum(weight(shard) - weight(partner), 0), jnp.int32(2))
            spare = kept[shard] if back else kept[shard] - left_ref[shard]
            room = jnp.minimum(most, capacity - numbers[partner])
            sent_ref[shard] = jnp.minimum(excess, jnp.minimum(room, spare))

        def hand_over(shard):
            partner, sent = shard ^ stride, sent_ref[shard]
            here, there = kept[shard] - sent, numbers[partner]
            there_late = there - kept[partner]

            def one(i):
                old = spot(back, shard, here + i)

                @pl.when(shard == me)
                def _():
                    send_ref[send_at + i] = source_ref[old]

                if level == 0:
                    new = spot(back, partner, there + i)
                    place_ref[new] = place_ref[old]
                    source_ref[new] = so_far + i
                else:
                    new = late_spot(back, partner, there_late + i)
                    late_place_ref[new] = place_ref[old]
                    late_source_ref[new] = so_far + i

            times(sent, one)

        def settle(shard):
            got = sent_ref[shard ^ stride]
            numbers[shard] = numbers[shard] - sent_ref[shard] + got
            kept[shard] = kept[shard] - sent_ref[shard] + (got if level == 0 else 0)

        for work in (decide, hand_over, settle):
            times(shards, work)

    def lay_out(shard):
        front, back = fronts[shard], backs[shard]
        front_count_ref[shard] = front
        length_ref[shard] = front + back

        def copy(count, places, sources, at, start):
            def one(i):
                code_ref[shard * total + start + i] = places[at + i]

                @pl.when(shard == me)
                def _():
                    order_ref[start + i] = sources[at + i]

            times(count, one)

        for back, start, number, kept in ((0, 0, front, kept_fronts[shard]), (1, front, back, kept_backs[shard])):
            copy(kept, place_ref, source_ref, spot(back, shard, 0), start)
            copy(number - kept, late_place_ref, late_source_ref, late_spot(back, shard, 0), start + kept)

    def clear(ref):
        def one(i):
            ref[i] = 0

        times(ref.shape[0], one)

    clear(order_ref)
    clear(send_ref)
    times(shards, build)
    so_far, send_at = capacity, 0
    for level, (stride, most_front, most_back) in enumerate(levels):
        for back, most in ((0, most_front), (1, most_back)):
            if most:
                even(level, back, stride, most, so_far, send_at)
            so_far, send_at = so_far + most, send_at + most
    times(shards, lay_out)


def laid_out(levels, capacity, total, index, own, count, left, blk):
    shards, slots = index.shape
    smem = pl.BlockSpec(memory_space=pltpu.SMEM)
    sizes = [shards * total, shards, shards, total, sum(front + back for _, front, back in levels)]
    late_room = max(sum(front + back for _, front, back in levels[1:]), 1)
    scratch = [2 * shards * capacity] * 2 + [2 * shards * late_room] * 2 + [shards] * 5
    return pl.pallas_call(
        functools.partial(layout_kernel, levels, capacity),
        out_shape=[jax.ShapeDtypeStruct((size,), jnp.int32) for size in sizes],
        in_specs=[smem] * 5,
        out_specs=[smem] * 5,
        scratch_shapes=[pltpu.SMEM((size,), jnp.int32) for size in scratch],
        cost_estimate=pl.CostEstimate(flops=0, bytes_accessed=16 * shards * slots, transcendentals=0),
    )(index.reshape(-1), own.reshape(-1), count, left, blk.reshape(1))


def on_device(
    tokens,
    ln_gain,
    ln_bias,
    fc1_tiles,
    fc1_index,
    fc1_count,
    fc1_bias,
    fc2_tiles,
    fc2_index,
    fc2_count,
    fc2_bias,
    ffn_size,
):
    side = fc1_tiles.shape[-1]
    slots = fc1_tiles.shape[2]
    shards = lax.axis_size("blk")
    token_rows, width = tokens.shape
    first_blocks = fc1_bias.shape[0] // side
    second_blocks = width // side
    share = width // ffn_size
    blk, ffn = lax.axis_index("blk"), lax.axis_index("ffn")
    aligned = share % side == 0
    opening = slots * 7 // 11
    rest = slots - opening
    held = slots + slots // 14
    late_from = held - slots // 3
    levels = [
        (stride, slots // most, max(slots // least, 1))
        for stride, most, least in ((1, 4, 5), (2, 14, 16), (4, 25, 16), (8, 50, 16))
        if shards % (2 * stride) == 0
    ]
    slot_ids = jnp.arange(slots, dtype=jnp.int32)

    def gathered(value):
        return lax.all_gather(value, "blk", axis=0, tiled=True).reshape(shards, -1, side, side)

    tiles1 = gathered(fc1_tiles[0, 0, :opening])
    meta = jnp.concatenate([fc1_index[:, 0], fc2_index[:, 0], fc1_count, fc2_count], axis=1)
    meta = lax.all_gather(meta, "blk", axis=0, tiled=True)
    index1, index2 = meta[:, :slots], meta[:, slots : 2 * slots]
    count1, count2 = meta[:, 2 * slots], meta[:, 2 * slots + 1]
    left1 = jnp.maximum(count1 - opening, 0)

    def in_own_share(index):
        if not aligned:
            return jnp.zeros(index.shape, jnp.bool_)
        return index % second_blocks // (share // side) == ffn

    capacity = rest + slots
    total_ids = jnp.arange(2 * capacity + slots // 4, dtype=jnp.int32)
    codes, fronts, lengths, order, sends = laid_out(
        levels, capacity, total_ids.shape[0], index2, in_own_share(index2).astype(jnp.int32), count2, left1, blk
    )
    codes = codes.reshape(shards, -1)
    sources = jnp.concatenate([fc1_tiles[0, 0, opening:], fc2_tiles[0, 0]], axis=0)
    arrived = []
    for level, (stride, most_front, most_back) in enumerate(levels):
        sending, sends = sends[: most_front + most_back], sends[most_front + most_back :]
        arrived.append(
            lax.ppermute(
                jnp.take(sources, sending, axis=0, mode="clip"),
                "blk",
                [(i, i ^ stride) for i in range(shards)],
            )
        )
        if level == 0:
            sources = jnp.concatenate([sources, arrived.pop()], axis=0)
    sources = jnp.concatenate([sources, *arrived], axis=0)

    tiles2a = gathered(jnp.take(sources, order[:late_from], axis=0, mode="clip"))
    tiles2b = gathered(jnp.take(sources, order[late_from:held], axis=0, mode="clip"))
    misplaced = jnp.stack([jnp.max(fronts) - late_from, jnp.max(lengths) - held, jnp.max(lengths)])
    misplaced = lax.pmax(misplaced, "ffn")

    rows_f = tokens.astype(jnp.float32)
    center = jnp.mean(rows_f, axis=1, keepdims=True)
    spread = jnp.mean((rows_f - center) ** 2, axis=1, keepdims=True)
    normed = ((rows_f - center) / jnp.sqrt(spread + 1e-05) * ln_gain + ln_bias).astype(jnp.bfloat16)
    normed_blocks = normed.reshape(token_rows, second_blocks, side).transpose(1, 0, 2)
    normed_blocks = jnp.pad(normed_blocks, ((0, 1), (0, 0), (0, 0)))
    normed_blocks, misplaced = lax.optimization_barrier((normed_blocks, misplaced))
    some_late = jnp.max(misplaced[:2]) > 0

    (total,) = tile_pass(
        first_kernel,
        index1[:, :opening] // first_blocks,
        index1[:, :opening] % first_blocks,
        slot_ids[:opening] < count1[:, None],
        ffn,
        normed_blocks,
        tiles1,
        [fc1_bias.reshape(first_blocks, 1, side)],
        [fixed((first_blocks, 1, side))],
        [jax.ShapeDtypeStruct((first_blocks, token_rows, side), jnp.float32)],
        first_blocks,
        scratch=False,
    )
    (hidden,) = tile_pass(
        hidden_kernel,
        index1[:, opening:] // first_blocks,
        index1[:, opening:] % first_blocks,
        slot_ids[opening:] < count1[:, None],
        ffn,
        normed_blocks,
        tiles2a,
        [total],
        [fixed(total.shape)],
        [jax.ShapeDtypeStruct((first_blocks + 1, token_rows, side), jnp.bfloat16)],
        first_blocks,
    )

    def second_pass(places, live, tiles, steps=2, group=4):
        return tile_pass(
            partial_kernel,
            places // second_blocks,
            places % second_blocks,
            live,
            ffn,
            hidden,
            tiles,
            [],
            [],
            [
                jax.ShapeDtypeStruct((second_blocks, token_rows, side), jnp.float32),
                jax.ShapeDtypeStruct((token_rows, width), jnp.bfloat16),
            ],
            second_blocks,
            steps=steps,
            group=group,
            scratch=False,
        )

    def own_cols(value):
        return lax.dynamic_slice_in_dim(value, ffn * share, share, 1).astype(jnp.float32)

    def from_others(partial_value):
        branch = jnp.zeros((token_rows, share), jnp.float32)
        for shift in range(1, ffn_size):
            to = lax.rem(ffn + shift, ffn_size)
            arrived = lax.ppermute(
                lax.dynamic_slice_in_dim(partial_value, to * share, share, 1),
                "ffn",
                [(i, (i + shift) % ffn_size) for i in range(ffn_size)],
            )
            branch = branch + arrived.astype(jnp.float32)
        return branch

    in_front = total_ids < fronts[:, None]
    in_second = (total_ids >= left1[:, None]) & (total_ids < lengths[:, None])
    total, partial_value = second_pass(codes[:, :late_from], in_second[:, :late_from], tiles2a)
    last_codes = codes[:, late_from:held]
    last_own = (in_second & ~in_front)[:, late_from:held]
    branch = from_others(partial_value)

    def with_late(branch):
        chunk = slots // 4
        start = jnp.where(misplaced[0] > 0, late_from, held)
        late = in_second & (in_front | (total_ids >= held))

        def one_more(number, branch):
            at = start + number * chunk
            here = jnp.take(sources, lax.dynamic_slice_in_dim(order, at, chunk), axis=0, mode="clip")
            part = [lax.dynamic_slice_in_dim(v, at, chunk, 1) for v in (codes, late)]
            _, extra = second_pass(*part, gathered(here), steps=1, group=1)
            return branch + from_others(extra) + own_cols(extra)

        return lax.fori_loop(0, (misplaced[2] - start + chunk - 1) // chunk, one_more, branch)

    if not aligned:
        branch = lax.cond(some_late, with_late, lambda branch: branch, branch)
        more, _ = second_pass(last_codes, last_own, tiles2b)
        own = (total + more).transpose(1, 0, 2).reshape(token_rows, width)
        return (own_cols(tokens) + own_cols(own) + branch + fc2_bias).astype(jnp.bfloat16)

    share_blocks = share // side
    last_rows, last_cols = last_codes // second_blocks, last_codes % second_blocks % share_blocks
    last_steps = 4 if shards % 4 == 0 and token_rows % 64 == 0 else 1
    last_part = token_rows // last_steps
    last_plan = planned(last_rows, last_cols, last_own, share_blocks, first_blocks, last_steps, 4)
    bias_row = fc2_bias.reshape(1, share)
    last_plan, branch, bias_row = lax.optimization_barrier((last_plan, branch, bias_row))
    last_pass = functools.partial(
        tile_pass,
        result_kernel,
        last_rows,
        last_cols,
        last_own,
        ffn,
        hidden,
        tiles2b,
        more_specs=[
            pl.BlockSpec((share_blocks, last_part, side), lambda i, fields, counts, at: (at[0], i, 0)),
            pl.BlockSpec((last_part, share), lambda i, fields, counts, at: (i, at[0])),
            pl.BlockSpec((last_part, share), lambda i, *_: (i, 0)),
            fixed((1, share)),
        ],
        out_shapes=[jax.ShapeDtypeStruct((token_rows, share), jnp.bfloat16)],
        blocks=share_blocks,
        steps=last_steps,
        group=4,
        vmem=LAST_VMEM_BYTES,
        plan=last_plan,
    )

    def finished(branch):
        return last_pass(more=[total, tokens, branch, bias_row])[0]

    return lax.cond(some_late, lambda branch: finished(with_late(branch)), finished, branch)


def solution(mesh):
    placed = (
        P("blk", None),
        P(),
        P(),
        P("blk", "ffn", None, None, None),
        P("blk", "ffn", None),
        P("blk", "ffn"),
        P("ffn"),
        P("blk", "ffn", None, None, None),
        P("blk", "ffn", None),
        P("blk", "ffn"),
        P("ffn"),
    )
    return jax.shard_map(
        functools.partial(on_device, ffn_size=mesh.shape["ffn"]),
        mesh=mesh,
        in_specs=placed,
        out_specs=P("blk", "ffn"),
        check_vma=False,
    )
```

```python
import functools

import jax
import jax.numpy as jnp
from jax import lax
from jax.experimental import pallas as pl
from jax.experimental.pallas import tpu as pltpu
from jax.sharding import PartitionSpec as P

UNROLL = 8
VMEM_BYTES = 56 * 1024 * 1024
LAST_VMEM_BYTES = 26 * 1024 * 1024


def group_kernel(group, size, zero_row, row_ref, col_ref, field_ref, count_ref, fill_ref, open_ref):
    step, steps = pl.program_id(0), pl.num_programs(0)
    listed = row_ref.shape[0] // steps

    def field(number, at):
        return (number * steps + step) * size + at

    def clear(at, carry):
        field_ref[field(0, at)] = 0
        for g in range(group):
            field_ref[field(1 + g, at)] = 0
            field_ref[field(1 + group + g, at)] = zero_row
        return carry

    def no_group(c, carry):
        fill_ref[c] = 0
        open_ref[c] = 0
        return carry

    def place(tile, groups):
        col = col_ref[step * listed + tile]
        held = jnp.maximum(col, 0)
        filled = fill_ref[held]
        opens = (col >= 0) & (filled == 0)
        at = jnp.where(opens, groups, open_ref[held])

        @pl.when(col >= 0)
        def _():
            open_ref[held] = at
            fill_ref[held] = jnp.where(filled == group - 1, 0, filled + 1)
            field_ref[field(0, at)] = col
            field_ref[field(1 + filled, at)] = tile
            field_ref[field(1 + group + filled, at)] = row_ref[step * listed + tile]

        return groups + opens.astype(jnp.int32)

    lax.fori_loop(0, size, clear, 0)
    lax.fori_loop(0, fill_ref.shape[0], no_group, 0)
    count_ref[step] = lax.fori_loop(0, listed, place, jnp.int32(0))


def group_up(rows, cols, live, blocks, zero_row, group):
    steps, listed = rows.shape
    most = (listed + (group - 1) * min(blocks, listed)) // group
    size = -(-most // UNROLL) * UNROLL
    smem = pl.BlockSpec(memory_space=pltpu.SMEM)
    return pl.pallas_call(
        functools.partial(group_kernel, group, size, zero_row),
        out_shape=[
            jax.ShapeDtypeStruct(((2 * group + 1) * steps * size,), jnp.int32),
            jax.ShapeDtypeStruct((steps,), jnp.int32),
        ],
        grid=(steps,),
        in_specs=[smem, smem],
        out_specs=[smem, smem],
        scratch_shapes=[pltpu.SMEM((blocks,), jnp.int32), pltpu.SMEM((blocks,), jnp.int32)],
        cost_estimate=pl.CostEstimate(flops=0, bytes_accessed=16 * steps * listed, transcendentals=0),
    )(rows.reshape(-1), jnp.where(live, cols, -1).reshape(-1))


def add_block(field_ref, count_ref, x_ref, w_ref, acc, group):
    step, steps = pl.program_id(0), pl.num_programs(0)
    w_ref = w_ref.reshape(-1, *w_ref.shape[2:])
    fields = 2 * group + 1
    size = field_ref.shape[0] // (fields * steps)

    def one(at):
        col, *parts = (field_ref[(f * steps + step) * size + at] for f in range(fields))
        left = jnp.concatenate([x_ref[row] for row in parts[group:]], axis=1)
        right = jnp.concatenate([w_ref[tile] for tile in parts[:group]], axis=0)
        acc[col] += jnp.dot(left, right, preferred_element_type=jnp.float32)

    def several(turn, carry):
        for u in range(UNROLL):
            one(turn * UNROLL + u)
        return carry

    whole = lax.div(count_ref[step], jnp.int32(UNROLL))
    done = whole * UNROLL

    def few(turn, carry):
        for u in range(UNROLL // 2):
            one(done + turn * (UNROLL // 2) + u)
        return carry

    left_over = count_ref[step] - done + UNROLL // 2 - 1
    lax.fori_loop(0, whole, several, 0)
    lax.fori_loop(0, lax.div(left_over, jnp.int32(UNROLL // 2)), few, 0)


def for_blocks(count, work):
    def turn(c, carry):
        work(c)
        return carry

    lax.fori_loop(0, count, turn, 0)


def columns(c, width):
    return pl.ds(pl.multiple_of(c * width, width), width)


def at_start(work):
    pl.when(pl.program_id(0) == 0)(work)


def at_end(work):
    pl.when(pl.program_id(0) == pl.num_programs(0) - 1)(work)


def first_kernel(group, field_ref, count_ref, at_ref, x_ref, w_ref, bias_ref, sum_ref):
    @at_start
    def _():
        def fill(c):
            sum_ref[c] = jnp.broadcast_to(bias_ref[c], sum_ref.shape[1:])

        for_blocks(sum_ref.shape[0], fill)

    add_block(field_ref, count_ref, x_ref, w_ref, sum_ref, group)


def hidden_kernel(group, field_ref, count_ref, at_ref, x_ref, w_ref, sum_ref, out_ref, acc):
    blocks = acc.shape[0]

    @at_start
    def _():
        def fill(c):
            acc[c] = sum_ref[c]

        for_blocks(blocks, fill)

    add_block(field_ref, count_ref, x_ref, w_ref, acc, group)

    @at_end
    def _():
        def finish(c):
            out_ref[c] = jnp.maximum(acc[c], 0.0).astype(out_ref.dtype)

        for_blocks(blocks, finish)
        out_ref[blocks] = jnp.zeros(out_ref.shape[1:], out_ref.dtype)


def partial_kernel(group, field_ref, count_ref, at_ref, x_ref, w_ref, sum_ref, out_ref):
    blocks, width = sum_ref.shape[0], sum_ref.shape[2]

    @at_start
    def _():
        def fill(c):
            sum_ref[c] = jnp.zeros(sum_ref.shape[1:], sum_ref.dtype)

        for_blocks(blocks, fill)

    add_block(field_ref, count_ref, x_ref, w_ref, sum_ref, group)

    @at_end
    def _():
        def finish(c):
            out_ref[:, columns(c, width)] = sum_ref[c].astype(out_ref.dtype)

        for_blocks(blocks, finish)


def result_kernel(
    group, field_ref, count_ref, at_ref,
    x_ref, w_ref, sum_ref, token_ref, other_ref, bias_ref, out_ref, acc,
):
    blocks, width = acc.shape[0], acc.shape[2]
    part = token_ref.shape[0]
    rows = pl.ds(pl.multiple_of(pl.program_id(0) * part, part), part)

    @at_start
    def _():
        def fill(c):
            acc[c] = jnp.zeros(acc.shape[1:], acc.dtype)

        for_blocks(blocks, fill)

    def add_rows(c):
        cols = columns(c, width)
        value = token_ref[:, cols].astype(jnp.float32) + (sum_ref[c] + other_ref[:, cols])
        acc[c, rows] += value + bias_ref[:, cols]

    for_blocks(blocks, add_rows)
    add_block(field_ref, count_ref, x_ref, w_ref, acc, group)

    @at_end
    def _():
        def finish(c):
            out_ref[:, columns(c, width)] = acc[c].astype(out_ref.dtype)

        for_blocks(blocks, finish)


def fixed(shape):
    return pl.BlockSpec(shape, lambda i, *_: (0,) * len(shape), pipeline_mode=pl.Buffered(1))


def planned(rows, cols, live, blocks, zero_row, steps, group):
    steps = steps if rows.shape[0] % steps == 0 else 1
    return group_up(*(v.reshape(steps, -1) for v in (rows, cols, live)), blocks, zero_row, group)


def tile_pass(
    kernel, rows, cols, live, at, x, tiles, more, more_specs, out_shapes, blocks,
    steps=4, group=2, scratch=True, vmem=VMEM_BYTES, plan=None,
):
    shards, slots = rows.shape
    side, tokens = tiles.shape[-1], x.shape[1]
    steps = steps if shards % steps == 0 else 1
    if plan is None:
        plan = planned(rows, cols, live, blocks, x.shape[0] - 1, steps, group)
    fields, counts = plan
    return pl.pallas_call(
        functools.partial(kernel, group),
        out_shape=out_shapes,
        grid_spec=pltpu.PrefetchScalarGridSpec(
            num_scalar_prefetch=3,
            grid=(steps,),
            in_specs=[
                fixed(x.shape),
                pl.BlockSpec((shards // steps, slots, side, side), lambda i, *_: (i, 0, 0, 0)),
                *more_specs,
            ],
            out_specs=[
                pl.BlockSpec(o.shape, lambda i, *_, rank=len(o.shape): (0,) * rank) for o in out_shapes
            ],
            scratch_shapes=[pltpu.VMEM((blocks, tokens, side), jnp.float32)] if scratch else [],
        ),
        compiler_params=pltpu.CompilerParams(vmem_limit_bytes=vmem),
        cost_estimate=pl.CostEstimate(
            flops=4 * shards * slots * tokens * side * side,
            bytes_accessed=shards * slots * side * side * 2,
            transcendentals=0,
        ),
    )(fields, counts, at.reshape(1), x, tiles, *more)


def layout_kernel(
    levels, capacity, index_ref, own_ref, count_ref, left_ref, at_ref,
    code_ref, front_count_ref, length_ref, order_ref, send_ref,
    place_ref, source_ref, late_place_ref, late_source_ref, fronts, backs, kept_fronts, kept_backs, sent_ref,
):
    late_room = late_place_ref.shape[0] // (2 * count_ref.shape[0])
    shards = count_ref.shape[0]
    slots = index_ref.shape[0] // shards
    total = order_ref.shape[0]
    me = at_ref[0]

    def times(count, work):
        def turn(i, carry):
            work(i)
            return carry

        lax.fori_loop(0, count, turn, 0)

    def spot(back, shard, i):
        return (back * shards + shard) * capacity + i

    def build(shard):
        left = left_ref[shard]

        def first(i):
            place_ref[spot(0, shard, i)] = 0
            source_ref[spot(0, shard, i)] = i

        def second(slot, carry):
            front, back = carry
            own = own_ref[shard * slots + slot]
            at = spot(own, shard, jnp.where(own == 1, back, front))
            place_ref[at] = index_ref[shard * slots + slot]
            source_ref[at] = capacity - slots + slot
            return front + 1 - own, back + own

        times(left, first)
        front, back = lax.fori_loop(0, count_ref[shard], second, (left, jnp.int32(0)))
        fronts[shard], backs[shard] = front, back
        kept_fronts[shard], kept_backs[shard] = front, back

    def late_spot(back, shard, i):
        return (back * shards + shard) * late_room + i

    def even(level, back, stride, most, so_far, send_at):
        numbers, kept = (backs, kept_backs) if back else (fronts, kept_fronts)

        def weight(shard):
            return fronts[shard] + backs[shard] if back else fronts[shard]

        def decide(shard):
            partner = shard ^ stride
            excess = lax.div(jnp.maximum(weight(shard) - weight(partner), 0), jnp.int32(2))
            spare = kept[shard] if back else kept[shard] - left_ref[shard]
            room = jnp.minimum(most, capacity - numbers[partner])
            sent_ref[shard] = jnp.minimum(excess, jnp.minimum(room, spare))

        def hand_over(shard):
            partner, sent = shard ^ stride, sent_ref[shard]
            here, there = kept[shard] - sent, numbers[partner]
            there_late = there - kept[partner]

            def one(i):
                old = spot(back, shard, here + i)

                @pl.when(shard == me)
                def _():
                    send_ref[send_at + i] = source_ref[old]

                if level == 0:
                    new = spot(back, partner, there + i)
                    place_ref[new] = place_ref[old]
                    source_ref[new] = so_far + i
                else:
                    new = late_spot(back, partner, there_late + i)
                    late_place_ref[new] = place_ref[old]
                    late_source_ref[new] = so_far + i

            times(sent, one)

        def settle(shard):
            got = sent_ref[shard ^ stride]
            numbers[shard] = numbers[shard] - sent_ref[shard] + got
            kept[shard] = kept[shard] - sent_ref[shard] + (got if level == 0 else 0)

        for work in (decide, hand_over, settle):
            times(shards, work)

    def lay_out(shard):
        front, back = fronts[shard], backs[shard]
        front_count_ref[shard] = front
        length_ref[shard] = front + back

        def copy(count, places, sources, at, start):
            def one(i):
                code_ref[shard * total + start + i] = places[at + i]

                @pl.when(shard == me)
                def _():
                    order_ref[start + i] = sources[at + i]

            times(count, one)

        for back, start, number, kept in ((0, 0, front, kept_fronts[shard]), (1, front, back, kept_backs[shard])):
            copy(kept, place_ref, source_ref, spot(back, shard, 0), start)
            copy(number - kept, late_place_ref, late_source_ref, late_spot(back, shard, 0), start + kept)

    def clear(ref):
        def one(i):
            ref[i] = 0

        times(ref.shape[0], one)

    clear(order_ref)
    clear(send_ref)
    times(shards, build)
    so_far, send_at = capacity, 0
    for level, (stride, most_front, most_back) in enumerate(levels):
        for back, most in ((0, most_front), (1, most_back)):
            if most:
                even(level, back, stride, most, so_far, send_at)
            so_far, send_at = so_far + most, send_at + most
    times(shards, lay_out)


def laid_out(levels, capacity, total, index, own, count, left, blk):
    shards, slots = index.shape
    smem = pl.BlockSpec(memory_space=pltpu.SMEM)
    sizes = [shards * total, shards, shards, total, sum(front + back for _, front, back in levels)]
    late_room = max(sum(front + back for _, front, back in levels[1:]), 1)
    scratch = [2 * shards * capacity] * 2 + [2 * shards * late_room] * 2 + [shards] * 5
    return pl.pallas_call(
        functools.partial(layout_kernel, levels, capacity),
        out_shape=[jax.ShapeDtypeStruct((size,), jnp.int32) for size in sizes],
        in_specs=[smem] * 5,
        out_specs=[smem] * 5,
        scratch_shapes=[pltpu.SMEM((size,), jnp.int32) for size in scratch],
        cost_estimate=pl.CostEstimate(flops=0, bytes_accessed=16 * shards * slots, transcendentals=0),
    )(index.reshape(-1), own.reshape(-1), count, left, blk.reshape(1))


def on_device(
    tokens,
    ln_gain,
    ln_bias,
    fc1_tiles,
    fc1_index,
    fc1_count,
    fc1_bias,
    fc2_tiles,
    fc2_index,
    fc2_count,
    fc2_bias,
    ffn_size,
):
    side = fc1_tiles.shape[-1]
    slots = fc1_tiles.shape[2]
    shards = lax.axis_size("blk")
    token_rows, width = tokens.shape
    first_blocks = fc1_bias.shape[0] // side
    second_blocks = width // side
    share = width // ffn_size
    blk, ffn = lax.axis_index("blk"), lax.axis_index("ffn")
    aligned = share % side == 0
    opening = slots * 7 // 11
    rest = slots - opening
    held = slots + slots // 14
    late_from = held - slots // 3
    levels = [
        (stride, slots // most, max(slots // least, 1))
        for stride, most, least in ((1, 4, 5), (2, 14, 16), (4, 25, 16), (8, 50, 16))
        if shards % (2 * stride) == 0
    ]
    slot_ids = jnp.arange(slots, dtype=jnp.int32)

    def gathered(value):
        return lax.all_gather(value, "blk", axis=0, tiled=True).reshape(shards, -1, side, side)

    tiles1 = gathered(fc1_tiles[0, 0, :opening])
    meta = jnp.concatenate([fc1_index[:, 0], fc2_index[:, 0], fc1_count, fc2_count], axis=1)
    meta = lax.all_gather(meta, "blk", axis=0, tiled=True)
    index1, index2 = meta[:, :slots], meta[:, slots : 2 * slots]
    count1, count2 = meta[:, 2 * slots], meta[:, 2 * slots + 1]
    left1 = jnp.maximum(count1 - opening, 0)

    def in_own_share(index):
        if not aligned:
            return jnp.zeros(index.shape, jnp.bool_)
        return index % second_blocks // (share // side) == ffn

    capacity = rest + slots
    total_ids = jnp.arange(2 * capacity + slots // 4, dtype=jnp.int32)
    codes, fronts, lengths, order, sends = laid_out(
        levels, capacity, total_ids.shape[0], index2, in_own_share(index2).astype(jnp.int32), count2, left1, blk
    )
    codes = codes.reshape(shards, -1)
    sources = jnp.concatenate([fc1_tiles[0, 0, opening:], fc2_tiles[0, 0]], axis=0)
    arrived = []
    for level, (stride, most_front, most_back) in enumerate(levels):
        sending, sends = sends[: most_front + most_back], sends[most_front + most_back :]
        arrived.append(
            lax.ppermute(
                jnp.take(sources, sending, axis=0, mode="clip"),
                "blk",
                [(i, i ^ stride) for i in range(shards)],
            )
        )
        if level == 0:
            sources = jnp.concatenate([sources, arrived.pop()], axis=0)
    sources = jnp.concatenate([sources, *arrived], axis=0)

    tiles2a = gathered(jnp.take(sources, order[:late_from], axis=0, mode="clip"))
    tiles2b = gathered(jnp.take(sources, order[late_from:held], axis=0, mode="clip"))
    misplaced = jnp.stack([jnp.max(fronts) - late_from, jnp.max(lengths) - held, jnp.max(lengths)])
    misplaced = lax.pmax(misplaced, "ffn")

    rows_f = tokens.astype(jnp.float32)
    center = jnp.mean(rows_f, axis=1, keepdims=True)
    spread = jnp.mean((rows_f - center) ** 2, axis=1, keepdims=True)
    normed = ((rows_f - center) / jnp.sqrt(spread + 1e-05) * ln_gain + ln_bias).astype(jnp.bfloat16)
    normed_blocks = normed.reshape(token_rows, second_blocks, side).transpose(1, 0, 2)
    normed_blocks = jnp.pad(normed_blocks, ((0, 1), (0, 0), (0, 0)))
    normed_blocks, misplaced = lax.optimization_barrier((normed_blocks, misplaced))
    some_late = jnp.max(misplaced[:2]) > 0

    (total,) = tile_pass(
        first_kernel,
        index1[:, :opening] // first_blocks,
        index1[:, :opening] % first_blocks,
        slot_ids[:opening] < count1[:, None],
        ffn,
        normed_blocks,
        tiles1,
        [fc1_bias.reshape(first_blocks, 1, side)],
        [fixed((first_blocks, 1, side))],
        [jax.ShapeDtypeStruct((first_blocks, token_rows, side), jnp.float32)],
        first_blocks,
        scratch=False,
    )
    (hidden,) = tile_pass(
        hidden_kernel,
        index1[:, opening:] // first_blocks,
        index1[:, opening:] % first_blocks,
        slot_ids[opening:] < count1[:, None],
        ffn,
        normed_blocks,
        tiles2a,
        [total],
        [fixed(total.shape)],
        [jax.ShapeDtypeStruct((first_blocks + 1, token_rows, side), jnp.bfloat16)],
        first_blocks,
    )

    def second_pass(places, live, tiles, steps=2, group=4):
        return tile_pass(
            partial_kernel,
            places // second_blocks,
            places % second_blocks,
            live,
            ffn,
            hidden,
            tiles,
            [],
            [],
            [
                jax.ShapeDtypeStruct((second_blocks, token_rows, side), jnp.float32),
                jax.ShapeDtypeStruct((token_rows, width), jnp.bfloat16),
            ],
            second_blocks,
            steps=steps,
            group=group,
            scratch=False,
        )

    def own_cols(value):
        return lax.dynamic_slice_in_dim(value, ffn * share, share, 1).astype(jnp.float32)

    def from_others(partial_value):
        branch = jnp.zeros((token_rows, share), jnp.float32)
        for shift in range(1, ffn_size):
            to = lax.rem(ffn + shift, ffn_size)
            arrived = lax.ppermute(
                lax.dynamic_slice_in_dim(partial_value, to * share, share, 1),
                "ffn",
                [(i, (i + shift) % ffn_size) for i in range(ffn_size)],
            )
            branch = branch + arrived.astype(jnp.float32)
        return branch

    in_front = total_ids < fronts[:, None]
    in_second = (total_ids >= left1[:, None]) & (total_ids < lengths[:, None])
    total, partial_value = second_pass(codes[:, :late_from], in_second[:, :late_from], tiles2a)
    last_codes = codes[:, late_from:held]
    last_own = (in_second & ~in_front)[:, late_from:held]
    branch = from_others(partial_value)

    def with_late(branch):
        chunk = slots // 4
        start = jnp.where(misplaced[0] > 0, late_from, held)
        late = in_second & (in_front | (total_ids >= held))

        def one_more(number, branch):
            at = start + number * chunk
            here = jnp.take(sources, lax.dynamic_slice_in_dim(order, at, chunk), axis=0, mode="clip")
            part = [lax.dynamic_slice_in_dim(v, at, chunk, 1) for v in (codes, late)]
            _, extra = second_pass(*part, gathered(here), steps=1, group=1)
            return branch + from_others(extra) + own_cols(extra)

        return lax.fori_loop(0, (misplaced[2] - start + chunk - 1) // chunk, one_more, branch)

    if not aligned:
        branch = lax.cond(some_late, with_late, lambda branch: branch, branch)
        more, _ = second_pass(last_codes, last_own, tiles2b)
        own = (total + more).transpose(1, 0, 2).reshape(token_rows, width)
        return (own_cols(tokens) + own_cols(own) + branch + fc2_bias).astype(jnp.bfloat16)

    share_blocks = share // side
    last_rows, last_cols = last_codes // second_blocks, last_codes % second_blocks % share_blocks
    last_steps = 4 if shards % 4 == 0 and token_rows % 64 == 0 else 1
    last_part = token_rows // last_steps
    last_plan = planned(last_rows, last_cols, last_own, share_blocks, first_blocks, last_steps, 3)
    bias_row = fc2_bias.reshape(1, share)
    last_plan, branch, bias_row = lax.optimization_barrier((last_plan, branch, bias_row))
    last_pass = functools.partial(
        tile_pass,
        result_kernel,
        last_rows,
        last_cols,
        last_own,
        ffn,
        hidden,
        tiles2b,
        more_specs=[
            pl.BlockSpec((share_blocks, last_part, side), lambda i, fields, counts, at: (at[0], i, 0)),
            pl.BlockSpec((last_part, share), lambda i, fields, counts, at: (i, at[0])),
            pl.BlockSpec((last_part, share), lambda i, *_: (i, 0)),
            fixed((1, share)),
        ],
        out_shapes=[jax.ShapeDtypeStruct((token_rows, share), jnp.bfloat16)],
        blocks=share_blocks,
        steps=last_steps,
        group=3,
        vmem=LAST_VMEM_BYTES,
        plan=last_plan,
    )

    def finished(branch):
        return last_pass(more=[total, tokens, branch, bias_row])[0]

    return lax.cond(some_late, lambda branch: finished(with_late(branch)), finished, branch)


def solution(mesh):
    placed = (
        P("blk", None),
        P(),
        P(),
        P("blk", "ffn", None, None, None),
        P("blk", "ffn", None),
        P("blk", "ffn"),
        P("ffn"),
        P("blk", "ffn", None, None, None),
        P("blk", "ffn", None),
        P("blk", "ffn"),
        P("ffn"),
    )
    return jax.shard_map(
        functools.partial(on_device, ffn_size=mesh.shape["ffn"]),
        mesh=mesh,
        in_specs=placed,
        out_specs=P("blk", "ffn"),
        check_vma=False,
    )
```
